32 devices in a mesh: clip: 4 (over z), frame: 4 (over y, x), seg: 2 (over core).
Axes of the slice: x: 2, y: 2, z: 4, core: 2. Of those that a mesh axis runs over, the one named last changes fastest.
Arguments:
- video: bfloat16 [2, 40, 4, 197, 384], P(None, ('clip', 'seg'), 'frame'), may hold values from -6 to 6
- captions: bfloat16 [2, 8, 128, 384], P(None, ('clip', 'seg'), 'frame'), may hold values from -6 to 6
- caption_lengths: int32 [2, 8, 9], P(None, ('clip', 'seg')), may hold values from 1 to 64, 128 in all within a row
- message_weight: bfloat16 [384, 384], replicated, may hold values from -0.3125 to 0.3125
- message_gain: float32 [384], replicated, may hold values from 0.25 to 1.75
- qkv_weights: bfloat16 [3, 3, 384, 384], replicated, may hold values from -0.3125 to 0.3125
- out_weights: bfloat16 [3, 384, 384], replicated, may hold values from -0.875 to 0.875
- mlp_up: bfloat16 [384, 1536], replicated, may hold values from -0.3125 to 0.3125
- mlp_down: bfloat16 [1536, 384], replicated, may hold values from -0.15625 to 0.15625
- gains: float32 [4, 384], replicated, may hold values from 0.5 to 1.5
- video_cot: bfloat16 [2, 40, 4, 197, 384], P(None, ('clip', 'seg'), 'frame'), may hold values from -6 to 6
- caption_cot: bfloat16 [2, 8, 128, 384], P(None, ('clip', 'seg'), 'frame'), may hold values from -6 to 6
Outputs:
- video_out: bfloat16 [2, 40, 4, 197, 384], P(None, ('clip', 'seg'), 'frame')
- caption_out: bfloat16 [2, 8, 128, 384], P(None, ('clip', 'seg'), 'frame')
- video_grad: bfloat16 [2, 40, 4, 197, 384], P(None, ('clip', 'seg'), 'frame')
- caption_grad: bfloat16 [2, 8, 128, 384], P(None, ('clip', 'seg'), 'frame')
- message_weight_grad: float32 [384, 384], replicated
- message_gain_grad: float32 [384], replicated
- qkv_weights_grad: float32 [3, 3, 384, 384], replicated
- out_weights_grad: float32 [3, 384, 384], replicated
- mlp_up_grad: float32 [384, 1536], replicated
- mlp_down_grad: float32 [1536, 384], replicated
- gains_grad: float32 [4, 384], replicated
The draws below stay inside these ranges and needn't reach their ends.
Inputs may be any that keep to these rules, and one draw needn't show every extreme that they name: `caption_lengths`: the entries of each row sum to 128; the last entry is the padding at the end of the pack, the others are the lengths of its captions; caption j of a pack describes clip j mod 5 of its group.
All inputs are finite; a program needn't handle non-finite values.
Results may differ from the reference program's by a relative error of at most 0.019.
Values may be sent and summed in bfloat16 or wider, within the bound.
No kernel may reach another device: no remote copies, remote signals or barrier semaphores. Data moves between devices by JAX's collectives and lax.ppermute only.
A program may use at most 192 MiB of HBM per device.

```python
import math
import jax
import jax.numpy as jnp
import numpy as np
from jax import lax

D = 384
HEADS = 6
HEAD_DIM = 64
FF = 1536
PATCH = 197
MICRO = 2
CLIP_DEV = 5
GROUPS = 8
CLIPS = 40
FRAMES = 4
CAP_TOK = 128
NCAP = 9
CAP_LIMIT = 64


def block_levels(key, extent, shards, low, largest):
    def one(axis_at, blocks):
        draws = jax.random.uniform(jax.random.fold_in(jax.random.fold_in(key, 6), axis_at), (blocks,), jnp.float32, low / len(shards), largest / len(shards))
        return jnp.repeat(jnp.exp(draws), extent[axis_at] // blocks).reshape((-1,) + (1,) * (len(extent) - axis_at - 1))

    gain = one(*shards[0])
    for cut in shards[1:]:
        gain = gain * one(*cut)
    return gain


def profile(amount, total, reach, lean):
    loads = [(1 << 20) // math.isqrt(standing ** lean) + 1 for standing in range(2, amount + 1)]
    spare, counts = total - reach - (amount - 1), [1] * (amount - 1)
    while spare > 0:
        movable = [i for i in range(amount - 1) if counts[i] < reach]
        pool, left = sum([loads[i] for i in movable]), spare
        for i in movable:
            addition = min(reach - counts[i], max(1, left * loads[i] // pool), spare)
            counts[i] = counts[i] + addition
            spare = spare - addition
    return np.array([reach] + counts)


def ragged_sizes(rng, amount, total, limit, lean):
    if amount == 2:
        one = jax.random.randint(rng, (), max(1, total - limit), min(limit, total - 1) + 1)
        return jnp.stack([one, total - one])
    sizes = jnp.asarray(profile(amount, total, limit, lean), jnp.int32)
    couples = (amount - 1) // 2
    source_of, taker = sizes[1:1 + 2 * couples:2], sizes[2:2 + 2 * couples:2]
    margin = jnp.minimum(source_of - 1, limit - taker)
    passed = jax.random.randint(jax.random.fold_in(rng, 1), (couples,), 0, 1 << 20) % (margin + 1)
    sizes = sizes.at[1:1 + 2 * couples:2].set(source_of - passed).at[2:2 + 2 * couples:2].set(taker + passed)
    return sizes[jax.random.permutation(jax.random.fold_in(rng, 2), amount)]


def noise(rng, extent, scale, most, split=(), kind=jnp.bfloat16):
    array = scale * jax.random.normal(rng, extent, jnp.float32)
    if split:
        array = array * block_levels(rng, extent, split, -0.22, 0.18)
    return jnp.clip(array, -most, most).astype(kind)


def setup_inputs(seed: int = 0) -> dict:
    streams_of = jax.random.split(jax.random.key(seed), 13)
    return {
        "video": noise(streams_of[0], (MICRO, CLIPS, FRAMES, PATCH, D), 1.0, 6.0, ((1, 8), (2, 4))),
        "captions": noise(streams_of[1], (MICRO, GROUPS, CAP_TOK, D), 1.0, 6.0, ((1, 8), (2, 4))),
        "caption_lengths": jax.vmap(lambda own: ragged_sizes(own, NCAP, CAP_TOK, CAP_LIMIT, 2))(jax.random.split(streams_of[2], MICRO * GROUPS)).reshape((MICRO, GROUPS, NCAP)).astype(jnp.int32),
        "message_weight": noise(streams_of[3], (D, D), D ** -0.5, 0.3125),
        "message_gain": jnp.clip(1.0 + 0.15 * jax.random.normal(streams_of[4], (D,), jnp.float32), 0.25, 1.75),
        "qkv_weights": noise(streams_of[5], (3, 3, D, D), D ** -0.5, 0.3125),
        "out_weights": noise(streams_of[6], (3, D, D), (D // 8) ** -0.5, 0.875),
        "mlp_up": noise(streams_of[7], (D, FF), D ** -0.5, 0.3125),
        "mlp_down": noise(streams_of[8], (FF, D), FF ** -0.5, 0.15625),
        "gains": jnp.clip(1.0 + 0.1 * jax.random.normal(streams_of[9], (4, D), jnp.float32), 0.5, 1.5),
        "video_cot": noise(streams_of[10], (MICRO, CLIPS, FRAMES, PATCH, D), 1.0, 6.0, ((1, 8), (2, 4))),
        "caption_cot": noise(streams_of[11], (MICRO, GROUPS, CAP_TOK, D), 1.0, 6.0, ((1, 8), (2, 4))),
    }


@jax.custom_vjp
def low(v):
    return lax.optimization_barrier(v.astype(jnp.bfloat16)).astype(jnp.float32)

@jax.custom_vjp
def low_back(v):
    return v

def low_keep(v):
    return (low(v), None)

def low_pass(kept, grad):
    return (grad,)

def back_keep(v):
    return (v, None)

def back_low(kept, grad):
    return (low(grad),)
low.defvjp(low_keep, low_pass)
low_back.defvjp(back_keep, back_low)
epsilon = 1e-05
score_scale = 0.125
masked_score = -1e+30
precise = lax.Precision.HIGHEST

def both_round(values):
    return low_back(low(values))

def layer_norm(values, gain_row):
    center = values - lax.optimization_barrier(jnp.mean(values, axis=-1, keepdims=True))
    spread = lax.optimization_barrier(jnp.mean(center * center, axis=-1, keepdims=True))
    return center * lax.rsqrt(spread + epsilon) * gain_row

def quick_gelu(values):
    return values * jax.nn.sigmoid(1.702 * values)

def product(left, right):
    return jnp.dot(left, right, precision=precise)

def caption_masks(lengths):
    ends = jnp.cumsum(lengths)
    position = jnp.arange(CAP_TOK, dtype=jnp.int32)
    document = lax.optimization_barrier(jnp.sum((ends[None, :] <= position[:, None]).astype(jnp.int32), axis=1))
    valid = (document < NCAP - 1).astype(jnp.float32)
    token_clip = document % CLIP_DEV
    key_clip = jnp.arange(CLIP_DEV * FRAMES, dtype=jnp.int32) // FRAMES
    return (valid, token_clip[:, None] == key_clip[None, :])

def layer(weights, clip_video, pack, valid, allowed):
    message_weight, message_gain, qkv_weights, out_weights, mlp_up, mlp_down, gains = weights
    clip_count, frame_count, patch_count, width = clip_video.shape
    token_count = patch_count + 1
    class_rows = clip_video[:, :, 0, :]
    start_message = low(product(class_rows, message_weight))
    normed = low(layer_norm(start_message, message_gain))
    queries = low(product(normed, qkv_weights[0, 0])).reshape(clip_count, frame_count, HEADS, HEAD_DIM)
    keys = low(product(normed, qkv_weights[0, 1])).reshape(clip_count, frame_count, HEADS, HEAD_DIM)
    values = low(product(normed, qkv_weights[0, 2])).reshape(clip_count, frame_count, HEADS, HEAD_DIM)
    scores = jnp.einsum('cfhd,cghd->chfg', queries, keys, precision=precise) * score_scale
    probs = jax.nn.softmax(scores, axis=-1)
    context = low(jnp.einsum('chfg,cghd->cfhd', low(probs), values, precision=precise))
    context = context.reshape(clip_count, frame_count, width)
    message = start_message + product(context, out_weights[0])
    tokens = jnp.concatenate([clip_video, message[:, :, None, :]], axis=2)
    normed = low(layer_norm(tokens, gains[0]))
    head_shape = (clip_count, frame_count, token_count, HEADS, HEAD_DIM)
    queries = both_round(product(normed, qkv_weights[1, 0])).reshape(head_shape)
    keys = both_round(product(normed, qkv_weights[1, 1])).reshape(head_shape)
    values = both_round(product(normed, qkv_weights[1, 2])).reshape(head_shape)
    scores = low_back(jnp.einsum('cfqhd,cfkhd->cfhqk', queries, keys, precision=precise) * score_scale)
    probs = jax.nn.softmax(scores, axis=-1)
    context = both_round(jnp.einsum('cfhqk,cfkhd->cfqhd', low(probs), values, precision=precise))
    context = context.reshape(clip_count, frame_count, token_count, width)
    mixed = tokens + low_back(product(context, out_weights[1]))
    resid = mixed[:, :, :patch_count]
    normed = low(layer_norm(resid, gains[1]))
    hidden = low_back(product(normed, mlp_up))
    active = low(quick_gelu(hidden))
    final = resid + low_back(product(active, mlp_down))
    visual = low(layer_norm(final[:, :, 0], gains[2])).reshape(clip_count * frame_count, width)
    normed = low(layer_norm(pack, gains[3]))
    queries = both_round(product(normed, qkv_weights[2, 0])).reshape(-1, HEADS, HEAD_DIM)
    keys = low(product(visual, qkv_weights[2, 1])).reshape(-1, HEADS, HEAD_DIM)
    values = low(product(visual, qkv_weights[2, 2])).reshape(-1, HEADS, HEAD_DIM)
    scores = jnp.einsum('thd,khd->htk', queries, keys, precision=precise) * score_scale
    scores = low_back(jnp.where(allowed[None], scores, masked_score))
    probs = jax.nn.softmax(scores, axis=-1)
    context = both_round(jnp.einsum('htk,khd->thd', low(probs), values, precision=precise)).reshape(-1, width)
    caption_sum = pack + valid[:, None] * low_back(product(context, out_weights[2]))
    return (final, caption_sum)

def reference(video, captions, caption_lengths, message_weight, message_gain, qkv_weights, out_weights, mlp_up, mlp_down, gains, video_cot, caption_cot):
    weights = tuple((matrix.astype(jnp.float32) for matrix in (message_weight, message_gain, qkv_weights, out_weights, mlp_up, mlp_down, gains)))
    count = MICRO * GROUPS
    video_groups = video.reshape(count, CLIP_DEV, FRAMES, PATCH, D)
    cot_groups = video_cot.reshape(count, CLIP_DEV, FRAMES, PATCH, D)
    pack_groups = captions.reshape(count, CAP_TOK, D)
    pack_cots = caption_cot.reshape(count, CAP_TOK, D)
    length_groups = caption_lengths.reshape(count, NCAP)

    def group_step(totals, item):
        clip_video, pack, lengths, video_grad_in, pack_grad_in = item
        valid, allowed = caption_masks(lengths)

        def forward(weight_set, video_in, pack_in):
            return layer(weight_set, video_in, pack_in, valid, allowed)
        outputs, pull = jax.vjp(forward, weights, clip_video.astype(jnp.float32), pack.astype(jnp.float32))
        weight_grads, video_grad, pack_grad = pull((video_grad_in.astype(jnp.float32), pack_grad_in.astype(jnp.float32)))
        totals = jax.tree.map(lambda left, right: left + right, totals, weight_grads)
        return (totals, (outputs[0].astype(jnp.bfloat16), outputs[1].astype(jnp.bfloat16), video_grad.astype(jnp.bfloat16), pack_grad.astype(jnp.bfloat16)))
    zeros = jax.tree.map(jnp.zeros_like, weights)
    totals, stacked = lax.scan(group_step, zeros, (video_groups, pack_groups, length_groups, cot_groups, pack_cots))
    video_out = stacked[0].reshape(MICRO, CLIPS, FRAMES, PATCH, D)
    caption_out = stacked[1].reshape(MICRO, GROUPS, CAP_TOK, D)
    video_grad = stacked[2].reshape(MICRO, CLIPS, FRAMES, PATCH, D)
    caption_grad = stacked[3].reshape(MICRO, GROUPS, CAP_TOK, D)
    return (video_out, caption_out, video_grad, caption_grad, totals[0], totals[1], totals[2], totals[3], totals[4], totals[5], totals[6])
```

```python
import functools

import jax
import jax.numpy as jnp
from jax import lax
from jax.experimental import pallas as pl
from jax.experimental.pallas import tpu as pltpu
from jax.sharding import PartitionSpec as P

HEADS = 6
HEAD_DIM = 64
EPS = 1e-05
SCALE = 0.125
MASKED = -1e30
BIG = 56 * 1024 * 1024

f32 = jnp.float32
bf16 = jnp.bfloat16


def nn(a, b):
    return lax.dot_general(a, b, (((1,), (0,)), ((), ())), preferred_element_type=f32)


def nt(a, b):
    return lax.dot_general(a, b, (((1,), (1,)), ((), ())), preferred_element_type=f32)


def tn(a, b):
    return lax.dot_general(a, b, (((0,), (0,)), ((), ())), preferred_element_type=f32)


def exact(a, b):
    return lax.dot_general(
        a, b, (((1,), (0,)), ((), ())), precision=lax.Precision.HIGHEST, preferred_element_type=f32
    )


def unit_norm(x):
    center = x - jnp.mean(x, axis=-1, keepdims=True)
    inv = lax.rsqrt(jnp.mean(center * center, axis=-1, keepdims=True) + EPS)
    return center * inv, inv


def norm_back(unit, inv, gain, dy):
    du = dy * gain
    mean_du = jnp.mean(du, axis=-1, keepdims=True)
    mean_dot = jnp.mean(du * unit, axis=-1, keepdims=True)
    return inv * (du - mean_du - unit * mean_dot)


def row_sum(x):
    return jnp.sum(x, axis=0, keepdims=True)


def sigmoid(x):
    return 1.0 / (1.0 + jnp.exp(-x))


def head_mask(shape, lane_dim, head):
    lane = lax.broadcasted_iota(jnp.int32, shape, lane_dim)
    return (lane >= head * HEAD_DIM) & (lane < (head + 1) * HEAD_DIM)


def head_columns(width):
    lane = lax.broadcasted_iota(jnp.int32, (width, 128), 0)
    col = lax.broadcasted_iota(jnp.int32, (width, 128), 1)
    return ((lane >= col * HEAD_DIM) & (lane < (col + 1) * HEAD_DIM)).astype(f32)


def head_rows(width):
    col = lax.broadcasted_iota(jnp.int32, (128, width), 0)
    lane = lax.broadcasted_iota(jnp.int32, (128, width), 1)
    return ((lane >= col * HEAD_DIM) & (lane < (col + 1) * HEAD_DIM)).astype(f32)


def pad_rows(x, rows):
    if x.shape[0] == rows:
        return x
    return jnp.concatenate([x, jnp.zeros((rows - x.shape[0], x.shape[1]), x.dtype)], axis=0)


def put_row(block, at, row):
    top = at // 16 * 16
    tail = block[top : top + 16]
    index = lax.broadcasted_iota(jnp.int32, tail.shape, 0)
    tail = jnp.where(index == at - top, row, tail)
    pieces = [tail]
    if top:
        pieces.insert(0, block[:top])
    if top + 16 < block.shape[0]:
        pieces.append(block[top + 16 :])
    return jnp.concatenate(pieces, axis=0) if len(pieces) > 1 else tail


def full(shape):
    return pl.BlockSpec(shape, lambda *_: (0,) * len(shape))


def frame_block(shape):
    return pl.BlockSpec((1,) + shape, lambda i, *_: (i, 0, 0))


def scalars():
    return pl.BlockSpec(memory_space=pltpu.SMEM)


def shape_of(shape, dtype):
    return jax.ShapeDtypeStruct(shape, dtype)


def params(limit=BIG):
    return pltpu.CompilerParams(vmem_limit_bytes=limit)


def cost(flops, nbytes):
    return pl.CostEstimate(flops=int(flops), bytes_accessed=int(nbytes), transcendentals=0)


def class_kernel(count, video_ref, out_ref):
    rows = [video_ref[i, 0:1, :].astype(f32) for i in range(count)]
    out_ref[...] = pad_rows(jnp.concatenate(rows, axis=0), out_ref.shape[0]).astype(bf16)


def class_rows(video, slots):
    count, _, width = video.shape
    return pl.pallas_call(
        functools.partial(class_kernel, count),
        grid=(1,),
        in_specs=[pl.BlockSpec((count, 16, width), lambda i: (0, 0, 0))],
        out_specs=full((slots, width)),
        out_shape=shape_of((slots, width), bf16),
        name="class_rows",
    )(video)


def norm_kernel(rows, video_ref, gains_ref, wk_ref, wv_ref, normed_ref, k_ref, vt_ref, wvt):
    @pl.when(pl.program_id(0) == 0)
    def _():
        wvt[...] = wv_ref[...].T

    unit, _ = unit_norm(video_ref[0].astype(f32))
    normed = pad_rows(unit * gains_ref[0:1, :], rows).astype(bf16)
    normed_ref[0] = normed
    k_ref[0] = nn(normed, wk_ref[...]).astype(bf16)
    vt_ref[0] = nt(wvt[...], normed).astype(bf16)


def norm_tokens(video, gains, wk, wv, rows):
    count, patch, width = video.shape
    return pl.pallas_call(
        functools.partial(norm_kernel, rows),
        grid=(count,),
        in_specs=[
            frame_block((patch, width)),
            full(gains.shape),
            full(wk.shape),
            full(wv.shape),
        ],
        out_specs=[
            frame_block((rows, width)),
            frame_block((rows, width)),
            frame_block((width, rows)),
        ],
        out_shape=[
            shape_of((count, rows, width), bf16),
            shape_of((count, rows, width), bf16),
            shape_of((count, width, rows), bf16),
        ],
        scratch_shapes=[pltpu.VMEM((width, width), bf16)],
        compiler_params=params(),
        cost_estimate=cost(4 * count * rows * width * width, 8 * count * rows * width),
        name="norm_tokens",
    )(video, gains, wk, wv)


def message_scores(query, keys, columns):
    return [exact(query.astype(f32) * key.astype(f32), columns) * SCALE for key in keys]


def message_probs(scores):
    top = functools.reduce(jnp.maximum, scores)
    expo = [jnp.exp(score - top) for score in scores]
    total = functools.reduce(jnp.add, expo)
    return [e / total for e in expo]


def first_kernel(
    pieces, count, tokens, *refs
):
    gathered = refs[:pieces]
    (
        mw_ref, mg_ref, qkv_ref, outw_ref, up_ref, down_ref, gains_ref, k_ref, vt_ref,
        message_ref, nmsg_ref, visual_ref, final_ref, ctx,
    ) = refs[pieces:]
    width = mw_ref.shape[0]
    slots = gathered[0].shape[0]
    rows = k_ref.shape[1]
    classes = jnp.concatenate([g[...] for g in gathered], axis=0)
    start = nn(classes, mw_ref[...]).astype(bf16)
    unit, _ = unit_norm(start.astype(f32))
    normed = (unit * mg_ref[...]).astype(bf16)
    keys = nn(normed, qkv_ref[0, 1]).astype(bf16)
    values = nn(normed, qkv_ref[0, 2]).astype(bf16)
    query = nn(normed[:slots], qkv_ref[0, 0]).astype(bf16)
    columns, spread = head_columns(width), head_rows(width).astype(bf16)
    cut = [slice(g * slots, (g + 1) * slots) for g in range(pieces)]
    probs = message_probs(message_scores(query, [keys[c] for c in cut], columns))
    context = functools.reduce(
        jnp.add,
        [nn(p.astype(bf16), spread) * values[c].astype(f32) for p, c in zip(probs, cut)],
    ).astype(bf16)
    message = start[:slots].astype(f32) + nn(context, outw_ref[0])
    message_ref[...] = message
    unit, _ = unit_norm(message)
    nmsg = (unit * gains_ref[0:1, :]).astype(bf16)
    nmsg_ref[...] = nmsg.astype(f32)
    kmsg = nn(nmsg, qkv_ref[1, 1]).astype(bf16).astype(f32)
    vmsg = nn(nmsg, qkv_ref[1, 2]).astype(bf16).astype(f32)

    own = gathered[0][...].astype(f32)
    unit, _ = unit_norm(own)
    qcls = nn((unit * gains_ref[0:1, :]).astype(bf16), qkv_ref[1, 0]).astype(bf16).astype(f32) * SCALE
    head = lax.broadcasted_iota(jnp.int32, (16, width), 0)
    lane = lax.broadcasted_iota(jnp.int32, (16, width), 1)
    mine = (lane >= head * HEAD_DIM) & (lane < (head + 1) * HEAD_DIM)
    token = lax.broadcasted_iota(jnp.int32, (16, rows), 1)
    ctx[...] = jnp.zeros(ctx.shape, f32)
    for i in range(count):
        queries = jnp.where(mine, qcls[i : i + 1], 0.0)
        scores = nt(queries.astype(bf16), k_ref[i])
        last = jnp.sum(queries * kmsg[i : i + 1], axis=1, keepdims=True)
        scores = jnp.where(token == tokens - 1, last, scores)
        scores = jnp.where(token < tokens, scores, MASKED)
        expo = jnp.exp(scores - jnp.max(scores, axis=1, keepdims=True))
        prob = (expo / jnp.sum(expo, axis=1, keepdims=True)).astype(bf16)
        extra = jnp.sum(
            jnp.where(token == tokens - 1, prob.astype(f32), 0.0), axis=1, keepdims=True
        )
        out = nt(prob, vt_ref[i]) + extra * vmsg[i : i + 1]
        ctx[i : i + 1, :] = row_sum(jnp.where(mine, out, 0.0))
    resid = own + nn(ctx[...].astype(bf16), outw_ref[1])
    unit, _ = unit_norm(resid)
    hidden = nn((unit * gains_ref[1:2, :]).astype(bf16), up_ref[...])
    active = (hidden * sigmoid(1.702 * hidden)).astype(bf16)
    final = resid + nn(active, down_ref[...])
    final_ref[...] = final
    unit, _ = unit_norm(final)
    visual_ref[...] = (unit * gains_ref[2:3, :]).astype(bf16)


def first_rows(gathered, mw, mg, qkv, outw, up, down, gains, keys, values_t, tokens):
    count, rows, width = keys.shape
    slots = gathered[0].shape[0]
    operands = list(gathered) + [mw, mg, qkv, outw, up, down, gains, keys, values_t]
    return pl.pallas_call(
        functools.partial(first_kernel, len(gathered), count, tokens),
        grid=(1,),
        in_specs=[full(x.shape) for x in operands],
        out_specs=[full((slots, width))] * 4,
        out_shape=[
            shape_of((slots, width), f32),
            shape_of((slots, width), f32),
            shape_of((slots, width), bf16),
            shape_of((slots, width), f32),
        ],
        scratch_shapes=[pltpu.VMEM((slots, width), f32)],
        compiler_params=params(),
        cost_estimate=cost(4e9, 12e6),
        name="first_rows",
    )(*operands)


def with_message(normed_ref, nmsg_ref, tokens):
    normed = normed_ref[0]
    top = (tokens - 1) // 16 * 16
    tail = normed[top : top + 16].astype(f32)
    index = lax.broadcasted_iota(jnp.int32, tail.shape, 0)
    row = nmsg_ref[pl.ds(pl.program_id(0), 1), :]
    tail = jnp.where(index == tokens - 1 - top, row, tail).astype(bf16)
    pieces = [normed[:top], tail]
    if top + 16 < normed.shape[0]:
        pieces.append(normed[top + 16 :])
    return jnp.concatenate(pieces, axis=0)


def masked_tail(scores, tokens):
    top = tokens // 16 * 16
    if top >= scores.shape[0]:
        return scores
    tail = scores[top:]
    index = lax.broadcasted_iota(jnp.int32, tail.shape, 0)
    return jnp.concatenate([scores[:top], jnp.where(index < tokens - top, tail, MASKED)], axis=0)


def half_pair(block_t, head):
    own = block_t[head * HEAD_DIM : (head + 1) * HEAD_DIM]
    none = jnp.zeros(own.shape, own.dtype)
    return jnp.concatenate([own, none] if head % 2 == 0 else [none, own], axis=0)


def pair_lanes(block, head):
    at = head // 2 * 2 * HEAD_DIM
    return block[:, at : at + 2 * HEAD_DIM]


def attend_kernel(
    tokens, normed_ref, video_ref, message_ref, nmsg_ref, wq_ref, wk_ref, wv_ref, wo_ref,
    resid_ref, ctx_ref, lse_ref, wqt, wvt,
):
    @pl.when(pl.program_id(0) == 0)
    def _():
        wqt[...] = wq_ref[...].T
        wvt[...] = wv_ref[...].T

    normed = with_message(normed_ref, nmsg_ref, tokens)
    rows = normed.shape[0]
    keys = nn(normed, wk_ref[...]).astype(bf16)
    queries_t = nt(wqt[...], normed).astype(bf16) * jnp.bfloat16(SCALE)
    values_t = nt(wvt[...], normed).astype(bf16)
    contexts, stats = [], []
    for head in range(HEADS):
        scores = nn(pair_lanes(keys, head), half_pair(queries_t, head))
        scores = masked_tail(scores, tokens)
        top = jnp.max(scores, axis=0, keepdims=True)
        expo = jnp.exp(scores - top)
        total = row_sum(expo)
        own = values_t[head * HEAD_DIM : (head + 1) * HEAD_DIM]
        contexts.append(nn(own, expo.astype(bf16)) * (1.0 / total))
        stats.append(top + jnp.log(total))
    context_t = jnp.concatenate(contexts, axis=0).astype(bf16)
    ctx_ref[0] = context_t
    lse_ref[0] = jnp.concatenate(stats + [jnp.zeros((8 - HEADS, rows), f32)], axis=0)
    row = message_ref[pl.ds(pl.program_id(0), 1), :]
    base = put_row(pad_rows(video_ref[0].astype(f32), rows), tokens - 1, row)
    resid_ref[0] = base + tn(context_t, wo_ref[...])


def attend(normed, video, message, nmsg, wq, wk, wv, wo, tokens):
    count, rows, width = normed.shape
    slots = message.shape[0]
    return pl.pallas_call(
        functools.partial(attend_kernel, tokens),
        grid=(count,),
        in_specs=[
            frame_block((rows, width)),
            frame_block(video.shape[1:]),
            full((slots, width)),
            full((slots, width)),
        ]
        + [full((width, width))] * 4,
        out_specs=[
            frame_block((rows, width)),
            frame_block((width, rows)),
            frame_block((8, rows)),
        ],
        out_shape=[
            shape_of((count, rows, width), f32),
            shape_of((count, width, rows), bf16),
            shape_of((count, 8, rows), f32),
        ],
        scratch_shapes=[pltpu.VMEM((width, width), bf16)] * 2,
        compiler_params=params(),
        cost_estimate=cost(14e9, 10e6),
        name="attend",
    )(normed, video, message, nmsg, wq, wk, wv, wo)


def caption_kernel(
    pieces, groups, clips, local, where_ref, lengths_ref, *refs
):
    gathered = refs[:pieces]
    caps_ref, cot_ref, qkv_ref, outw_ref, gains_ref = refs[pieces : pieces + 5]
    out_ref, grad_ref, gain_ref = refs[pieces + 5 : pieces + 8]
    part_refs = refs[pieces + 8 : pieces + 8 + pieces]
    keep_ref, send_ref, acc = refs[pieces + 8 + pieces :]
    width = caps_ref.shape[1]
    slots = gathered[0].shape[0]
    count = caps_ref.shape[0]
    keys_n = pieces * slots
    runs = lengths_ref.shape[1]

    token = lax.broadcasted_iota(jnp.int32, (count, keys_n), 0)
    key = lax.broadcasted_iota(jnp.int32, (count, keys_n), 1)
    slot = key % slots
    group = token // local
    position = token - group * local + where_ref[0] * local
    document = jnp.zeros((count, keys_n), jnp.int32)
    for m in range(groups):
        end = jnp.int32(0)
        for j in range(runs):
            end = end + lengths_ref[m, j]
            document = document + jnp.where((group == m) & (position >= end), 1, 0)
    allowed = slot == group * clips + document % clips
    valid = (document[:, 0:1] < runs - 1).astype(f32)

    pack = caps_ref[...].astype(f32)
    unit, inv = unit_norm(pack)
    gain = gains_ref[3:4, :]
    normed = (unit * gain).astype(bf16)
    visual = jnp.concatenate([g[...] for g in gathered], axis=0)
    queries = nn(normed, qkv_ref[2, 0]).astype(bf16)
    keys = nn(visual, qkv_ref[2, 1]).astype(bf16)
    values = nn(visual, qkv_ref[2, 2]).astype(bf16)

    masks = [head_mask((count, width), 1, h) for h in range(HEADS)]
    zero = jnp.zeros((count, width), bf16)

    def by_head(x):
        return jnp.concatenate([jnp.where(m, x, zero) for m in masks], axis=0)

    def merge(x):
        cut = [x[h * count : (h + 1) * count] for h in range(HEADS)]
        return functools.reduce(jnp.add, [jnp.where(m, c, 0.0) for m, c in zip(masks, cut)])

    allowed_all = jnp.concatenate([allowed.astype(jnp.int32)] * HEADS, axis=0) > 0
    split_q = by_head(queries)
    scores = jnp.where(allowed_all, nt(split_q, keys) * SCALE, MASKED)
    expo = jnp.exp(scores - jnp.max(scores, axis=1, keepdims=True))
    probs = expo / jnp.sum(expo, axis=1, keepdims=True)
    low = probs.astype(bf16)
    context = merge(nn(low, values)).astype(bf16)
    out_ref[...] = (pack + valid * nn(context, outw_ref[2])).astype(bf16)

    cot = cot_ref[...].astype(f32)
    branch = (cot * valid).astype(bf16)
    split_d = by_head(nt(branch, outw_ref[2]).astype(bf16))
    dvalues = tn(low, split_d)
    dprobs = nt(split_d, values)
    dscores = probs * (dprobs - jnp.sum(dprobs * probs, axis=1, keepdims=True))
    dscores = jnp.where(allowed_all, dscores, 0.0).astype(bf16)
    dqueries = (merge(nn(dscores, keys)) * SCALE).astype(bf16)
    dkeys = tn(dscores, split_q) * SCALE
    dnormed = nt(dqueries, qkv_ref[2, 0])
    grad_ref[...] = (cot + norm_back(unit, inv, gain, dnormed)).astype(bf16)
    gain_ref[...] = jnp.concatenate([row_sum(dnormed * unit), jnp.zeros((7, width), f32)], axis=0)
    low_k, low_v = dkeys.astype(bf16), dvalues.astype(bf16)
    part = nt(low_k, qkv_ref[2, 1]) + nt(low_v, qkv_ref[2, 2])
    for g in range(pieces):
        part_refs[g][...] = part[g * slots : (g + 1) * slots]
    if acc.shape[0] > 4 * width:
        acc[...] = jnp.zeros(acc.shape, f32)
    acc[0:width, :] = tn(normed, dqueries)
    acc[width : 2 * width, :] = tn(visual, low_k)
    acc[2 * width : 3 * width, :] = tn(visual, low_v)
    acc[3 * width : 4 * width, :] = tn(context, branch)
    emit(where_ref, acc, keep_ref, send_ref)


def captions_step(where, lengths, gathered, caps, cot, qkv, outw, gains, plan):
    count, width = caps.shape
    groups = lengths.shape[0]
    pieces = len(gathered)
    slots = gathered[0].shape[0]
    operands = list(gathered) + [caps, cot, qkv, outw, gains]
    acc_rows, packet_specs, packet_shapes = plan.packet(4 * width, width)
    return pl.pallas_call(
        functools.partial(caption_kernel, pieces, groups, plan.clips, count // groups),
        grid=(1,),
        in_specs=[scalars(), scalars()] + [full(x.shape) for x in operands],
        out_specs=[full((count, width))] * 2
        + [full((8, width))]
        + [full((slots, width))] * pieces
        + packet_specs,
        out_shape=[shape_of((count, width), bf16)] * 2
        + [shape_of((8, width), f32)]
        + [shape_of((slots, width), f32)] * pieces
        + packet_shapes,
        scratch_shapes=[pltpu.VMEM((acc_rows, width), f32)],
        compiler_params=params(),
        cost_estimate=cost(4e9, 8e6),
        name="captions_step",
    )(where, lengths, *operands)


def mlp_kernel(
    pieces, patch, ff, where_ref, resid_ref, cot_ref, final_ref, gains_ref, up_ref, down_ref, *refs
):
    parts = refs[:pieces]
    out_ref, dresid_ref, gain_ref, keep_ref, send_ref, acc, dcls = refs[pieces:]
    step = pl.program_id(0)
    rows, width = resid_ref.shape[1:]
    blocks = ff // width

    @pl.when(step == 0)
    def _():
        acc[...] = jnp.zeros(acc.shape, f32)
        dvisual = functools.reduce(jnp.add, [p[...] for p in parts])
        unit, inv = unit_norm(final_ref[...])
        dcls[...] = norm_back(unit, inv, gains_ref[2:3, :], dvisual)
        gain_ref[...] = jnp.concatenate(
            [jnp.zeros((1, width), f32), row_sum(dvisual * unit), jnp.zeros((6, width), f32)],
            axis=0,
        )

    resid = resid_ref[0]
    gain = gains_ref[1:2, :]
    unit, inv = unit_norm(resid)
    normed32 = unit * gain
    normed = normed32.astype(bf16)
    normed_t = normed32.T.astype(bf16)
    dfinal = pad_rows(cot_ref[0].astype(f32), rows)
    dfinal = put_row(dfinal, 0, dfinal[0:1] + dcls[pl.ds(step, 1), :])
    branch = dfinal.astype(bf16)
    branch_t = dfinal.T.astype(bf16)
    final = resid
    dnormed = jnp.zeros((rows, width), f32)
    for c in range(blocks):
        span = slice(c * width, (c + 1) * width)
        hidden = nn(normed, up_ref[:, span])
        gate = sigmoid(1.702 * hidden)
        active = (hidden * gate).astype(bf16)
        final = final + nn(active, down_ref[span, :])
        dactive = nt(branch, down_ref[span, :])
        dhidden = (dactive * gate * (1.0 + 1.702 * hidden * (1.0 - gate))).astype(bf16)
        dnormed = dnormed + nt(dhidden, up_ref[:, span])
        acc[span, :] += nn(normed_t, dhidden)
        acc[(blocks + c) * width : (blocks + c + 1) * width, :] += nn(branch_t, active)
    out_ref[0] = final[:patch].astype(bf16)
    dresid_ref[0] = dfinal + norm_back(unit, inv, gain, dnormed)
    gain_ref[0:1, :] += row_sum(dnormed * unit)

    @pl.when(step == pl.num_programs(0) - 1)
    def _():
        emit(where_ref, acc, keep_ref, send_ref)


def mlp_step(where, resid, cot, final, gains, up, down, parts, plan):
    count, rows, width = resid.shape
    patch = cot.shape[1]
    ff = up.shape[1]
    slots = final.shape[0]
    acc_rows, packet_specs, packet_shapes = plan.packet(2 * ff, width)
    return pl.pallas_call(
        functools.partial(mlp_kernel, len(parts), patch, ff),
        grid=(count,),
        in_specs=[
            scalars(),
            frame_block((rows, width)),
            frame_block((patch, width)),
            full((slots, width)),
            full(gains.shape),
            full(up.shape),
            full(down.shape),
        ]
        + [full((slots, width))] * len(parts),
        out_specs=[frame_block((patch, width)), frame_block((rows, width)), full((8, width))]
        + packet_specs,
        out_shape=[
            shape_of((count, patch, width), bf16),
            shape_of((count, rows, width), f32),
            shape_of((8, width), f32),
        ]
        + packet_shapes,
        scratch_shapes=[pltpu.VMEM((acc_rows, width), f32), pltpu.VMEM((slots, width), f32)],
        compiler_params=params(),
        cost_estimate=cost(20e9, 20e6),
        name="mlp_step",
    )(where, resid, cot, final, gains, up, down, *parts)


def attend_back_kernel(
    tokens, where_ref, normed_ref, video_ref, message_ref, nmsg_ref, ctx_ref, lse_ref, dresid_ref,
    gains_ref, wq_ref, wk_ref, wv_ref, wo_ref,
    grad_ref, dmsg_ref, dcls_ref, gain_ref, keep_ref, send_ref, acc, wqt, wkt, wall,
):
    step = pl.program_id(0)
    rows, width = dresid_ref.shape[1:]
    patch = tokens - 1

    @pl.when(step == 0)
    def _():
        acc[...] = jnp.zeros(acc.shape, f32)
        wqt[...] = wq_ref[...].T
        wkt[...] = wk_ref[...].T
        wall[:, 0:width] = wq_ref[...]
        wall[:, width : 2 * width] = wk_ref[...]
        wall[:, 2 * width : 3 * width] = wv_ref[...]
        dmsg_ref[...] = jnp.zeros(dmsg_ref.shape, f32)
        dcls_ref[...] = jnp.zeros(dcls_ref.shape, f32)
        gain_ref[...] = jnp.zeros(gain_ref.shape, f32)

    normed = with_message(normed_ref, nmsg_ref, tokens)
    keys = nn(normed, wk_ref[...]).astype(bf16)
    values = nn(normed, wv_ref[...]).astype(bf16)
    queries_t = nt(wqt[...], normed).astype(bf16) * jnp.bfloat16(SCALE)
    keys_t = nt(wkt[...], normed).astype(bf16)
    dmixed = dresid_ref[0]
    branch = dmixed.astype(bf16)
    context_t = ctx_ref[0]
    acc[3 * width : 4 * width, :] += nn(context_t, branch)
    dcontext_t = nt(wo_ref[...], branch).astype(bf16)
    dq, dk, dv = [], [], []
    for head in range(HEADS):
        own = slice(head * HEAD_DIM, (head + 1) * HEAD_DIM)
        scores = nn(pair_lanes(keys, head), half_pair(queries_t, head))
        probs = jnp.exp(masked_tail(scores, tokens) - lse_ref[0, head : head + 1, :])
        dprobs = nn(pair_lanes(values, head), half_pair(dcontext_t, head))
        dscores = (probs * (dprobs - row_sum(dprobs * probs))).astype(bf16)
        dv.append(nt(dcontext_t[own], probs.astype(bf16)))
        dq.append(nn(keys_t[own], dscores) * SCALE)
        dk.append(nt(queries_t[own], dscores))
    dall = jnp.concatenate(dq + dk + dv, axis=0).astype(bf16)
    acc[0 : 3 * width, :] += nn(dall, normed)
    dnormed = nn(wall[...], dall).T
    row = message_ref[pl.ds(step, 1), :]
    base = put_row(pad_rows(video_ref[0].astype(f32), rows), tokens - 1, row)
    unit, inv = unit_norm(base)
    dtokens = dmixed + norm_back(unit, inv, gains_ref[0:1, :], dnormed)
    gain_ref[0:1, :] += row_sum(dnormed * unit)
    grad_ref[0] = dtokens[:patch].astype(bf16)
    dcls_ref[pl.ds(step, 1), :] = dtokens[0:1]
    dmsg_ref[pl.ds(step, 1), :] = dtokens[patch : patch + 1]

    @pl.when(step == pl.num_programs(0) - 1)
    def _():
        emit(where_ref, acc, keep_ref, send_ref)


def attend_back(where, normed, video, message, nmsg, ctx, lse, dresid, gains, wq, wk, wv, wo, plan):
    count, rows, width = normed.shape
    patch = video.shape[1]
    slots = message.shape[0]
    acc_rows, packet_specs, packet_shapes = plan.packet(4 * width, width)
    return pl.pallas_call(
        functools.partial(attend_back_kernel, patch + 1),
        grid=(count,),
        in_specs=[
            scalars(),
            frame_block((rows, width)),
            frame_block((patch, width)),
            full((slots, width)),
            full((slots, width)),
            frame_block((width, rows)),
            frame_block((8, rows)),
            frame_block((rows, width)),
            full(gains.shape),
        ]
        + [full((width, width))] * 4,
        out_specs=[frame_block((patch, width))]
        + [full((slots, width))] * 2
        + [full((8, width))]
        + packet_specs,
        out_shape=[shape_of((count, patch, width), bf16)]
        + [shape_of((slots, width), f32)] * 2
        + [shape_of((8, width), f32)]
        + packet_shapes,
        scratch_shapes=[
            pltpu.VMEM((acc_rows, width), f32),
            pltpu.VMEM((width, width), bf16),
            pltpu.VMEM((width, width), bf16),
            pltpu.VMEM((width, 3 * width), bf16),
        ],
        compiler_params=params(),
        cost_estimate=cost(25e9, 20e6),
        name="attend_back",
    )(where, normed, video, message, nmsg, ctx, lse, dresid, gains, wq, wk, wv, wo)


def message_back_kernel(
    layout, together, where_ref, *refs
):
    segs, frames, clips = layout
    pieces = refs[: segs * frames]
    (
        mw_ref, mg_ref, qkv_ref, outw_ref, big_in, out_in,
        big_ref, out_ref, mwg_ref, gain_ref, gains_ref, dclass_ref,
        classes, dmsgs, keys, values, queries, context, dcontext, dq, dk, dv, dstart,
    ) = refs[segs * frames :]
    del big_in, out_in
    width = mw_ref.shape[0]
    slots = dclass_ref.shape[0]
    me_f, me_s, me_c = where_ref[0], where_ref[1], where_ref[2]
    total = together * slots
    rows = frames * total
    steps = segs * clips // together

    def row_of(s, f, c):
        group = s * clips + c
        step, inside = group // together, group % together
        return step, pl.multiple_of(f * total + inside * slots, 16)

    for a in range(segs):
        for b in range(frames):
            for d in range(clips):
                piece = pieces[a * frames + b][d]
                step, at = row_of(me_s ^ a, me_f ^ b, me_c ^ d)
                classes[step, pl.ds(at, slots), :] = piece[:slots]
                dmsgs[step, pl.ds(at, slots), :] = piece[slots : 2 * slots]
    gain_total = jnp.zeros((slots, width), f32)
    for i in range(frames * together):
        for step in range(steps):
            gain_total += dmsgs[step, i * slots : (i + 1) * slots, :].astype(f32)
    gains_ref[...] = gain_total[slots - 4 : slots]

    index = lax.broadcasted_iota(jnp.int32, (rows, 1), 0) % slots
    columns, spread = head_columns(width), head_rows(width)
    spread_low = spread.astype(bf16)
    cut = [slice(g * total, (g + 1) * total) for g in range(frames)]
    my_step, my_at = row_of(me_s, me_f, me_c)

    def batch(step, put):
        dm = jnp.where(index < slots - 6, dmsgs[step].astype(f32), 0.0).astype(bf16)
        cls = classes[step]
        start = nn(cls, mw_ref[...]).astype(bf16)
        unit, inv = unit_norm(start.astype(f32))
        normed = (unit * mg_ref[...]).astype(bf16)
        queries[...] = nn(normed, qkv_ref[0, 0]).astype(bf16)
        keys[...] = nn(normed, qkv_ref[0, 1]).astype(bf16)
        values[...] = nn(normed, qkv_ref[0, 2]).astype(bf16)
        dcontext[...] = nt(dm, outw_ref[0])
        dk[...] = jnp.zeros(dk.shape, f32)
        dv[...] = jnp.zeros(dv.shape, f32)

        @pl.loop(0, frames)
        def _(f):
            here = pl.ds(pl.multiple_of(f * total, 16), total)
            query = queries[here, :].astype(f32)
            dctx = dcontext[here, :]
            probs = message_probs(message_scores(query, [keys[c, :] for c in cut], columns))
            wide = [nn(p.astype(bf16), spread_low) for p in probs]
            context[here, :] = functools.reduce(
                jnp.add, [w * values[c, :].astype(f32) for w, c in zip(wide, cut)]
            ).astype(bf16)
            dprobs = [exact(dctx * values[c, :].astype(f32), columns) for c in cut]
            inner = functools.reduce(jnp.add, [p * d for p, d in zip(probs, dprobs)])
            total_dq = jnp.zeros((total, width), f32)
            for g in range(frames):
                dscore = exact(probs[g] * (dprobs[g] - inner) * SCALE, spread)
                total_dq = total_dq + dscore * keys[cut[g], :].astype(f32)
                dk[cut[g], :] += dscore * query
                dv[cut[g], :] += wide[g] * dctx
            dq[here, :] = total_dq

        low_q, low_k, low_v = dq[...].astype(bf16), dk[...].astype(bf16), dv[...].astype(bf16)
        put(big_ref, (0, 0), tn(normed, low_q))
        put(big_ref, (0, 1), tn(normed, low_k))
        put(big_ref, (0, 2), tn(normed, low_v))
        put(out_ref, 0, tn(context[...], dm))
        dnormed = nt(low_q, qkv_ref[0, 0]) + nt(low_k, qkv_ref[0, 1]) + nt(low_v, qkv_ref[0, 2])
        put(gain_ref, ..., row_sum(dnormed * unit))
        dstart[...] = norm_back(unit, inv, mg_ref[...], dnormed) + dm.astype(f32)
        put(mwg_ref, ..., tn(cls, dstart[...].astype(bf16)))

        @pl.when(my_step == step)
        def _():
            dclass_ref[...] = nt(dstart[pl.ds(my_at, slots), :].astype(bf16), mw_ref[...])

    def first(ref, at, value):
        ref[at] = value

    def more(ref, at, value):
        ref[at] += value

    batch(0, first)
    if steps > 1:
        pl.loop(1, steps)(lambda step: batch(step, more))


def message_back(where, pieces, mw, mg, qkv, outw, big, out, layout, slots):
    segs, frames, clips = layout
    width = mw.shape[0]
    groups = segs * clips
    together = max(1, min(groups, 512 // (frames * slots)))
    rows = frames * together * slots
    everyone = (groups // together, rows, width)
    operands = list(pieces) + [mw, mg, qkv, outw]
    where_big = 1 + len(operands)
    return pl.pallas_call(
        functools.partial(message_back_kernel, layout, together),
        grid=(1,),
        in_specs=[scalars()]
        + [full(x.shape) for x in operands]
        + [pl.BlockSpec(memory_space=pl.ANY)] * 2,
        out_specs=[
            pl.BlockSpec((1, 3, width, width), lambda i: (0, 0, 0, 0)),
            pl.BlockSpec((1, width, width), lambda i: (0, 0, 0)),
            full((width, width)),
            full((1, width)),
            full((4, width)),
            full((slots, width)),
        ],
        out_shape=[
            shape_of(big.shape, f32),
            shape_of(out.shape, f32),
            shape_of((width, width), f32),
            shape_of((1, width), f32),
            shape_of((4, width), f32),
            shape_of((slots, width), f32),
        ],
        input_output_aliases={where_big: 0, where_big + 1: 1},
        scratch_shapes=[pltpu.VMEM(everyone, bf16)] * 2
        + [pltpu.VMEM((rows, width), bf16)] * 4
        + [pltpu.VMEM((rows, width), f32)] * 5,
        compiler_params=params(),
        cost_estimate=cost(6e9, 12e6),
        name="message_back",
    )(where, *operands, big, out)


def class_fix_kernel(count, dclass_ref, dcls_ref, grad_in, grad_ref):
    fixed = dclass_ref[...] + dcls_ref[...]
    for i in range(count):
        block = grad_in[i].astype(f32)
        grad_ref[i] = put_row(block, 0, fixed[i : i + 1]).astype(bf16)


def class_fix(dclass, dcls, grad):
    count, _, width = grad.shape
    block = pl.BlockSpec((count, 16, width), lambda i: (0, 0, 0))
    return pl.pallas_call(
        functools.partial(class_fix_kernel, count),
        grid=(1,),
        in_specs=[full(dclass.shape), full(dcls.shape), block],
        out_specs=block,
        out_shape=shape_of(grad.shape, bf16),
        input_output_aliases={2: 0},
        name="class_fix",
    )(dclass, dcls, grad)


def emit(where_ref, acc, keep_ref, send_ref):
    frames, clips, chunk = keep_ref.shape[:3]
    me_f, me_s, me_c = where_ref[0], where_ref[1], where_ref[2]
    for a, out in enumerate((keep_ref, send_ref)):
        for b in range(frames):
            for d in range(clips):
                to = ((me_s ^ a) * frames + (me_f ^ b)) * clips + (me_c ^ d)
                at = pl.multiple_of(to * chunk, 16)
                out[b, d] = acc[pl.ds(at, chunk), :].astype(bf16)


class Plan:
    def __init__(self, clips):
        self.clips = clips
        self.segs = lax.axis_size("seg")
        self.frames = lax.axis_size("frame")
        self.rings = lax.axis_size("clip")
        self.layout = (self.segs, self.frames, self.rings)
        self.devices = self.segs * self.frames * self.rings

    def chunk(self, rows):
        share = -(-rows // self.devices)
        return -(-share // 16) * 16

    def packet(self, rows, width):
        chunk = self.chunk(rows)
        shape = (self.frames, self.rings, chunk, width)
        return chunk * self.devices, [full(shape)] * 2, [shape_of(shape, bf16)] * 2


def swap(x, axis, k):
    count = lax.axis_size(axis)
    return lax.ppermute(x, axis, [(i, i ^ k) for i in range(count)])


def add_first_kernel(keep_ref, got_ref, *outs):
    for b, out in enumerate(outs):
        out[...] = (keep_ref[b].astype(f32) + got_ref[b].astype(f32)).astype(bf16)


def add_first(keep, got):
    shape = keep.shape[1:]
    return pl.pallas_call(
        add_first_kernel,
        out_shape=[shape_of(shape, bf16)] * keep.shape[0],
        compiler_params=params(),
        cost_estimate=cost(keep.size, keep.size * 6),
        name="add_first",
    )(keep, got)


def add_split_kernel(count, *refs):
    terms, outs = refs[:count], refs[count:]
    for d, out in enumerate(outs):
        total = functools.reduce(jnp.add, [t[d].astype(f32) for t in terms])
        out[...] = total.astype(bf16)


def add_split(terms):
    shape = terms[0].shape[1:]
    return pl.pallas_call(
        functools.partial(add_split_kernel, len(terms)),
        out_shape=[shape_of(shape, bf16)] * terms[0].shape[0],
        compiler_params=params(),
        cost_estimate=cost(terms[0].size * len(terms), terms[0].size * 2 * (len(terms) + 1)),
        name="add_split",
    )(*terms)


def add_last_kernel(*refs):
    refs[-1][...] = functools.reduce(jnp.add, [t[...].astype(f32) for t in refs[:-1]]).astype(bf16)


def add_last(terms):
    return pl.pallas_call(
        add_last_kernel,
        out_shape=shape_of(terms[0].shape, bf16),
        compiler_params=params(),
        cost_estimate=cost(terms[0].size * len(terms), terms[0].size * 2 * (len(terms) + 1)),
        name="add_last",
    )(*terms)


def stack_kernel(*refs):
    for d, ref in enumerate(refs[:-1]):
        refs[-1][d] = ref[...]


def stack(parts):
    return pl.pallas_call(
        stack_kernel,
        out_shape=shape_of((len(parts),) + parts[0].shape, parts[0].dtype),
        compiler_params=params(),
        cost_estimate=cost(0, parts[0].size * 4 * len(parts)),
        name="stack",
    )(*parts)


def reduce_packet(keep, send):
    got = swap(send, "seg", 1)
    mine = add_first(keep, got)
    got = [swap(mine[b], "frame", b) for b in range(1, len(mine))]
    mine = add_split([mine[0]] + got)
    got = [swap(mine[d], "clip", d) for d in range(1, len(mine))]
    return add_last([mine[0]] + got)


def gather_packet(own):
    held = stack([own] + [swap(own, "clip", d) for d in range(1, lax.axis_size("clip"))])
    held = [held] + [swap(held, "frame", b) for b in range(1, lax.axis_size("frame"))]
    return held + [swap(h, "seg", 1) for h in held]


def place(layout, where_ref, pieces, whole):
    segs, frames, clips = layout
    chunk = pieces[0].shape[1]
    me_f, me_s, me_c = where_ref[0], where_ref[1], where_ref[2]
    for a in range(segs):
        for b in range(frames):
            for d in range(clips):
                of = ((me_s ^ a) * frames + (me_f ^ b)) * clips + (me_c ^ d)
                at = pl.multiple_of(of * chunk, 16)
                whole[pl.ds(at, chunk), :] = pieces[a * frames + b][d]


def unpack_mlp_kernel(layout, where_ref, *refs):
    count = layout[0] * layout[1]
    up_ref, down_ref, whole = refs[count:]
    width, ff = up_ref.shape
    place(layout, where_ref, refs[:count], whole)
    blocks = ff // width
    for c in range(blocks):
        span = slice(c * width, (c + 1) * width)
        up_ref[:, span] = whole[span, :].astype(f32)
        other = whole[(blocks + c) * width : (blocks + c + 1) * width, :]
        down_ref[span, :] = other.astype(f32).T


def unpack_mlp(where, pieces, width, ff, plan):
    whole = plan.devices * pieces[0].shape[1]
    return pl.pallas_call(
        functools.partial(unpack_mlp_kernel, plan.layout),
        grid=(1,),
        in_specs=[scalars()] + [full(x.shape) for x in pieces],
        out_specs=[full((width, ff)), full((ff, width))],
        out_shape=[shape_of((width, ff), f32), shape_of((ff, width), f32)],
        scratch_shapes=[pltpu.VMEM((whole, width), bf16)],
        compiler_params=params(),
        cost_estimate=cost(0, 8e6),
        name="unpack_mlp",
    )(where, *pieces)


def unpack_four_kernel(layout, flip, held, where_ref, *refs):
    count = layout[0] * layout[1]
    big_ref, out_ref, whole = refs[count + held :]
    width = out_ref.shape[-1]
    place(layout, where_ref, refs[:count], whole)
    for j in range(3):
        block = whole[j * width : (j + 1) * width, :].astype(f32)
        big_ref[0, j] = block.T if flip else block
    out_ref[0] = whole[3 * width : 4 * width, :].astype(f32)


def unpack_four(where, pieces, layer, flip, width, plan, held=()):
    whole = plan.devices * pieces[0].shape[1]
    at = 1 + len(pieces)
    return pl.pallas_call(
        functools.partial(unpack_four_kernel, plan.layout, flip, len(held)),
        grid=(1,),
        in_specs=[scalars()]
        + [full(x.shape) for x in pieces]
        + [pl.BlockSpec(memory_space=pl.ANY)] * len(held),
        out_specs=[
            pl.BlockSpec((1, 3, width, width), lambda i: (layer, 0, 0, 0)),
            pl.BlockSpec((1, width, width), lambda i: (layer, 0, 0)),
        ],
        out_shape=[shape_of((3, 3, width, width), f32), shape_of((3, width, width), f32)],
        input_output_aliases={at + i: i for i in range(len(held))},
        scratch_shapes=[pltpu.VMEM((whole, width), bf16)],
        compiler_params=params(),
        cost_estimate=cost(0, 5e6),
        name="unpack_four",
    )(where, *pieces, *held)


def last_rows_kernel(gain_a, gain_b, gain_c, dmsg_ref, classes_ref, out_ref):
    slots, width = dmsg_ref.shape
    filled = dmsg_ref[0 : slots - 6, :]
    rows = [
        filled,
        jnp.zeros((2, width), f32),
        gain_a[0:1, :],
        gain_b[0:1, :],
        gain_b[1:2, :],
        gain_c[0:1, :],
    ]
    out_ref[slots:, :] = jnp.concatenate(rows, axis=0).astype(bf16)
    out_ref[:slots, :] = classes_ref[...]


def last_rows(gain_a, gain_b, gain_c, dmsg, classes):
    slots, width = dmsg.shape
    return pl.pallas_call(
        last_rows_kernel,
        out_shape=shape_of((2 * slots, width), bf16),
        name="last_rows",
    )(gain_a, gain_b, gain_c, dmsg, classes)


def local(
    video, captions, caption_lengths, message_weight, message_gain, qkv_weights, out_weights,
    mlp_up, mlp_down, gains, video_cot, caption_cot,
):
    micro, clips, per_frame, patch, width = video.shape
    count = micro * clips * per_frame
    ff = mlp_up.shape[1]
    plan = Plan(clips)
    tokens = patch + 1
    rows = -(-tokens // 16) * 16
    slots = -(-(count + 6) // 16) * 16
    where = jnp.stack(
        [lax.axis_index("frame"), lax.axis_index("seg"), lax.axis_index("clip")]
    ).astype(jnp.int32)
    frames = video.reshape(count, patch, width)
    cots = video_cot.reshape(count, patch, width)
    caps = captions.reshape(-1, width)
    cap_cots = caption_cot.reshape(-1, width)
    lengths = caption_lengths.reshape(micro, -1)
    gain = message_gain.reshape(1, width)
    wq, wk, wv = qkv_weights[1, 0], qkv_weights[1, 1], qkv_weights[1, 2]
    wo = out_weights[1]

    classes = class_rows(frames, slots)
    gathered = [classes] + [swap(classes, "frame", b) for b in range(1, plan.frames)]
    normed, keys, values_t = norm_tokens(frames, gains, wk, wv, rows)
    message, nmsg, visual, final = first_rows(
        gathered, message_weight, gain, qkv_weights, out_weights, mlp_up, mlp_down, gains,
        keys, values_t, tokens,
    )
    visuals = [visual] + [swap(visual, "frame", b) for b in range(1, plan.frames)]
    resid, ctx, lse = attend(normed, frames, message, nmsg, wq, wk, wv, wo, tokens)
    results = captions_step(
        where, lengths, visuals, caps, cap_cots, qkv_weights, out_weights, gains, plan
    )
    caption_out, caption_grad, gain_c = results[:3]
    parts = list(results[3:-2])
    caption_packet = results[-2:]
    parts = [parts[0]] + [swap(parts[b], "frame", b) for b in range(1, plan.frames)]
    video_out, dresid, gain_b, keep, send = mlp_step(
        where, resid, cots, final, gains, mlp_up, mlp_down, parts, plan
    )
    caption_sum = gather_packet(reduce_packet(*caption_packet))
    mlp_sum = gather_packet(reduce_packet(keep, send))
    grad, dmsg, dcls, gain_a, keep, send = attend_back(
        where, normed, frames, message, nmsg, ctx, lse, dresid, gains, wq, wk, wv, wo, plan
    )
    rest = last_rows(gain_a, gain_b, gain_c, dmsg, classes)
    held = stack([rest] + [swap(rest, "clip", d) for d in range(1, plan.rings)])
    held = [held] + [swap(held, "frame", b) for b in range(1, plan.frames)]
    held = held + [swap(h, "seg", 1) for h in held]
    frame_sum = gather_packet(reduce_packet(keep, send))

    up_grad, down_grad = unpack_mlp(where, mlp_sum, width, ff, plan)
    big, out = unpack_four(where, caption_sum, 2, False, width, plan)
    big, out, mw_grad, mg_grad, gains_grad, dclass = message_back(
        where, held, message_weight, gain, qkv_weights, out_weights, big, out, plan.layout, slots
    )
    big, out = unpack_four(where, frame_sum, 1, True, width, plan, (big, out))
    grad = class_fix(dclass, dcls, grad)
    return (
        video_out.reshape(video.shape),
        caption_out.reshape(captions.shape),
        grad.reshape(video.shape),
        caption_grad.reshape(captions.shape),
        mw_grad,
        mg_grad.reshape(width),
        big,
        out,
        up_grad,
        down_grad,
        gains_grad,
    )


def solution(mesh):
    rows = P(None, ("clip", "seg"), "frame", None, None)
    caps = P(None, ("clip", "seg"), "frame", None)
    return jax.shard_map(
        local,
        mesh=mesh,
        in_specs=(rows, caps, P(None, ("clip", "seg"), None)) + (P(),) * 7 + (rows, caps),
        out_specs=(rows, caps, rows, caps) + (P(),) * 7,
        check_vma=False,
    )
```

```python
import functools

import jax
import jax.numpy as jnp
from jax import lax
from jax.experimental import pallas as pl
from jax.experimental.pallas import tpu as pltpu
from jax.sharding import PartitionSpec as P

HEADS = 6
HEAD_DIM = 64
EPS = 1e-05
SCALE = 0.125
MASKED = -1e30
BIG = 56 * 1024 * 1024

f32 = jnp.float32
bf16 = jnp.bfloat16


def nn(a, b):
    return lax.dot_general(a, b, (((1,), (0,)), ((), ())), preferred_element_type=f32)


def nt(a, b):
    return lax.dot_general(a, b, (((1,), (1,)), ((), ())), preferred_element_type=f32)


def tn(a, b):
    return lax.dot_general(a, b, (((0,), (0,)), ((), ())), preferred_element_type=f32)


def exact(a, b):
    return lax.dot_general(
        a, b, (((1,), (0,)), ((), ())), precision=lax.Precision.HIGHEST, preferred_element_type=f32
    )


def unit_norm(x):
    center = x - jnp.mean(x, axis=-1, keepdims=True)
    inv = lax.rsqrt(jnp.mean(center * center, axis=-1, keepdims=True) + EPS)
    return center * inv, inv


def norm_back(unit, inv, gain, dy):
    du = dy * gain
    mean_du = jnp.mean(du, axis=-1, keepdims=True)
    mean_dot = jnp.mean(du * unit, axis=-1, keepdims=True)
    return inv * (du - mean_du - unit * mean_dot)


def row_sum(x):
    return jnp.sum(x, axis=0, keepdims=True)


def sigmoid(x):
    return 0.5 + 0.5 * jnp.tanh(0.5 * x)


def head_mask(shape, lane_dim, head):
    lane = lax.broadcasted_iota(jnp.int32, shape, lane_dim)
    return (lane >= head * HEAD_DIM) & (lane < (head + 1) * HEAD_DIM)


def head_columns(width):
    lane = lax.broadcasted_iota(jnp.int32, (width, 128), 0)
    col = lax.broadcasted_iota(jnp.int32, (width, 128), 1)
    return ((lane >= col * HEAD_DIM) & (lane < (col + 1) * HEAD_DIM)).astype(f32)


def head_rows(width):
    col = lax.broadcasted_iota(jnp.int32, (128, width), 0)
    lane = lax.broadcasted_iota(jnp.int32, (128, width), 1)
    return ((lane >= col * HEAD_DIM) & (lane < (col + 1) * HEAD_DIM)).astype(f32)


def pad_rows(x, rows):
    if x.shape[0] == rows:
        return x
    return jnp.concatenate([x, jnp.zeros((rows - x.shape[0], x.shape[1]), x.dtype)], axis=0)


def put_row(block, at, row):
    top = at // 16 * 16
    tail = block[top : top + 16]
    index = lax.broadcasted_iota(jnp.int32, tail.shape, 0)
    tail = jnp.where(index == at - top, row, tail)
    pieces = [tail]
    if top:
        pieces.insert(0, block[:top])
    if top + 16 < block.shape[0]:
        pieces.append(block[top + 16 :])
    return jnp.concatenate(pieces, axis=0) if len(pieces) > 1 else tail


def full(shape):
    return pl.BlockSpec(shape, lambda *_: (0,) * len(shape))


def frame_block(shape):
    return pl.BlockSpec((1,) + shape, lambda i, *_: (i, 0, 0))


def frames_block(batch, shape):
    return pl.BlockSpec((batch,) + shape, lambda i, *_: (i, 0, 0))


def stagger(jobs, stages, gap):
    for at in range(len(jobs) + (len(stages) - 1) * gap):
        for k, stage in enumerate(stages):
            j = at - k * gap
            if 0 <= j < len(jobs):
                stage(jobs[j])


def share_of(count, most):
    return max(b for b in range(1, most + 1) if count % b == 0)


def square(width, *at):
    return pl.BlockSpec((None,) * len(at) + (width, width), lambda *_: at + (0, 0))


def scalars():
    return pl.BlockSpec(memory_space=pltpu.SMEM)


def shape_of(shape, dtype):
    return jax.ShapeDtypeStruct(shape, dtype)


def params(limit=BIG):
    return pltpu.CompilerParams(vmem_limit_bytes=limit)


def cost(flops, nbytes):
    return pl.CostEstimate(flops=int(flops), bytes_accessed=int(nbytes), transcendentals=0)


def class_kernel(video_ref, out_ref):
    clips, _, micro, width = video_ref.shape
    rows = [video_ref[c, 0, m : m + 1, :].astype(f32) for m in range(micro) for c in range(clips)]
    out_ref[...] = pad_rows(jnp.concatenate(rows, axis=0), out_ref.shape[0]).astype(bf16)


def class_rows(video, slots):
    micro, clips, per_frame, patch, width = video.shape
    turned = video.transpose(1, 2, 3, 0, 4).reshape(clips * per_frame, patch, micro, width)
    return pl.pallas_call(
        class_kernel,
        grid=(1,),
        in_specs=[pl.BlockSpec((clips * per_frame, 1, micro, width), lambda i: (0, 0, 0, 0))],
        out_specs=full((slots, width)),
        out_shape=shape_of((slots, width), bf16),
        name="class_rows",
    )(turned)


def norm_kernel(video_ref, gains_ref, wk_ref, wv_ref, normed_ref, kv_ref, wkv):
    batch, rows, width = normed_ref.shape

    @pl.when(pl.program_id(0) == 0)
    def _():
        wkv[:, :width] = wk_ref[...]
        wkv[:, width:] = wv_ref[...]

    parts = []
    for i in range(batch):
        unit, _ = unit_norm(video_ref[i].astype(f32))
        parts.append(pad_rows(unit * gains_ref[0:1, :], rows).astype(bf16))
        normed_ref[i] = parts[i]
    normed = jnp.concatenate(parts, axis=0)
    kv_ref[...] = nn(normed, wkv[...]).astype(bf16).reshape(batch, rows, 2 * width)


def norm_tokens(video, gains, qkv, rows):
    count, patch, width = video.shape
    batch = share_of(count, 5)
    return pl.pallas_call(
        norm_kernel,
        grid=(count // batch,),
        in_specs=[
            frames_block(batch, (patch, width)),
            full(gains.shape),
            square(width, 1, 1),
            square(width, 1, 2),
        ],
        out_specs=[
            frames_block(batch, (rows, width)),
            frames_block(batch, (rows, 2 * width)),
        ],
        out_shape=[
            shape_of((count, rows, width), bf16),
            shape_of((count, rows, 2 * width), bf16),
        ],
        scratch_shapes=[pltpu.VMEM((width, 2 * width), bf16)],
        compiler_params=params(),
        cost_estimate=cost(4 * count * rows * width * width, 8 * count * rows * width),
        name="norm_tokens",
    )(video, gains, qkv, qkv)


def message_scores(query, keys, columns):
    return [exact(query.astype(f32) * key.astype(f32), columns) * SCALE for key in keys]


def message_probs(scores):
    top = functools.reduce(jnp.maximum, scores)
    expo = [jnp.exp(score - top) for score in scores]
    total = functools.reduce(jnp.add, expo)
    return [e / total for e in expo]


def first_kernel(
    pieces, count, tokens, *refs
):
    gathered = refs[:pieces]
    (
        mw_ref, mg_ref, qkv_ref, outw_ref, up_ref, down_ref, gains_ref, kv_ref,
        message_ref, nmsg_ref, kvmsg_ref, visual_ref, final_ref, ctx,
    ) = refs[pieces:]
    width = mw_ref.shape[0]
    slots = gathered[0].shape[0]
    rows = kv_ref.shape[1]
    classes = jnp.concatenate([g[...] for g in gathered], axis=0)
    start = nn(classes, mw_ref[...]).astype(bf16)
    unit, _ = unit_norm(start.astype(f32))
    normed = (unit * mg_ref[...]).astype(bf16)
    keys = nn(normed, qkv_ref[0, 1]).astype(bf16)
    values = nn(normed, qkv_ref[0, 2]).astype(bf16)
    query = nn(normed[:slots], qkv_ref[0, 0]).astype(bf16)
    columns, spread = head_columns(width), head_rows(width).astype(bf16)
    cut = [slice(g * slots, (g + 1) * slots) for g in range(pieces)]
    probs = message_probs(message_scores(query, [keys[c] for c in cut], columns))
    context = functools.reduce(
        jnp.add,
        [nn(p.astype(bf16), spread) * values[c].astype(f32) for p, c in zip(probs, cut)],
    ).astype(bf16)
    message = start[:slots].astype(f32) + nn(context, outw_ref[0])
    message_ref[...] = message
    unit, _ = unit_norm(message)
    nmsg = (unit * gains_ref[0:1, :]).astype(bf16)
    nmsg_ref[...] = nmsg.astype(f32)
    kmsg = nn(nmsg, qkv_ref[1, 1]).astype(bf16).astype(f32)
    vmsg = nn(nmsg, qkv_ref[1, 2]).astype(bf16).astype(f32)

    own = gathered[0][...].astype(f32)
    unit, _ = unit_norm(own)
    qcls = nn((unit * gains_ref[0:1, :]).astype(bf16), qkv_ref[1, 0]).astype(bf16).astype(f32) * SCALE
    head = lax.broadcasted_iota(jnp.int32, (16, width), 0)
    lane = lax.broadcasted_iota(jnp.int32, (16, width), 1)
    mine = (lane >= head * HEAD_DIM) & (lane < (head + 1) * HEAD_DIM)
    token = lax.broadcasted_iota(jnp.int32, (16, rows), 1)
    ctx[...] = jnp.zeros(ctx.shape, f32)
    kvmsg_ref[:, :width] = kmsg
    kvmsg_ref[:, width:] = vmsg
    queries = [jnp.where(mine, qcls[i : i + 1], 0.0) for i in range(count)]
    scores = [nt(queries[i].astype(bf16), kv_ref[i, :, :width]) for i in range(count)]
    probs = []
    for i in range(count):
        last = jnp.sum(queries[i] * kmsg[i : i + 1], axis=1, keepdims=True)
        score = jnp.where(token == tokens - 1, last, scores[i])
        score = jnp.where(token < tokens, score, MASKED)
        expo = jnp.exp(score - jnp.max(score, axis=1, keepdims=True))
        probs.append((expo / jnp.sum(expo, axis=1, keepdims=True)).astype(bf16))
    outs = [nn(probs[i], kv_ref[i, :, width:]) for i in range(count)]
    for i in range(count):
        extra = jnp.sum(
            jnp.where(token == tokens - 1, probs[i].astype(f32), 0.0), axis=1, keepdims=True
        )
        out = outs[i] + extra * vmsg[i : i + 1]
        ctx[i : i + 1, :] = row_sum(jnp.where(mine, out, 0.0))
    resid = own + nn(ctx[...].astype(bf16), outw_ref[1])
    unit, _ = unit_norm(resid)
    hidden = nn((unit * gains_ref[1:2, :]).astype(bf16), up_ref[...])
    active = (hidden * sigmoid(1.702 * hidden)).astype(bf16)
    final = resid + nn(active, down_ref[...])
    final_ref[...] = final
    unit, _ = unit_norm(final)
    visual_ref[...] = (unit * gains_ref[2:3, :]).astype(bf16)


def first_rows(gathered, mw, mg, qkv, outw, up, down, gains, kv, tokens):
    count, width = kv.shape[0], mw.shape[0]
    slots = gathered[0].shape[0]
    operands = list(gathered) + [mw, mg, qkv, outw, up, down, gains, kv]
    return pl.pallas_call(
        functools.partial(first_kernel, len(gathered), count, tokens),
        grid=(1,),
        in_specs=[full(x.shape) for x in operands],
        out_specs=[full((slots, width))] * 2 + [full((slots, 2 * width))] + [full((slots, width))] * 2,
        out_shape=[
            shape_of((slots, width), f32),
            shape_of((slots, width), f32),
            shape_of((slots, 2 * width), f32),
            shape_of((slots, width), bf16),
            shape_of((slots, width), f32),
        ],
        scratch_shapes=[pltpu.VMEM((slots, width), f32)],
        compiler_params=params(),
        cost_estimate=cost(4e9, 12e6),
        name="first_rows",
    )(*operands)


def with_message(block, rows_ref, tokens, frame):
    top = (tokens - 1) // 16 * 16
    tail = block[top : top + 16].astype(f32)
    index = lax.broadcasted_iota(jnp.int32, tail.shape, 0)
    tail = jnp.where(index == tokens - 1 - top, rows_ref[pl.ds(frame, 1), :], tail).astype(bf16)
    pieces = [block[:top], tail]
    if top + 16 < block.shape[0]:
        pieces.append(block[top + 16 :])
    return jnp.concatenate(pieces, axis=0)


def masked_tail(scores, tokens):
    top = tokens // 16 * 16
    if top >= scores.shape[0]:
        return scores
    tail = scores[top:]
    index = lax.broadcasted_iota(jnp.int32, tail.shape, 0)
    return jnp.concatenate([scores[:top], jnp.where(index < tokens - top, tail, MASKED)], axis=0)


def half_pair(block_t, head):
    own = block_t[head * HEAD_DIM : (head + 1) * HEAD_DIM]
    none = jnp.zeros(own.shape, own.dtype)
    return jnp.concatenate([own, none] if head % 2 == 0 else [none, own], axis=0)


def pair_lanes(block, head):
    at = head // 2 * 2 * HEAD_DIM
    return block[:, at : at + 2 * HEAD_DIM]


def attend_kernel(
    tokens, normed_ref, kv_ref, video_ref, message_ref, nmsg_ref, kvmsg_ref, wq_ref, wv_ref, wo_ref,
    resid_ref, ctx_ref, lse_ref, wqt, wvt,
):
    step = pl.program_id(0)

    @pl.when(step == 0)
    def _():
        wqt[...] = wq_ref[...].T
        wvt[...] = wv_ref[...].T

    batch, rows, width = normed_ref.shape
    normed, keys = [], []
    for i in range(batch):
        frame = step * batch + i
        normed.append(with_message(normed_ref[i], nmsg_ref, tokens, frame))
        keys.append(with_message(kv_ref[i], kvmsg_ref, tokens, frame))
    queries_t = [nt(wqt[...], n).astype(bf16) * jnp.bfloat16(SCALE) for n in normed]
    values_t = [nt(wvt[...], n).astype(bf16) for n in normed]
    jobs = [(i, h) for i in range(batch) for h in range(HEADS)]
    contexts, stats, scores, expos, totals = {}, {}, {}, {}, {}

    def score(job):
        i, head = job
        scores[job] = nn(pair_lanes(keys[i], head), half_pair(queries_t[i], head))

    def soften(job):
        one = masked_tail(scores.pop(job), tokens)
        top = jnp.max(one, axis=0, keepdims=True)
        expo = jnp.exp(one - top)
        totals[job] = row_sum(expo)
        expos[job] = expo.astype(bf16)
        stats[job] = top + jnp.log(totals[job])

    def mix(job):
        i, head = job
        own = values_t[i][head * HEAD_DIM : (head + 1) * HEAD_DIM]
        contexts[job] = nn(own, expos.pop(job)) * (1.0 / totals[job])

    stagger(jobs, [score, soften, mix], 3)
    for i in range(batch):
        context_t = jnp.concatenate([contexts[i, h] for h in range(HEADS)], axis=0).astype(bf16)
        ctx_ref[i] = context_t
        pad = [jnp.zeros((8 - HEADS, rows), f32)]
        lse_ref[i] = jnp.concatenate([stats[i, h] for h in range(HEADS)] + pad, axis=0)
        row = message_ref[pl.ds(step * batch + i, 1), :]
        base = put_row(pad_rows(video_ref[i].astype(f32), rows), tokens - 1, row)
        resid_ref[i] = base + tn(context_t, wo_ref[...])


def attend(normed, kv, video, message, nmsg, kvmsg, qkv, outw, tokens):
    count, rows, width = normed.shape
    slots = message.shape[0]
    batch = share_of(count, 2)
    return pl.pallas_call(
        functools.partial(attend_kernel, tokens),
        grid=(count // batch,),
        in_specs=[
            frames_block(batch, (rows, width)),
            frames_block(batch, (rows, 2 * width)),
            frames_block(batch, video.shape[1:]),
            full((slots, width)),
            full((slots, width)),
            full((slots, 2 * width)),
            square(width, 1, 0),
            square(width, 1, 2),
            square(width, 1),
        ],
        out_specs=[
            frames_block(batch, (rows, width)),
            frames_block(batch, (width, rows)),
            frames_block(batch, (8, rows)),
        ],
        out_shape=[
            shape_of((count, rows, width), f32),
            shape_of((count, width, rows), bf16),
            shape_of((count, 8, rows), f32),
        ],
        scratch_shapes=[pltpu.VMEM((width, width), bf16)] * 2,
        compiler_params=params(),
        cost_estimate=cost(14e9, 10e6),
        name="attend",
    )(normed, kv, video, message, nmsg, kvmsg, qkv, qkv, outw)


def caption_kernel(
    pieces, groups, clips, local, where_ref, lengths_ref, *refs
):
    gathered = refs[:pieces]
    caps_ref, cot_ref, qkv_ref, outw_ref, gains_ref = refs[pieces : pieces + 5]
    out_ref, grad_ref, gain_ref = refs[pieces + 5 : pieces + 8]
    part_refs = refs[pieces + 8 : pieces + 8 + pieces]
    keep_ref, send_ref, acc = refs[pieces + 8 + pieces :]
    width = caps_ref.shape[1]
    slots = gathered[0].shape[0]
    count = caps_ref.shape[0]
    keys_n = pieces * slots
    runs = lengths_ref.shape[1]

    token = lax.broadcasted_iota(jnp.int32, (count, keys_n), 0)
    key = lax.broadcasted_iota(jnp.int32, (count, keys_n), 1)
    slot = key % slots
    group = token // local
    position = token - group * local + where_ref[0] * local
    document = jnp.zeros((count, keys_n), jnp.int32)
    for m in range(groups):
        end = jnp.int32(0)
        for j in range(runs):
            end = end + lengths_ref[m, j]
            document = document + jnp.where((group == m) & (position >= end), 1, 0)
    allowed = slot == group * clips + document % clips
    valid = (document[:, 0:1] < runs - 1).astype(f32)

    pack = caps_ref[...].astype(f32)
    unit, inv = unit_norm(pack)
    gain = gains_ref[3:4, :]
    normed = (unit * gain).astype(bf16)
    visual = jnp.concatenate([g[...] for g in gathered], axis=0)
    queries = nn(normed, qkv_ref[2, 0]).astype(bf16)
    keys = nn(visual, qkv_ref[2, 1]).astype(bf16)
    values = nn(visual, qkv_ref[2, 2]).astype(bf16)

    masks = [head_mask((count, width), 1, h) for h in range(HEADS)]
    zero = jnp.zeros((count, width), bf16)

    def by_head(x):
        return jnp.concatenate([jnp.where(m, x, zero) for m in masks], axis=0)

    def merge(x):
        cut = [x[h * count : (h + 1) * count] for h in range(HEADS)]
        return functools.reduce(jnp.add, [jnp.where(m, c, 0.0) for m, c in zip(masks, cut)])

    allowed_all = jnp.concatenate([allowed.astype(jnp.int32)] * HEADS, axis=0) > 0
    split_q = by_head(queries)
    scores = jnp.where(allowed_all, nt(split_q, keys) * SCALE, MASKED)
    expo = jnp.exp(scores - jnp.max(scores, axis=1, keepdims=True))
    probs = expo / jnp.sum(expo, axis=1, keepdims=True)
    low = probs.astype(bf16)
    context = merge(nn(low, values)).astype(bf16)
    out_ref[...] = (pack + valid * nn(context, outw_ref[2])).astype(bf16)

    cot = cot_ref[...].astype(f32)
    branch = (cot * valid).astype(bf16)
    split_d = by_head(nt(branch, outw_ref[2]).astype(bf16))
    dvalues = tn(low, split_d)
    dprobs = nt(split_d, values)
    dscores = probs * (dprobs - jnp.sum(dprobs * probs, axis=1, keepdims=True))
    dscores = jnp.where(allowed_all, dscores, 0.0).astype(bf16)
    dqueries = (merge(nn(dscores, keys)) * SCALE).astype(bf16)
    dkeys = tn(dscores, split_q) * SCALE
    dnormed = nt(dqueries, qkv_ref[2, 0])
    grad_ref[...] = (cot + norm_back(unit, inv, gain, dnormed)).astype(bf16)
    gain_ref[...] = jnp.concatenate([row_sum(dnormed * unit), jnp.zeros((7, width), f32)], axis=0)
    low_k, low_v = dkeys.astype(bf16), dvalues.astype(bf16)
    part = nt(low_k, qkv_ref[2, 1]) + nt(low_v, qkv_ref[2, 2])
    for g in range(pieces):
        part_refs[g][...] = part[g * slots : (g + 1) * slots]
    if acc.shape[0] > 4 * width:
        acc[...] = jnp.zeros(acc.shape, f32)
    acc[0:width, :] = tn(normed, dqueries)
    acc[width : 2 * width, :] = tn(visual, low_k)
    acc[2 * width : 3 * width, :] = tn(visual, low_v)
    acc[3 * width : 4 * width, :] = tn(context, branch)
    emit(where_ref, acc, keep_ref, send_ref)


def captions_step(where, lengths, gathered, caps, cot, qkv, outw, gains, plan):
    count, width = caps.shape
    groups = lengths.shape[0]
    pieces = len(gathered)
    slots = gathered[0].shape[0]
    operands = list(gathered) + [caps, cot, qkv, outw, gains]
    acc_rows, packet_specs, packet_shapes = plan.packet(4 * width, width)
    return pl.pallas_call(
        functools.partial(caption_kernel, pieces, groups, plan.clips, count // groups),
        grid=(1,),
        in_specs=[scalars(), scalars()] + [full(x.shape) for x in operands],
        out_specs=[full((count, width))] * 2
        + [full((8, width))]
        + [full((slots, width))] * pieces
        + packet_specs,
        out_shape=[shape_of((count, width), bf16)] * 2
        + [shape_of((8, width), f32)]
        + [shape_of((slots, width), f32)] * pieces
        + packet_shapes,
        scratch_shapes=[pltpu.VMEM((acc_rows, width), f32)],
        compiler_params=params(),
        cost_estimate=cost(4e9, 8e6),
        name="captions_step",
    )(where, lengths, *operands)


def mlp_kernel(
    pieces, patch, ff, where_ref, resid_ref, cot_ref, final_ref, gains_ref, up_ref, down_ref, *refs
):
    parts = refs[:pieces]
    more_keep, more_send, out_ref, dresid_ref, gain_ref, keep_ref, send_ref, acc, dcls = refs[pieces:]
    step = pl.program_id(0)
    batch, rows, width = resid_ref.shape
    wide = acc.shape[1]
    blocks = ff // wide

    @pl.when(step == 0)
    def _():
        acc[...] = jnp.zeros(acc.shape, f32)
        dvisual = functools.reduce(jnp.add, [p[...] for p in parts])
        unit, inv = unit_norm(final_ref[...])
        dcls[...] = norm_back(unit, inv, gains_ref[2:3, :], dvisual)
        gain_ref[...] = jnp.concatenate(
            [jnp.zeros((1, width), f32), row_sum(dvisual * unit), jnp.zeros((6, width), f32)],
            axis=0,
        )

    resid = resid_ref[...].reshape(batch * rows, width)
    gain = gains_ref[1:2, :]
    unit, inv = unit_norm(resid)
    normed32 = unit * gain
    normed = normed32.astype(bf16)
    normed_t = normed32.T.astype(bf16)
    pieces_d = []
    for i in range(batch):
        one = pad_rows(cot_ref[i].astype(f32), rows)
        pieces_d.append(put_row(one, 0, one[0:1] + dcls[pl.ds(step * batch + i, 1), :]))
    dfinal = jnp.concatenate(pieces_d, axis=0)
    branch = dfinal.astype(bf16)
    branch_t = dfinal.T.astype(bf16)
    final = resid
    dnormed = jnp.zeros((batch * rows, width), f32)
    for c in range(blocks):
        span = slice(c * wide, (c + 1) * wide)
        hidden = nn(normed, up_ref[:, span])
        gate = sigmoid(1.702 * hidden)
        active = (hidden * gate).astype(bf16)
        final = final + nn(active, down_ref[span, :])
        dactive = nt(branch, down_ref[span, :])
        dhidden = (dactive * gate * (1.0 + 1.702 * hidden * (1.0 - gate))).astype(bf16)
        dnormed = dnormed + nt(dhidden, up_ref[:, span])
        acc[c * width : (c + 1) * width, :] += nn(normed_t, dhidden)
        acc[(blocks + c) * width : (blocks + c + 1) * width, :] += nn(branch_t, active)
    for i in range(batch):
        out_ref[i] = final[i * rows : i * rows + patch].astype(bf16)
    dresid = dfinal + norm_back(unit, inv, gain, dnormed)
    dresid_ref[...] = dresid.reshape(batch, rows, width)
    gain_ref[0:1, :] += row_sum(dnormed * unit)

    @pl.when(step == pl.num_programs(0) - 1)
    def _():
        emit(where_ref, acc, keep_ref, send_ref, more_keep, more_send)


def mlp_step(where, resid, cot, final, gains, up, down, parts, more, plan):
    count, rows, width = resid.shape
    patch = cot.shape[1]
    ff = up.shape[1]
    slots = final.shape[0]
    batch = share_of(count, 2)
    wide = 2 * width
    acc_rows, packet_specs, packet_shapes = plan.packet(
        2 * ff * width // wide, wide, more[0].shape[-1]
    )
    return pl.pallas_call(
        functools.partial(mlp_kernel, len(parts), patch, ff),
        grid=(count // batch,),
        in_specs=[
            scalars(),
            frames_block(batch, (rows, width)),
            frames_block(batch, (patch, width)),
            full((slots, width)),
            full(gains.shape),
            full(up.shape),
            full(down.shape),
        ]
        + [full((slots, width))] * len(parts)
        + [full(x.shape) for x in more],
        out_specs=[
            frames_block(batch, (patch, width)),
            frames_block(batch, (rows, width)),
            full((8, width)),
        ]
        + packet_specs,
        out_shape=[
            shape_of((count, patch, width), bf16),
            shape_of((count, rows, width), f32),
            shape_of((8, width), f32),
        ]
        + packet_shapes,
        scratch_shapes=[pltpu.VMEM((acc_rows, wide), f32), pltpu.VMEM((slots, width), f32)],
        compiler_params=params(),
        cost_estimate=cost(20e9, 20e6),
        name="mlp_step",
    )(where, resid, cot, final, gains, up, down, *parts, *more)


def attend_back_kernel(tokens, first, last, waits, where_ref, normed_ref, kv_ref, *refs):
    (
        video_ref, message_ref, nmsg_ref, kvmsg_ref, ctx_ref, lse_ref, dresid_ref, gains_ref,
        wq_ref, wk_ref, wv_ref, wo_ref,
    ) = refs[:12]
    refs = refs[12:]
    if first:
        carried, refs = refs[1:5], refs[5:]
    refs = refs[waits:]
    outs = refs[: 6 if last else 5]
    grad_ref, dmsg_ref, dcls_ref, gain_ref = outs[:4]
    acc, wqt, wkt, wall = refs[len(outs) :]
    here = pl.program_id(0)
    step = here + first
    batch, rows, width = dresid_ref.shape
    patch = tokens - 1

    @pl.when(here == 0)
    def _():
        wqt[...] = wq_ref[...].T
        wkt[...] = wk_ref[...].T
        wall[:, 0:width] = wq_ref[...]
        wall[:, width : 2 * width] = wk_ref[...]
        wall[:, 2 * width : 3 * width] = wv_ref[...]
        for k, ref in enumerate((dmsg_ref, dcls_ref, gain_ref, acc)):
            ref[...] = carried[k][...] if first else jnp.zeros(ref.shape, f32)

    frames = range(batch)
    normed, kv = [], []
    for i in frames:
        normed.append(with_message(normed_ref[i], nmsg_ref, tokens, step * batch + i))
        kv.append(with_message(kv_ref[i], kvmsg_ref, tokens, step * batch + i))
    branch = [dresid_ref[i].astype(bf16) for i in frames]
    queries_t = [nt(wqt[...], n).astype(bf16) * jnp.bfloat16(SCALE) for n in normed]
    dcontext_t = [nt(wo_ref[...], b).astype(bf16) for b in branch]
    keys_t = [nt(wkt[...], n).astype(bf16) for n in normed]
    acc[3 * width : 4 * width, :] += functools.reduce(
        jnp.add, [nn(ctx_ref[i], branch[i]) for i in frames]
    )
    jobs = [(i, h) for i in frames for h in range(HEADS)]
    own = [slice(h * HEAD_DIM, (h + 1) * HEAD_DIM) for h in range(HEADS)]
    scores, dprobs, low, dscores, dq, dk, dv = {}, {}, {}, {}, {}, {}, {}

    def score(job):
        i, h = job
        scores[job] = nn(pair_lanes(kv[i], h), half_pair(queries_t[i], h))
        dprobs[job] = nn(pair_lanes(kv[i], HEADS + h), half_pair(dcontext_t[i], h))

    def soften(job):
        i, h = job
        probs = jnp.exp(masked_tail(scores.pop(job), tokens) - lse_ref[i, h : h + 1, :])
        low[job] = probs.astype(bf16)
        weighted = dprobs.pop(job) * probs
        dscores[job] = (weighted - probs * row_sum(weighted)).astype(bf16)

    def mix(job):
        i, h = job
        dq[job] = nn(keys_t[i][own[h]], dscores[job]) * SCALE
        dk[job] = nt(queries_t[i][own[h]], dscores.pop(job))
        dv[job] = nt(dcontext_t[i][own[h]], low.pop(job))

    stagger(jobs, [score, soften, mix], 2)
    dall = []
    for i in frames:
        parts = [d[i, h] for d in (dq, dk, dv) for h in range(HEADS)]
        dall.append(jnp.concatenate(parts, axis=0).astype(bf16))
    acc[0 : 3 * width, :] += functools.reduce(
        jnp.add, [nn(dall[i], normed[i]) for i in frames]
    )
    gain_sum = jnp.zeros((1, width), f32)
    for i in frames:
        dnormed = nn(wall[...], dall[i]).T
        at = pl.ds(step * batch + i, 1)
        base = put_row(pad_rows(video_ref[i].astype(f32), rows), tokens - 1, message_ref[at, :])
        unit, inv = unit_norm(base)
        dtokens = dresid_ref[i] + norm_back(unit, inv, gains_ref[0:1, :], dnormed)
        gain_sum = gain_sum + row_sum(dnormed * unit)
        grad_ref[i] = dtokens[:patch].astype(bf16)
        dcls_ref[at, :] = dtokens[0:1]
        dmsg_ref[at, :] = dtokens[patch : patch + 1]
    gain_ref[0:1, :] += gain_sum

    @pl.when(here == pl.num_programs(0) - 1)
    def _():
        if last:
            emit(where_ref, acc, *outs[4:])
        else:
            outs[4][...] = acc[...]


def attend_back(
    where, normed, kv, video, message, nmsg, kvmsg, ctx, lse, dresid, gains, qkv, outw, plan,
    batch, first, steps, carried=(), after=(),
):
    count, rows, width = normed.shape
    patch = video.shape[1]
    slots = message.shape[0]
    last = (first + steps) * batch == count
    acc_rows, packet_specs, packet_shapes = plan.packet(4 * width, width)
    if not last:
        packet_specs, packet_shapes = [full((acc_rows, width))], [shape_of((acc_rows, width), f32)]

    def block(shape):
        return pl.BlockSpec((batch,) + shape, lambda i, *_: (i + first, 0, 0))

    anywhere = pl.BlockSpec(memory_space=pl.ANY)
    carry_specs = [anywhere] + [full(x.shape) for x in carried[1:]] if carried else []
    return pl.pallas_call(
        functools.partial(attend_back_kernel, patch + 1, first, last, len(after)),
        grid=(steps,),
        in_specs=[
            scalars(),
            block((rows, width)),
            block((rows, 2 * width)),
            block((patch, width)),
            full((slots, width)),
            full((slots, width)),
            full((slots, 2 * width)),
            block((width, rows)),
            block((8, rows)),
            block((rows, width)),
            full(gains.shape),
            square(width, 1, 0),
            square(width, 1, 1),
            square(width, 1, 2),
            square(width, 1),
        ]
        + carry_specs
        + [anywhere] * len(after),
        out_specs=[block((patch, width))]
        + [full((slots, width))] * 2
        + [full((8, width))]
        + packet_specs,
        out_shape=[shape_of((count, patch, width), bf16)]
        + [shape_of((slots, width), f32)] * 2
        + [shape_of((8, width), f32)]
        + packet_shapes,
        input_output_aliases={15: 0} if carried else {},
        scratch_shapes=[
            pltpu.VMEM((acc_rows, width), f32),
            pltpu.VMEM((width, width), bf16),
            pltpu.VMEM((width, width), bf16),
            pltpu.VMEM((width, 3 * width), bf16),
        ],
        compiler_params=params(),
        cost_estimate=cost(4.5e9 * steps, 4e6 * steps),
        name="attend_back",
    )(
        where, normed, kv, video, message, nmsg, kvmsg, ctx, lse, dresid, gains, qkv, qkv, qkv,
        outw, *carried, *after,
    )


def message_back_kernel(
    layout, together, where_ref, *refs
):
    segs, frames, clips = layout
    pieces = refs[: segs * frames]
    (
        mw_ref, mg_ref, qkv_ref, outw_ref, big_in, out_in,
        big_ref, out_ref, mwg_ref, gain_ref, gains_ref, dclass_ref,
        whole, classes, dmsgs, keys, values, queries, context, dcontext, dq, dk, dv, dstart,
    ) = refs[segs * frames :]
    del big_in, out_in
    width = mw_ref.shape[0]
    slots = dclass_ref.shape[0]
    chunk = pieces[0].shape[1] - 2 * slots
    place(layout, where_ref, pieces, whole, slice(0, chunk), slice(0, width))
    for j in range(3):
        big_ref[1, j] = whole[j * width : (j + 1) * width, :].astype(f32).T
    out_ref[1] = whole[3 * width : 4 * width, :].astype(f32)
    me_f, me_s, me_c = where_ref[0], where_ref[1], where_ref[2]
    total = together * slots
    rows = frames * total
    steps = segs * clips // together

    def row_of(s, f, c):
        group = s * clips + c
        step, inside = group // together, group % together
        return step, pl.multiple_of(f * total + inside * slots, 16)

    for a in range(segs):
        for b in range(frames):
            for d in range(clips):
                piece = pieces[a * frames + b][d]
                step, at = row_of(me_s ^ a, me_f ^ b, me_c ^ d)
                classes[step, pl.ds(at, slots), :] = piece[chunk : chunk + slots]
                dmsgs[step, pl.ds(at, slots), :] = piece[chunk + slots :]
    gain_total = jnp.zeros((slots, width), f32)
    for i in range(frames * together):
        for step in range(steps):
            gain_total += dmsgs[step, i * slots : (i + 1) * slots, :].astype(f32)
    gains_ref[...] = gain_total[slots - 4 : slots]

    index = lax.broadcasted_iota(jnp.int32, (rows, 1), 0) % slots
    columns, spread = head_columns(width), head_rows(width)
    spread_low = spread.astype(bf16)
    cut = [slice(g * total, (g + 1) * total) for g in range(frames)]
    my_step, my_at = row_of(me_s, me_f, me_c)

    def batch(step, put):
        dm = jnp.where(index < slots - 6, dmsgs[step].astype(f32), 0.0).astype(bf16)
        cls = classes[step]
        start = nn(cls, mw_ref[...]).astype(bf16)
        unit, inv = unit_norm(start.astype(f32))
        normed = (unit * mg_ref[...]).astype(bf16)
        queries[...] = nn(normed, qkv_ref[0, 0]).astype(bf16)
        keys[...] = nn(normed, qkv_ref[0, 1]).astype(bf16)
        values[...] = nn(normed, qkv_ref[0, 2]).astype(bf16)
        dcontext[...] = nt(dm, outw_ref[0])
        dk[...] = jnp.zeros(dk.shape, f32)
        dv[...] = jnp.zeros(dv.shape, f32)

        @pl.loop(0, frames)
        def _(f):
            here = pl.ds(pl.multiple_of(f * total, 16), total)
            query = queries[here, :].astype(f32)
            dctx = dcontext[here, :]
            probs = message_probs(message_scores(query, [keys[c, :] for c in cut], columns))
            wide = [nn(p.astype(bf16), spread_low) for p in probs]
            context[here, :] = functools.reduce(
                jnp.add, [w * values[c, :].astype(f32) for w, c in zip(wide, cut)]
            ).astype(bf16)
            dprobs = [exact(dctx * values[c, :].astype(f32), columns) for c in cut]
            inner = functools.reduce(jnp.add, [p * d for p, d in zip(probs, dprobs)])
            total_dq = jnp.zeros((total, width), f32)
            for g in range(frames):
                dscore = exact(probs[g] * (dprobs[g] - inner) * SCALE, spread)
                total_dq = total_dq + dscore * keys[cut[g], :].astype(f32)
                dk[cut[g], :] += dscore * query
                dv[cut[g], :] += wide[g] * dctx
            dq[here, :] = total_dq

        low_q, low_k, low_v = dq[...].astype(bf16), dk[...].astype(bf16), dv[...].astype(bf16)
        put(big_ref, (0, 0), tn(normed, low_q))
        put(big_ref, (0, 1), tn(normed, low_k))
        put(big_ref, (0, 2), tn(normed, low_v))
        put(out_ref, 0, tn(context[...], dm))
        dnormed = nt(low_q, qkv_ref[0, 0]) + nt(low_k, qkv_ref[0, 1]) + nt(low_v, qkv_ref[0, 2])
        put(gain_ref, ..., row_sum(dnormed * unit))
        dstart[...] = norm_back(unit, inv, mg_ref[...], dnormed) + dm.astype(f32)
        put(mwg_ref, ..., tn(cls, dstart[...].astype(bf16)))

        @pl.when(my_step == step)
        def _():
            dclass_ref[...] = nt(dstart[pl.ds(my_at, slots), :].astype(bf16), mw_ref[...])

    def first(ref, at, value):
        ref[at] = value

    def more(ref, at, value):
        ref[at] += value

    batch(0, first)
    if steps > 1:
        pl.loop(1, steps)(lambda step: batch(step, more))


def message_back(where, pieces, mw, mg, qkv, outw, big, out, layout, slots):
    segs, frames, clips = layout
    width = mw.shape[0]
    groups = segs * clips
    together = max(1, min(groups, 512 // (frames * slots)))
    rows = frames * together * slots
    everyone = (groups // together, rows, width)
    operands = list(pieces) + [mw, mg, qkv, outw]
    where_big = 1 + len(operands)
    return pl.pallas_call(
        functools.partial(message_back_kernel, layout, together),
        grid=(1,),
        in_specs=[scalars()]
        + [full(x.shape) for x in operands]
        + [pl.BlockSpec(memory_space=pl.ANY)] * 2,
        out_specs=[
            pl.BlockSpec((2, 3, width, width), lambda i: (0, 0, 0, 0)),
            pl.BlockSpec((2, width, width), lambda i: (0, 0, 0)),
            full((width, width)),
            full((1, width)),
            full((4, width)),
            full((slots, width)),
        ],
        out_shape=[
            shape_of(big.shape, f32),
            shape_of(out.shape, f32),
            shape_of((width, width), f32),
            shape_of((1, width), f32),
            shape_of((4, width), f32),
            shape_of((slots, width), f32),
        ],
        input_output_aliases={where_big: 0, where_big + 1: 1},
        scratch_shapes=[
            pltpu.VMEM((groups * frames * (pieces[0].shape[1] - 2 * slots), width), bf16)
        ]
        + [pltpu.VMEM(everyone, bf16)] * 2
        + [pltpu.VMEM((rows, width), bf16)] * 4
        + [pltpu.VMEM((rows, width), f32)] * 5,
        compiler_params=params(),
        cost_estimate=cost(6e9, 12e6),
        name="message_back",
    )(where, *operands, big, out)


def emit(where_ref, acc, keep_ref, send_ref, more_keep=None, more_send=None):
    frames, clips, chunk = keep_ref.shape[:3]
    width = acc.shape[1]
    me_f, me_s, me_c = where_ref[0], where_ref[1], where_ref[2]
    for a, out in enumerate((keep_ref, send_ref)):
        more = (more_keep, more_send)[a]
        for b in range(frames):
            for d in range(clips):
                to = ((me_s ^ a) * frames + (me_f ^ b)) * clips + (me_c ^ d)
                at = pl.multiple_of(to * chunk, 16)
                out[b, d, :, :width] = acc[pl.ds(at, chunk), :].astype(bf16)
                if more is not None:
                    out[b, d, :, width:] = more[b, d]


class Plan:
    def __init__(self, clips):
        self.clips = clips
        self.segs = lax.axis_size("seg")
        self.frames = lax.axis_size("frame")
        self.rings = lax.axis_size("clip")
        self.layout = (self.segs, self.frames, self.rings)
        self.devices = self.segs * self.frames * self.rings

    def chunk(self, rows):
        share = -(-rows // self.devices)
        return -(-share // 16) * 16

    def packet(self, rows, width, more=0):
        chunk = self.chunk(rows)
        shape = (self.frames, self.rings, chunk, width + more)
        return chunk * self.devices, [full(shape)] * 2, [shape_of(shape, bf16)] * 2


def swap(x, axis, k):
    count = lax.axis_size(axis)
    return lax.ppermute(x, axis, [(i, i ^ k) for i in range(count)])


def total(terms):
    return functools.reduce(jnp.add, [t.astype(f32) for t in terms]).astype(bf16)


def reduce_seg(keep, send):
    return [keep, swap(send, "seg", 1)]


def frame_sends(terms):
    return [total([t[b] for t in terms]) for b in range(1, terms[0].shape[0])]


def reduce_frame(terms, sends):
    return [t[0] for t in terms] + [swap(x, "frame", b + 1) for b, x in enumerate(sends)]


def reduce_clip(terms):
    count = lax.axis_size("clip")
    bit = 1
    while bit < count:
        paired = [t.reshape((-1, 2) + t.shape[1:]) for t in terms]
        send = total([p[:, 1] for p in paired])
        terms = [p[:, 0] for p in paired] + [swap(send, "clip", bit)]
        bit *= 2
    return total([t[0] for t in terms])


def gather_clip(own):
    held = own[None]
    bit = lax.axis_size("clip") // 2
    while bit:
        held = jnp.stack([held, swap(held, "clip", bit)], axis=1)
        held = held.reshape((-1,) + own.shape)
        bit //= 2
    return held


def gather_frame(held):
    return [held] + [swap(held, "frame", b) for b in range(1, lax.axis_size("frame"))]


def gather_seg(held):
    return held + [swap(h, "seg", 1) for h in held]


def place(layout, where_ref, pieces, whole, rows, lanes):
    segs, frames, clips = layout
    chunk = rows.stop - rows.start
    me_f, me_s, me_c = where_ref[0], where_ref[1], where_ref[2]
    for a in range(segs):
        for b in range(frames):
            for d in range(clips):
                of = ((me_s ^ a) * frames + (me_f ^ b)) * clips + (me_c ^ d)
                at = pl.multiple_of(of * chunk, 16)
                whole[pl.ds(at, chunk), :] = pieces[a * frames + b][d, rows, lanes]


def unpack_kernel(layout, where_ref, *refs):
    count = layout[0] * layout[1]
    pieces = refs[:count]
    up_ref, down_ref, big_ref, out_ref, whole, more = refs[count:]
    width, ff = up_ref.shape
    wide = whole.shape[1]
    rows = slice(0, pieces[0].shape[1])
    place(layout, where_ref, pieces, whole, rows, slice(0, wide))
    place(layout, where_ref, pieces, more, rows, slice(wide, wide + width))
    blocks = ff // wide
    for c in range(blocks):
        span = slice(c * wide, (c + 1) * wide)
        up_ref[:, span] = whole[c * width : (c + 1) * width, :].astype(f32)
        other = whole[(blocks + c) * width : (blocks + c + 1) * width, :]
        down_ref[span, :] = other.astype(f32).T
    for j in range(3):
        big_ref[0, j] = more[j * width : (j + 1) * width, :].astype(f32)
    out_ref[0] = more[3 * width : 4 * width, :].astype(f32)


def unpack(where, pieces, width, ff, plan):
    chunk, wide = pieces[0].shape[1:]
    everything = plan.devices * chunk
    return pl.pallas_call(
        functools.partial(unpack_kernel, plan.layout),
        grid=(1,),
        in_specs=[scalars()] + [full(x.shape) for x in pieces],
        out_specs=[
            full((width, ff)),
            full((ff, width)),
            pl.BlockSpec((1, 3, width, width), lambda i: (2, 0, 0, 0)),
            pl.BlockSpec((1, width, width), lambda i: (2, 0, 0)),
        ],
        out_shape=[
            shape_of((width, ff), f32),
            shape_of((ff, width), f32),
            shape_of((3, 3, width, width), f32),
            shape_of((3, width, width), f32),
        ],
        scratch_shapes=[
            pltpu.VMEM((everything, wide - width), bf16),
            pltpu.VMEM((everything, width), bf16),
        ],
        compiler_params=params(),
        cost_estimate=cost(2e9, 12e6),
        name="unpack",
    )(where, *pieces)


def last_rows_kernel(gain_a, gain_b, gain_c, dmsg_ref, classes_ref, out_ref):
    slots, width = dmsg_ref.shape
    filled = dmsg_ref[0 : slots - 6, :]
    rows = [
        filled,
        jnp.zeros((2, width), f32),
        gain_a[0:1, :],
        gain_b[0:1, :],
        gain_b[1:2, :],
        gain_c[0:1, :],
    ]
    out_ref[slots:, :] = jnp.concatenate(rows, axis=0).astype(bf16)
    out_ref[:slots, :] = classes_ref[...]


def last_rows(gain_a, gain_b, gain_c, dmsg, classes):
    slots, width = dmsg.shape
    return pl.pallas_call(
        last_rows_kernel,
        out_shape=shape_of((2 * slots, width), bf16),
        name="last_rows",
    )(gain_a, gain_b, gain_c, dmsg, classes)


def local(
    video, captions, caption_lengths, message_weight, message_gain, qkv_weights, out_weights,
    mlp_up, mlp_down, gains, video_cot, caption_cot,
):
    micro, clips, per_frame, patch, width = video.shape
    count = micro * clips * per_frame
    ff = mlp_up.shape[1]
    plan = Plan(clips)
    tokens = patch + 1
    rows = -(-tokens // 16) * 16
    slots = -(-(count + 6) // 16) * 16
    where = jnp.stack(
        [lax.axis_index("frame"), lax.axis_index("seg"), lax.axis_index("clip")]
    ).astype(jnp.int32)
    frames = video.reshape(count, patch, width)
    cots = video_cot.reshape(count, patch, width)
    caps = captions.reshape(-1, width)
    cap_cots = caption_cot.reshape(-1, width)
    lengths = caption_lengths.reshape(micro, -1)
    gain = message_gain.reshape(1, width)

    classes = class_rows(video, slots)
    gathered = gather_frame(classes)
    normed, kv = norm_tokens(frames, gains, qkv_weights, rows)
    message, nmsg, kvmsg, visual, final = first_rows(
        gathered, message_weight, gain, qkv_weights, out_weights, mlp_up, mlp_down, gains,
        kv, tokens,
    )
    visuals = gather_frame(visual)
    resid, ctx, lse = attend(
        normed, kv, frames, message, nmsg, kvmsg, qkv_weights, out_weights, tokens
    )
    results = captions_step(
        where, lengths, visuals, caps, cap_cots, qkv_weights, out_weights, gains, plan
    )
    caption_out, caption_grad, gain_c = results[:3]
    parts = list(results[3:-2])
    parts = [parts[0]] + [swap(parts[b], "frame", b) for b in range(1, plan.frames)]
    video_out, dresid, gain_b, keep, send = mlp_step(
        where, resid, cots, final, gains, mlp_up, mlp_down, parts, results[-2:], plan
    )
    terms = reduce_seg(keep, send)
    batch = share_of(count, 2)
    steps = count // batch
    early = min(1, steps - 1)
    back = functools.partial(
        attend_back, where, normed, kv, frames, message, nmsg, kvmsg, ctx, lse, dresid, gains,
        qkv_weights, out_weights, plan, batch,
    )
    carried = back(0, early) if early else ()
    sends = frame_sends(terms)
    grad, dmsg, dcls, gain_a, keep, send = back(early, steps - early, carried, sends)
    terms = reduce_frame(terms, sends)
    rest = last_rows(gain_a, gain_b, gain_c, dmsg, classes)
    late = reduce_seg(keep, send)
    mlp_own = reduce_clip(terms)
    late = reduce_frame(late, frame_sends(late))
    mlp_held = gather_clip(mlp_own)
    late_own = reduce_clip(late)
    mlp_all = gather_seg(gather_frame(mlp_held))
    late_all = gather_seg(gather_frame(gather_clip(jnp.concatenate([late_own, rest], axis=0))))

    up_grad, down_grad, big, out = unpack(where, mlp_all, width, ff, plan)
    big, out, mw_grad, mg_grad, gains_grad, dclass = message_back(
        where, late_all, message_weight, gain, qkv_weights, out_weights, big, out, plan.layout, slots
    )
    fixed = (dclass + dcls)[:count].astype(bf16).reshape(micro, clips, per_frame, 1, width)
    grad = lax.dynamic_update_slice(grad.reshape(video.shape), fixed, (0, 0, 0, 0, 0))
    return (
        video_out.reshape(video.shape),
        caption_out.reshape(captions.shape),
        grad,
        caption_grad.reshape(captions.shape),
        mw_grad,
        mg_grad.reshape(width),
        big,
        out,
        up_grad,
        down_grad,
        gains_grad,
    )


def solution(mesh):
    rows = P(None, ("clip", "seg"), "frame", None, None)
    caps = P(None, ("clip", "seg"), "frame", None)
    return jax.shard_map(
        local,
        mesh=mesh,
        in_specs=(rows, caps, P(None, ("clip", "seg"), None)) + (P(),) * 7 + (rows, caps),
        out_specs=(rows, caps, rows, caps) + (P(),) * 7,
        check_vma=False,
    )
```

```python
import functools

import jax
import jax.numpy as jnp
from jax import lax
from jax.experimental import pallas as pl
from jax.experimental.pallas import tpu as pltpu
from jax.sharding import PartitionSpec as P

HEADS = 6
HEAD_DIM = 64
EPS = 1e-05
SCALE = 0.125
MASKED = -1e30

f32 = jnp.float32
bf16 = jnp.bfloat16


def nn(a, b):
    return lax.dot_general(a, b, (((1,), (0,)), ((), ())), preferred_element_type=f32)


def nt(a, b):
    return lax.dot_general(a, b, (((1,), (1,)), ((), ())), preferred_element_type=f32)


def tn(a, b):
    return lax.dot_general(a, b, (((0,), (0,)), ((), ())), preferred_element_type=f32)


def exact(a, b):
    return lax.dot_general(
        a, b, (((1,), (0,)), ((), ())), precision=lax.Precision.HIGHEST, preferred_element_type=f32
    )


def unit_norm(x):
    center = x - jnp.mean(x, axis=-1, keepdims=True)
    inv = lax.rsqrt(jnp.mean(center * center, axis=-1, keepdims=True) + EPS)
    return center * inv, inv


def norm_back(unit, inv, gain, dy):
    du = dy * gain
    mean_du = jnp.mean(du, axis=-1, keepdims=True)
    mean_dot = jnp.mean(du * unit, axis=-1, keepdims=True)
    return inv * (du - mean_du - unit * mean_dot)


def row_sum(x):
    return jnp.sum(x, axis=0, keepdims=True)


def sigmoid(x):
    return 0.5 + 0.5 * jnp.tanh(0.5 * x)


def head_mask(shape, lane_dim, head):
    lane = lax.broadcasted_iota(jnp.int32, shape, lane_dim)
    return (lane >= head * HEAD_DIM) & (lane < (head + 1) * HEAD_DIM)


def head_columns(width):
    lane = lax.broadcasted_iota(jnp.int32, (width, 128), 0)
    col = lax.broadcasted_iota(jnp.int32, (width, 128), 1)
    return ((lane >= col * HEAD_DIM) & (lane < (col + 1) * HEAD_DIM)).astype(f32)


def head_rows(width):
    col = lax.broadcasted_iota(jnp.int32, (128, width), 0)
    lane = lax.broadcasted_iota(jnp.int32, (128, width), 1)
    return ((lane >= col * HEAD_DIM) & (lane < (col + 1) * HEAD_DIM)).astype(f32)


def pad_rows(x, rows):
    if x.shape[0] == rows:
        return x
    return jnp.concatenate([x, jnp.zeros((rows - x.shape[0], x.shape[1]), x.dtype)], axis=0)


def put_row(block, at, row):
    top = at // 16 * 16
    tail = block[top : top + 16]
    index = lax.broadcasted_iota(jnp.int32, tail.shape, 0)
    tail = jnp.where(index == at - top, row, tail)
    pieces = [tail]
    if top:
        pieces.insert(0, block[:top])
    if top + 16 < block.shape[0]:
        pieces.append(block[top + 16 :])
    return jnp.concatenate(pieces, axis=0) if len(pieces) > 1 else tail


def full(shape):
    return pl.BlockSpec(shape, lambda *_: (0,) * len(shape))


def frame_block(shape):
    return pl.BlockSpec((1,) + shape, lambda i, *_: (i, 0, 0))


def frames_block(batch, shape):
    return pl.BlockSpec((batch,) + shape, lambda i, *_: (i, 0, 0))


def stagger(jobs, stages, gap):
    for at in range(len(jobs) + (len(stages) - 1) * gap):
        for k, stage in enumerate(stages):
            j = at - k * gap
            if 0 <= j < len(jobs):
                stage(jobs[j])


def share_of(count, most):
    return max(b for b in range(1, most + 1) if count % b == 0)


def square(width, *at):
    return pl.BlockSpec((None,) * len(at) + (width, width), lambda *_: at + (0, 0))


def scalars():
    return pl.BlockSpec(memory_space=pltpu.SMEM)


def shape_of(shape, dtype):
    return jax.ShapeDtypeStruct(shape, dtype)


def params(mib):
    return pltpu.CompilerParams(vmem_limit_bytes=mib * 1024 * 1024)


def cost(flops, nbytes):
    return pl.CostEstimate(flops=int(flops), bytes_accessed=int(nbytes), transcendentals=0)


def class_kernel(video_ref, out_ref):
    clips, _, micro, width = video_ref.shape
    rows = [video_ref[c, 0, m : m + 1, :].astype(f32) for m in range(micro) for c in range(clips)]
    out_ref[...] = pad_rows(jnp.concatenate(rows, axis=0), out_ref.shape[0]).astype(bf16)


def class_rows(video, slots):
    micro, clips, per_frame, patch, width = video.shape
    turned = video.transpose(1, 2, 3, 0, 4).reshape(clips * per_frame, patch, micro, width)
    return pl.pallas_call(
        class_kernel,
        grid=(1,),
        in_specs=[pl.BlockSpec((clips * per_frame, 1, micro, width), lambda i: (0, 0, 0, 0))],
        out_specs=full((slots, width)),
        out_shape=shape_of((slots, width), bf16),
        name="class_rows",
    )(turned)


def norm_kernel(video_ref, gains_ref, wk_ref, wv_ref, normed_ref, kv_ref, wkv):
    batch, rows, width = normed_ref.shape

    @pl.when(pl.program_id(0) == 0)
    def _():
        wkv[:, :width] = wk_ref[...]
        wkv[:, width:] = wv_ref[...]

    parts = []
    for i in range(batch):
        unit, _ = unit_norm(video_ref[i].astype(f32))
        parts.append(pad_rows(unit * gains_ref[0:1, :], rows).astype(bf16))
        normed_ref[i] = parts[i]
    normed = jnp.concatenate(parts, axis=0)
    kv_ref[...] = nn(normed, wkv[...]).astype(bf16).reshape(batch, rows, 2 * width)


def norm_tokens(video, gains, qkv, rows):
    count, patch, width = video.shape
    batch = share_of(count, 5)
    return pl.pallas_call(
        norm_kernel,
        grid=(count // batch,),
        in_specs=[
            frames_block(batch, (patch, width)),
            full(gains.shape),
            square(width, 1, 1),
            square(width, 1, 2),
        ],
        out_specs=[
            frames_block(batch, (rows, width)),
            frames_block(batch, (rows, 2 * width)),
        ],
        out_shape=[
            shape_of((count, rows, width), bf16),
            shape_of((count, rows, 2 * width), bf16),
        ],
        scratch_shapes=[pltpu.VMEM((width, 2 * width), bf16)],
        compiler_params=params(20),
        cost_estimate=cost(4 * count * rows * width * width, 8 * count * rows * width),
        name="norm_tokens",
    )(video, gains, qkv, qkv)


def message_scores(query, keys, columns):
    return [exact(query.astype(f32) * key.astype(f32), columns) * SCALE for key in keys]


def message_probs(scores):
    top = functools.reduce(jnp.maximum, scores)
    expo = [jnp.exp(score - top) for score in scores]
    total = functools.reduce(jnp.add, expo)
    return [e / total for e in expo]


def first_kernel(
    pieces, count, tokens, *refs
):
    gathered = refs[:pieces]
    (
        mw_ref, mg_ref, qkv_ref, outw_ref, up_ref, down_ref, gains_ref, kv_ref,
        message_ref, nmsg_ref, kvmsg_ref, visual_ref, final_ref, ctx,
    ) = refs[pieces:]
    width = mw_ref.shape[0]
    slots = gathered[0].shape[0]
    rows = kv_ref.shape[1]
    classes = jnp.concatenate([g[...] for g in gathered], axis=0)
    start = nn(classes, mw_ref[...]).astype(bf16)
    unit, _ = unit_norm(start.astype(f32))
    normed = (unit * mg_ref[...]).astype(bf16)
    keys = nn(normed, qkv_ref[0, 1]).astype(bf16)
    values = nn(normed, qkv_ref[0, 2]).astype(bf16)
    query = nn(normed[:slots], qkv_ref[0, 0]).astype(bf16)
    columns, spread = head_columns(width), head_rows(width).astype(bf16)
    cut = [slice(g * slots, (g + 1) * slots) for g in range(pieces)]
    probs = message_probs(message_scores(query, [keys[c] for c in cut], columns))
    context = functools.reduce(
        jnp.add,
        [nn(p.astype(bf16), spread) * values[c].astype(f32) for p, c in zip(probs, cut)],
    ).astype(bf16)
    message = start[:slots].astype(f32) + nn(context, outw_ref[0])
    message_ref[...] = message
    unit, _ = unit_norm(message)
    nmsg = (unit * gains_ref[0:1, :]).astype(bf16)
    nmsg_ref[...] = nmsg.astype(f32)
    kmsg = nn(nmsg, qkv_ref[1, 1]).astype(bf16).astype(f32)
    vmsg = nn(nmsg, qkv_ref[1, 2]).astype(bf16).astype(f32)

    own = gathered[0][...].astype(f32)
    unit, _ = unit_norm(own)
    qcls = nn((unit * gains_ref[0:1, :]).astype(bf16), qkv_ref[1, 0]).astype(bf16).astype(f32) * SCALE
    head = lax.broadcasted_iota(jnp.int32, (16, width), 0)
    lane = lax.broadcasted_iota(jnp.int32, (16, width), 1)
    mine = (lane >= head * HEAD_DIM) & (lane < (head + 1) * HEAD_DIM)
    token = lax.broadcasted_iota(jnp.int32, (16, rows), 1)
    ctx[...] = jnp.zeros(ctx.shape, f32)
    kvmsg_ref[:, :width] = kmsg
    kvmsg_ref[:, width:] = vmsg
    queries = [jnp.where(mine, qcls[i : i + 1], 0.0) for i in range(count)]
    scores = [nt(queries[i].astype(bf16), kv_ref[i, :, :width]) for i in range(count)]
    probs = []
    for i in range(count):
        last = jnp.sum(queries[i] * kmsg[i : i + 1], axis=1, keepdims=True)
        score = jnp.where(token == tokens - 1, last, scores[i])
        score = jnp.where(token < tokens, score, MASKED)
        expo = jnp.exp(score - jnp.max(score, axis=1, keepdims=True))
        probs.append((expo / jnp.sum(expo, axis=1, keepdims=True)).astype(bf16))
    outs = [nn(probs[i], kv_ref[i, :, width:]) for i in range(count)]
    for i in range(count):
        extra = jnp.sum(
            jnp.where(token == tokens - 1, probs[i].astype(f32), 0.0), axis=1, keepdims=True
        )
        out = outs[i] + extra * vmsg[i : i + 1]
        ctx[i : i + 1, :] = row_sum(jnp.where(mine, out, 0.0))
    resid = own + nn(ctx[...].astype(bf16), outw_ref[1])
    unit, _ = unit_norm(resid)
    hidden = nn((unit * gains_ref[1:2, :]).astype(bf16), up_ref[...])
    active = (hidden * sigmoid(1.702 * hidden)).astype(bf16)
    final = resid + nn(active, down_ref[...])
    final_ref[...] = final
    unit, _ = unit_norm(final)
    visual_ref[...] = (unit * gains_ref[2:3, :]).astype(bf16)


def first_rows(gathered, mw, mg, qkv, outw, up, down, gains, kv, tokens):
    count, width = kv.shape[0], mw.shape[0]
    slots = gathered[0].shape[0]
    operands = list(gathered) + [mw, mg, qkv, outw, up, down, gains, kv]
    return pl.pallas_call(
        functools.partial(first_kernel, len(gathered), count, tokens),
        grid=(1,),
        in_specs=[full(x.shape) for x in gathered]
        + [
            full(mw.shape),
            full(mg.shape),
            pl.BlockSpec((2, 3, width, width), lambda i: (0, 0, 0, 0)),
            pl.BlockSpec((2, width, width), lambda i: (0, 0, 0)),
            full(up.shape),
            full(down.shape),
            full(gains.shape),
            full(kv.shape),
        ],
        out_specs=[full((slots, width))] * 2 + [full((slots, 2 * width))] + [full((slots, width))] * 2,
        out_shape=[
            shape_of((slots, width), f32),
            shape_of((slots, width), f32),
            shape_of((slots, 2 * width), f32),
            shape_of((slots, width), bf16),
            shape_of((slots, width), f32),
        ],
        scratch_shapes=[pltpu.VMEM((slots, width), f32)],
        compiler_params=params(16),
        cost_estimate=cost(4e9, 12e6),
        name="first_rows",
    )(*operands)


def with_message(block, rows_ref, tokens, frame):
    top = (tokens - 1) // 16 * 16
    tail = block[top : top + 16].astype(f32)
    index = lax.broadcasted_iota(jnp.int32, tail.shape, 0)
    tail = jnp.where(index == tokens - 1 - top, rows_ref[pl.ds(frame, 1), :], tail).astype(bf16)
    pieces = [block[:top], tail]
    if top + 16 < block.shape[0]:
        pieces.append(block[top + 16 :])
    return jnp.concatenate(pieces, axis=0)


def masked_tail(scores, tokens):
    top = tokens // 16 * 16
    if top >= scores.shape[0]:
        return scores
    tail = scores[top:]
    index = lax.broadcasted_iota(jnp.int32, tail.shape, 0)
    return jnp.concatenate([scores[:top], jnp.where(index < tokens - top, tail, MASKED)], axis=0)


def half_pair(block_t, head):
    own = block_t[head * HEAD_DIM : (head + 1) * HEAD_DIM]
    none = jnp.zeros(own.shape, own.dtype)
    return jnp.concatenate([own, none] if head % 2 == 0 else [none, own], axis=0)


def pair_lanes(block, head):
    at = head // 2 * 2 * HEAD_DIM
    return block[:, at : at + 2 * HEAD_DIM]


def attend_kernel(
    tokens, normed_ref, kv_ref, video_ref, message_ref, nmsg_ref, kvmsg_ref, wq_ref, wv_ref, wo_ref,
    *refs,
):
    resid_ref, ctx_ref, lse_ref, wqt, wvt = refs[-5:]
    step = pl.program_id(0)

    @pl.when(step == 0)
    def _():
        wqt[...] = wq_ref[...].T
        wvt[...] = wv_ref[...].T

    batch, rows, width = normed_ref.shape
    normed, keys = [], []
    for i in range(batch):
        frame = step * batch + i
        normed.append(with_message(normed_ref[i], nmsg_ref, tokens, frame))
        keys.append(with_message(kv_ref[i], kvmsg_ref, tokens, frame))
    queries_t = [nt(wqt[...], n).astype(bf16) * jnp.bfloat16(SCALE) for n in normed]
    values_t = [nt(wvt[...], n).astype(bf16) for n in normed]
    jobs = [(i, h) for i in range(batch) for h in range(HEADS)]
    contexts, stats, scores, expos, totals = {}, {}, {}, {}, {}

    def score(job):
        i, head = job
        scores[job] = nn(pair_lanes(keys[i], head), half_pair(queries_t[i], head))

    def soften(job):
        one = masked_tail(scores.pop(job), tokens)
        top = jnp.max(one, axis=0, keepdims=True)
        expo = jnp.exp(one - top)
        totals[job] = row_sum(expo)
        expos[job] = expo.astype(bf16)
        stats[job] = top + jnp.log(totals[job])

    def mix(job):
        i, head = job
        own = values_t[i][head * HEAD_DIM : (head + 1) * HEAD_DIM]
        contexts[job] = nn(own, expos.pop(job)) * (1.0 / totals[job])

    stagger(jobs, [score, soften, mix], 3)
    for i in range(batch):
        context_t = jnp.concatenate([contexts[i, h] for h in range(HEADS)], axis=0).astype(bf16)
        ctx_ref[i] = context_t
        pad = [jnp.zeros((8 - HEADS, rows), f32)]
        lse_ref[i] = jnp.concatenate([stats[i, h] for h in range(HEADS)] + pad, axis=0)
        row = message_ref[pl.ds(step * batch + i, 1), :]
        base = put_row(pad_rows(video_ref[i].astype(f32), rows), tokens - 1, row)
        resid_ref[i] = base + tn(context_t, wo_ref[...])


def attend(normed, kv, video, message, nmsg, kvmsg, qkv, outw, tokens, after=()):
    count, rows, width = normed.shape
    slots = message.shape[0]
    batch = share_of(count, 2)
    return pl.pallas_call(
        functools.partial(attend_kernel, tokens),
        grid=(count // batch,),
        in_specs=[
            frames_block(batch, (rows, width)),
            frames_block(batch, (rows, 2 * width)),
            frames_block(batch, video.shape[1:]),
            full((slots, width)),
            full((slots, width)),
            full((slots, 2 * width)),
            square(width, 1, 0),
            square(width, 1, 2),
            square(width, 1),
        ]
        + [pl.BlockSpec(memory_space=pl.ANY)] * len(after),
        out_specs=[
            frames_block(batch, (rows, width)),
            frames_block(batch, (width, rows)),
            frames_block(batch, (8, rows)),
        ],
        out_shape=[
            shape_of((count, rows, width), f32),
            shape_of((count, width, rows), bf16),
            shape_of((count, 8, rows), f32),
        ],
        scratch_shapes=[pltpu.VMEM((width, width), bf16)] * 2,
        compiler_params=params(20),
        cost_estimate=cost(14e9, 10e6),
        name="attend",
    )(normed, kv, video, message, nmsg, kvmsg, qkv, qkv, outw, *after)


def caption_kernel(
    pieces, groups, clips, local, where_ref, lengths_ref, *refs
):
    gathered = refs[:pieces]
    caps_ref, cot_ref, qkv_ref, outw_ref, gains_ref = refs[pieces : pieces + 5]
    out_ref, grad_ref, gain_ref = refs[pieces + 5 : pieces + 8]
    part_refs = refs[pieces + 8 : pieces + 8 + pieces]
    keep_ref, send_ref, acc = refs[pieces + 8 + pieces :]
    width = caps_ref.shape[1]
    slots = gathered[0].shape[0]
    count = caps_ref.shape[0]
    keys_n = pieces * slots
    runs = lengths_ref.shape[1]

    token = lax.broadcasted_iota(jnp.int32, (count, keys_n), 0)
    key = lax.broadcasted_iota(jnp.int32, (count, keys_n), 1)
    slot = key % slots
    group = token // local
    position = token - group * local + where_ref[0] * local
    document = jnp.zeros((count, keys_n), jnp.int32)
    for m in range(groups):
        end = jnp.int32(0)
        for j in range(runs):
            end = end + lengths_ref[m, j]
            document = document + jnp.where((group == m) & (position >= end), 1, 0)
    allowed = slot == group * clips + document % clips
    valid = (document[:, 0:1] < runs - 1).astype(f32)

    pack = caps_ref[...].astype(f32)
    unit, inv = unit_norm(pack)
    gain = gains_ref[3:4, :]
    normed = (unit * gain).astype(bf16)
    visual = jnp.concatenate([g[...] for g in gathered], axis=0)
    queries = nn(normed, qkv_ref[0, 0]).astype(bf16)
    keys = nn(visual, qkv_ref[0, 1]).astype(bf16)
    values = nn(visual, qkv_ref[0, 2]).astype(bf16)

    masks = [head_mask((count, width), 1, h) for h in range(HEADS)]
    zero = jnp.zeros((count, width), bf16)

    def by_head(x):
        return jnp.concatenate([jnp.where(m, x, zero) for m in masks], axis=0)

    def merge(x):
        cut = [x[h * count : (h + 1) * count] for h in range(HEADS)]
        return functools.reduce(jnp.add, [jnp.where(m, c, 0.0) for m, c in zip(masks, cut)])

    allowed_all = jnp.concatenate([allowed.astype(jnp.int32)] * HEADS, axis=0) > 0
    split_q = by_head(queries)
    scores = jnp.where(allowed_all, nt(split_q, keys) * SCALE, MASKED)
    expo = jnp.exp(scores - jnp.max(scores, axis=1, keepdims=True))
    probs = expo / jnp.sum(expo, axis=1, keepdims=True)
    low = probs.astype(bf16)
    context = merge(nn(low, values)).astype(bf16)
    out_ref[...] = (pack + valid * nn(context, outw_ref[0])).astype(bf16)

    cot = cot_ref[...].astype(f32)
    branch = (cot * valid).astype(bf16)
    split_d = by_head(nt(branch, outw_ref[0]).astype(bf16))
    dvalues = tn(low, split_d)
    dprobs = nt(split_d, values)
    dscores = probs * (dprobs - jnp.sum(dprobs * probs, axis=1, keepdims=True))
    dscores = jnp.where(allowed_all, dscores, 0.0).astype(bf16)
    dqueries = (merge(nn(dscores, keys)) * SCALE).astype(bf16)
    dkeys = tn(dscores, split_q) * SCALE
    dnormed = nt(dqueries, qkv_ref[0, 0])
    grad_ref[...] = (cot + norm_back(unit, inv, gain, dnormed)).astype(bf16)
    gain_ref[...] = jnp.concatenate([row_sum(dnormed * unit), jnp.zeros((7, width), f32)], axis=0)
    low_k, low_v = dkeys.astype(bf16), dvalues.astype(bf16)
    part = nt(low_k, qkv_ref[0, 1]) + nt(low_v, qkv_ref[0, 2])
    for g in range(pieces):
        part_refs[g][...] = part[g * slots : (g + 1) * slots]
    if acc.shape[0] > 4 * width:
        acc[...] = jnp.zeros(acc.shape, f32)
    acc[0:width, :] = tn(normed, dqueries)
    acc[width : 2 * width, :] = tn(visual, low_k)
    acc[2 * width : 3 * width, :] = tn(visual, low_v)
    acc[3 * width : 4 * width, :] = tn(context, branch)
    emit(where_ref, acc, keep_ref, send_ref, True)


def captions_step(where, lengths, gathered, caps, cot, qkv, outw, gains, plan):
    count, width = caps.shape
    groups = lengths.shape[0]
    pieces = len(gathered)
    slots = gathered[0].shape[0]
    operands = list(gathered) + [caps, cot, qkv, outw, gains]
    acc_rows, packet_specs, packet_shapes = plan.packet(4 * width, width, True)
    return pl.pallas_call(
        functools.partial(caption_kernel, pieces, groups, plan.clips, count // groups),
        grid=(1,),
        in_specs=[scalars(), scalars()]
        + [full(x.shape) for x in operands[:-3]]
        + [
            pl.BlockSpec((1, 3, width, width), lambda i: (2, 0, 0, 0)),
            pl.BlockSpec((1, width, width), lambda i: (2, 0, 0)),
            full(gains.shape),
        ],
        out_specs=[full((count, width))] * 2
        + [full((8, width))]
        + [full((slots, width))] * pieces
        + packet_specs,
        out_shape=[shape_of((count, width), bf16)] * 2
        + [shape_of((8, width), f32)]
        + [shape_of((slots, width), f32)] * pieces
        + packet_shapes,
        scratch_shapes=[pltpu.VMEM((acc_rows, width), f32)],
        compiler_params=params(12),
        cost_estimate=cost(4e9, 8e6),
        name="captions_step",
    )(where, lengths, *operands)


def mlp_kernel(
    pieces, patch, ff, where_ref, resid_ref, cot_ref, final_ref, gains_ref, up_ref, down_ref, *refs
):
    parts = refs[:pieces]
    out_ref, dresid_ref, gain_ref, keep_ref, send_ref, acc, dcls = refs[-7:]
    step = pl.program_id(0)
    batch, rows, width = resid_ref.shape
    wide = acc.shape[1]
    blocks = ff // wide

    @pl.when(step == 0)
    def _():
        acc[...] = jnp.zeros(acc.shape, f32)
        dvisual = functools.reduce(jnp.add, [p[...] for p in parts])
        unit, inv = unit_norm(final_ref[...])
        dcls[...] = norm_back(unit, inv, gains_ref[2:3, :], dvisual)
        gain_ref[...] = jnp.concatenate(
            [jnp.zeros((1, width), f32), row_sum(dvisual * unit), jnp.zeros((6, width), f32)],
            axis=0,
        )

    resid = resid_ref[...].reshape(batch * rows, width)
    gain = gains_ref[1:2, :]
    unit, inv = unit_norm(resid)
    normed32 = unit * gain
    normed = normed32.astype(bf16)
    normed_t = normed32.T.astype(bf16)
    pieces_d = []
    for i in range(batch):
        one = pad_rows(cot_ref[i].astype(f32), rows)
        pieces_d.append(put_row(one, 0, one[0:1] + dcls[pl.ds(step * batch + i, 1), :]))
    dfinal = jnp.concatenate(pieces_d, axis=0)
    branch = dfinal.astype(bf16)
    branch_t = dfinal.T.astype(bf16)
    final = resid
    dnormed = jnp.zeros((batch * rows, width), f32)
    for c in range(blocks):
        span = slice(c * wide, (c + 1) * wide)
        hidden = nn(normed, up_ref[:, span])
        gate = sigmoid(1.702 * hidden)
        active = (hidden * gate).astype(bf16)
        final = final + nn(active, down_ref[span, :])
        dactive = nt(branch, down_ref[span, :])
        dhidden = (dactive * gate * (1.0 + 1.702 * hidden * (1.0 - gate))).astype(bf16)
        dnormed = dnormed + nt(dhidden, up_ref[:, span])
        acc[c * width : (c + 1) * width, :] += nn(normed_t, dhidden)
        acc[(blocks + c) * width : (blocks + c + 1) * width, :] += nn(branch_t, active)
    for i in range(batch):
        out_ref[i] = final[i * rows : i * rows + patch].astype(bf16)
    dresid = dfinal + norm_back(unit, inv, gain, dnormed)
    dresid_ref[...] = dresid.reshape(batch, rows, width)
    gain_ref[0:1, :] += row_sum(dnormed * unit)

    @pl.when(step == pl.num_programs(0) - 1)
    def _():
        emit(where_ref, acc, keep_ref, send_ref)


def mlp_step(where, resid, cot, final, gains, up, down, parts, plan, after=()):
    count, rows, width = resid.shape
    patch = cot.shape[1]
    ff = up.shape[1]
    slots = final.shape[0]
    batch = share_of(count, 2)
    wide = 2 * width
    acc_rows, packet_specs, packet_shapes = plan.packet(2 * ff * width // wide, wide)
    return pl.pallas_call(
        functools.partial(mlp_kernel, len(parts), patch, ff),
        grid=(count // batch,),
        in_specs=[
            scalars(),
            frames_block(batch, (rows, width)),
            frames_block(batch, (patch, width)),
            full((slots, width)),
            full(gains.shape),
            full(up.shape),
            full(down.shape),
        ]
        + [full((slots, width))] * len(parts)
        + [pl.BlockSpec(memory_space=pl.ANY)] * len(after),
        out_specs=[
            frames_block(batch, (patch, width)),
            frames_block(batch, (rows, width)),
            full((8, width)),
        ]
        + packet_specs,
        out_shape=[
            shape_of((count, patch, width), bf16),
            shape_of((count, rows, width), f32),
            shape_of((8, width), f32),
        ]
        + packet_shapes,
        scratch_shapes=[pltpu.VMEM((acc_rows, wide), f32), pltpu.VMEM((slots, width), f32)],
        compiler_params=params(36),
        cost_estimate=cost(20e9, 20e6),
        name="mlp_step",
    )(where, resid, cot, final, gains, up, down, *parts, *after)


def attend_back_kernel(tokens, first, last, waits, where_ref, normed_ref, kv_ref, *refs):
    (
        video_ref, message_ref, nmsg_ref, kvmsg_ref, ctx_ref, lse_ref, dresid_ref, gains_ref,
        wq_ref, wk_ref, wv_ref, wo_ref,
    ) = refs[:12]
    refs = refs[12:]
    if first:
        carried, refs = refs[1:5], refs[5:]
    refs = refs[waits:]
    outs = refs[: 6 if last else 5]
    grad_ref, dmsg_ref, dcls_ref, gain_ref = outs[:4]
    acc, wqt, wkt, wall = refs[len(outs) :]
    here = pl.program_id(0)
    step = here + first
    batch, rows, width = dresid_ref.shape
    patch = tokens - 1

    @pl.when(here == 0)
    def _():
        wqt[...] = wq_ref[...].T
        wkt[...] = wk_ref[...].T
        wall[:, 0:width] = wq_ref[...]
        wall[:, width : 2 * width] = wk_ref[...]
        wall[:, 2 * width : 3 * width] = wv_ref[...]
        for k, ref in enumerate((dmsg_ref, dcls_ref, gain_ref, acc)):
            ref[...] = carried[k][...] if first else jnp.zeros(ref.shape, f32)

    frames = range(batch)
    normed, kv = [], []
    for i in frames:
        normed.append(with_message(normed_ref[i], nmsg_ref, tokens, step * batch + i))
        kv.append(with_message(kv_ref[i], kvmsg_ref, tokens, step * batch + i))
    branch = [dresid_ref[i].astype(bf16) for i in frames]
    queries_t = [nt(wqt[...], n).astype(bf16) * jnp.bfloat16(SCALE) for n in normed]
    dcontext_t = [nt(wo_ref[...], b).astype(bf16) for b in branch]
    keys_t = [nt(wkt[...], n).astype(bf16) for n in normed]
    acc[3 * width : 4 * width, :] += functools.reduce(
        jnp.add, [nn(ctx_ref[i], branch[i]) for i in frames]
    )
    jobs = [(i, h) for i in frames for h in range(HEADS)]
    own = [slice(h * HEAD_DIM, (h + 1) * HEAD_DIM) for h in range(HEADS)]
    scores, dprobs, low, dscores, dq, dk, dv = {}, {}, {}, {}, {}, {}, {}

    def score(job):
        i, h = job
        scores[job] = nn(pair_lanes(kv[i], h), half_pair(queries_t[i], h))
        dprobs[job] = nn(pair_lanes(kv[i], HEADS + h), half_pair(dcontext_t[i], h))

    def soften(job):
        i, h = job
        probs = jnp.exp(masked_tail(scores.pop(job), tokens) - lse_ref[i, h : h + 1, :])
        low[job] = probs.astype(bf16)
        weighted = dprobs.pop(job) * probs
        dscores[job] = (weighted - probs * row_sum(weighted)).astype(bf16)

    def mix(job):
        i, h = job
        dq[job] = nn(keys_t[i][own[h]], dscores[job]) * SCALE
        dk[job] = nt(queries_t[i][own[h]], dscores.pop(job))
        dv[job] = nt(dcontext_t[i][own[h]], low.pop(job))

    stagger(jobs, [score, soften, mix], 2)
    dall = []
    for i in frames:
        parts = [d[i, h] for d in (dq, dk, dv) for h in range(HEADS)]
        dall.append(jnp.concatenate(parts, axis=0).astype(bf16))
    acc[0 : 3 * width, :] += functools.reduce(
        jnp.add, [nn(dall[i], normed[i]) for i in frames]
    )
    gain_sum = jnp.zeros((1, width), f32)
    for i in frames:
        dnormed = nn(wall[...], dall[i]).T
        at = pl.ds(step * batch + i, 1)
        base = put_row(pad_rows(video_ref[i].astype(f32), rows), tokens - 1, message_ref[at, :])
        unit, inv = unit_norm(base)
        dtokens = dresid_ref[i] + norm_back(unit, inv, gains_ref[0:1, :], dnormed)
        gain_sum = gain_sum + row_sum(dnormed * unit)
        grad_ref[i] = dtokens[:patch].astype(bf16)
        dcls_ref[at, :] = dtokens[0:1]
        dmsg_ref[at, :] = dtokens[patch : patch + 1]
    gain_ref[0:1, :] += gain_sum

    @pl.when(here == pl.num_programs(0) - 1)
    def _():
        if last:
            emit(where_ref, acc, *outs[4:])
        else:
            outs[4][...] = acc[...]


def attend_back(
    where, normed, kv, video, message, nmsg, kvmsg, ctx, lse, dresid, gains, qkv, outw, plan,
    batch, first, steps, carried=(), after=(),
):
    count, rows, width = normed.shape
    patch = video.shape[1]
    slots = message.shape[0]
    last = (first + steps) * batch == count
    acc_rows, packet_specs, packet_shapes = plan.packet(4 * width, width)
    if not last:
        packet_specs, packet_shapes = [full((acc_rows, width))], [shape_of((acc_rows, width), f32)]

    def block(shape):
        return pl.BlockSpec((batch,) + shape, lambda i, *_: (i + first, 0, 0))

    anywhere = pl.BlockSpec(memory_space=pl.ANY)
    carry_specs = [anywhere] + [full(x.shape) for x in carried[1:]] if carried else []
    return pl.pallas_call(
        functools.partial(attend_back_kernel, patch + 1, first, last, len(after)),
        grid=(steps,),
        in_specs=[
            scalars(),
            block((rows, width)),
            block((rows, 2 * width)),
            block((patch, width)),
            full((slots, width)),
            full((slots, width)),
            full((slots, 2 * width)),
            block((width, rows)),
            block((8, rows)),
            block((rows, width)),
            full(gains.shape),
            square(width, 1, 0),
            square(width, 1, 1),
            square(width, 1, 2),
            square(width, 1),
        ]
        + carry_specs
        + [anywhere] * len(after),
        out_specs=[block((patch, width))]
        + [full((slots, width))] * 2
        + [full((8, width))]
        + packet_specs,
        out_shape=[shape_of((count, patch, width), bf16)]
        + [shape_of((slots, width), f32)] * 2
        + [shape_of((8, width), f32)]
        + packet_shapes,
        input_output_aliases={15: 0} if carried else {},
        scratch_shapes=[
            pltpu.VMEM((acc_rows, width), f32),
            pltpu.VMEM((width, width), bf16),
            pltpu.VMEM((width, width), bf16),
            pltpu.VMEM((width, 3 * width), bf16),
        ],
        compiler_params=params(26),
        cost_estimate=cost(4.5e9 * steps, 4e6 * steps),
        name="attend_back",
    )(
        where, normed, kv, video, message, nmsg, kvmsg, ctx, lse, dresid, gains, qkv, qkv, qkv,
        outw, *carried, *after,
    )


def message_back_kernel(layout, together, where_ref, *refs):
    segs, frames, clips = layout
    pieces, more = refs[: segs * frames], refs[segs * frames : segs * frames + segs]
    refs = refs[segs * frames + segs :]
    mw_ref, mg_ref, qkv_ref, outw_ref = refs[:4]
    (
        big_ref, out_ref, mwg_ref, gain_ref, gains_ref, dclass_ref,
        whole, classes, dmsgs, dstart, wqt, wkt, wvt, wall,
    ) = refs[6:]
    width = mw_ref.shape[0]
    slots = dclass_ref.shape[0]
    chunk = pieces[0].shape[1] - slots
    place(
        layout, where_ref, lambda a, b, d: pieces[a * frames + b][d, :chunk, :], whole, chunk
    )
    for j in range(3):
        big_ref[1, j] = whole[j * width : (j + 1) * width, :].astype(f32).T
    out_ref[1] = whole[3 * width : 4 * width, :].astype(f32)
    me_f, me_s, me_c = where_ref[0], where_ref[1], where_ref[2]
    rows = frames * together * slots
    steps = segs * clips // together
    side = frames * slots * max(1, min(together, 128 // (frames * slots)))
    blocks = [slice(at, at + side) for at in range(0, rows, side)]

    def row_of(s, f, c):
        group = s * clips + c
        step, inside = group // together, group % together
        return step, pl.multiple_of((inside * frames + f) * slots, 16)

    for a in range(segs):
        for b in range(frames):
            for d in range(clips):
                step, at = row_of(me_s ^ a, me_f ^ b, me_c ^ d)
                classes[step, pl.ds(at, slots), :] = more[a][d, b, more[a].shape[2] - slots :, :]
                dmsgs[step, pl.ds(at, slots), :] = pieces[a * frames + b][d, chunk:, :]
    gain_total = jnp.zeros((slots, width), f32)
    for i in range(frames * together):
        for step in range(steps):
            gain_total += dmsgs[step, i * slots : (i + 1) * slots, :].astype(f32)
    gains_ref[...] = gain_total[slots - 4 : slots]

    wqt[...] = qkv_ref[0, 0].T
    wkt[...] = qkv_ref[0, 1].T
    wvt[...] = qkv_ref[0, 2].T
    for j in range(3):
        wall[:, j * width : (j + 1) * width] = qkv_ref[0, j]
    index = lax.broadcasted_iota(jnp.int32, (rows, 1), 0) % slots
    key = lax.broadcasted_iota(jnp.int32, (side, side), 0)
    query = lax.broadcasted_iota(jnp.int32, (side, side), 1)
    same = (key % slots == query % slots) & (key // (frames * slots) == query // (frames * slots))
    my_step, my_at = row_of(me_s, me_f, me_c)
    own = [slice(h * HEAD_DIM, (h + 1) * HEAD_DIM) for h in range(HEADS)]

    def batch(step, put):
        dm = jnp.where(index < slots - 6, dmsgs[step].astype(f32), 0.0).astype(bf16)
        cls = classes[step]
        start = nn(cls, mw_ref[...]).astype(bf16)
        unit, inv = unit_norm(start.astype(f32))
        normed = (unit * mg_ref[...]).astype(bf16)
        keys = nn(normed, qkv_ref[0, 1]).astype(bf16)
        values = nn(normed, qkv_ref[0, 2]).astype(bf16)
        queries_t = nt(wqt[...], normed).astype(bf16) * jnp.bfloat16(SCALE)
        keys_t = nt(wkt[...], normed).astype(bf16)
        values_t = nt(wvt[...], normed).astype(bf16)
        dcontext_t = nt(outw_ref[0], dm).astype(bf16)
        scores, dprobs, low, dscores, ctx, dq, dk, dv = {}, {}, {}, {}, {}, {}, {}, {}

        def score(job):
            i, h = job
            at = blocks[i]
            scores[job] = nn(pair_lanes(keys[at], h), half_pair(queries_t[:, at], h))
            dprobs[job] = nn(pair_lanes(values[at], h), half_pair(dcontext_t[:, at], h))

        def soften(job):
            one = jnp.where(same, scores.pop(job), MASKED)
            expo = jnp.exp(one - jnp.max(one, axis=0, keepdims=True))
            probs = expo * (1.0 / row_sum(expo))
            low[job] = probs.astype(bf16)
            weighted = dprobs.pop(job) * probs
            dscores[job] = (weighted - probs * row_sum(weighted)).astype(bf16)

        def mix(job):
            i, h = job
            at = blocks[i]
            ctx[job] = nn(values_t[own[h], at], low[job])
            dq[job] = nn(keys_t[own[h], at], dscores[job]) * SCALE
            dk[job] = nt(queries_t[own[h], at], dscores.pop(job))
            dv[job] = nt(dcontext_t[own[h], at], low.pop(job))

        jobs = [(i, h) for i in range(len(blocks)) for h in range(HEADS)]
        stagger(jobs, [score, soften, mix], 2)

        def gather(parts):
            lanes = [
                jnp.concatenate([p[i, h] for p in parts for h in range(HEADS)], axis=0)
                for i in range(len(blocks))
            ]
            return (jnp.concatenate(lanes, axis=1) if len(lanes) > 1 else lanes[0]).astype(bf16)

        put(out_ref, 0, nn(gather([ctx]), dm))
        dall = gather([dq, dk, dv])
        grads = nn(dall, normed)
        for j in range(3):
            put(big_ref, (0, j), grads[j * width : (j + 1) * width].T)
        dnormed = nn(wall[...], dall).T
        put(gain_ref, ..., jnp.sum(dnormed * unit, axis=0))
        ds = norm_back(unit, inv, mg_ref[...], dnormed) + dm.astype(f32)
        dstart[...] = ds
        put(mwg_ref, ..., tn(cls, ds.astype(bf16)))

        @pl.when(my_step == step)
        def _():
            dclass_ref[...] = nt(dstart[pl.ds(my_at, slots), :].astype(bf16), mw_ref[...])

    def first(ref, at, value):
        ref[at] = value

    def again(ref, at, value):
        ref[at] += value

    batch(0, first)
    if steps > 1:
        pl.loop(1, steps)(lambda step: batch(step, again))


def message_back(where, pieces, side, mw, mg, qkv, outw, big, out, layout, slots):
    segs, frames, clips = layout
    width = mw.shape[0]
    groups = segs * clips
    together = max(1, min(groups, 512 // (frames * slots)))
    rows = frames * together * slots
    everyone = (groups // together, rows, width)
    operands = list(pieces) + list(side) + [mw, mg]
    chunk = pieces[0].shape[1] - slots
    return pl.pallas_call(
        functools.partial(message_back_kernel, layout, together),
        grid=(1,),
        in_specs=[scalars()]
        + [full(x.shape) for x in operands]
        + [
            pl.BlockSpec((1, 3, width, width), lambda i: (0, 0, 0, 0)),
            pl.BlockSpec((1, width, width), lambda i: (0, 0, 0)),
            pl.BlockSpec(memory_space=pl.ANY),
            pl.BlockSpec(memory_space=pl.ANY),
        ],
        out_specs=[
            pl.BlockSpec((2, 3, width, width), lambda i: (0, 0, 0, 0)),
            pl.BlockSpec((2, width, width), lambda i: (0, 0, 0)),
            full((width, width)),
            full((width,)),
            full((4, width)),
            full((slots, width)),
        ],
        out_shape=[
            shape_of((3, 3, width, width), f32),
            shape_of((3, width, width), f32),
            shape_of((width, width), f32),
            shape_of((width,), f32),
            shape_of((4, width), f32),
            shape_of((slots, width), f32),
        ],
        input_output_aliases={len(operands) + 3: 0, len(operands) + 4: 1},
        scratch_shapes=[pltpu.VMEM((groups * frames * chunk, width), bf16)]
        + [pltpu.VMEM(everyone, bf16)] * 2
        + [pltpu.VMEM((rows, width), f32)]
        + [pltpu.VMEM((width, width), bf16)] * 3
        + [pltpu.VMEM((width, 3 * width), bf16)],
        compiler_params=params(56),
        cost_estimate=cost(6e9, 12e6),
        name="message_back",
    )(where, *operands, qkv, outw, big, out)


def emit(where_ref, acc, keep_ref, send_ref, clip_first=False):
    frames, clips, chunk = keep_ref.shape[:3]
    if clip_first:
        frames, clips = clips, frames
    me_f, me_s, me_c = where_ref[0], where_ref[1], where_ref[2]
    for a, out in enumerate((keep_ref, send_ref)):
        for b in range(frames):
            for d in range(clips):
                f = b if clip_first else me_f ^ b
                to = ((me_s ^ a) * frames + f) * clips + (me_c ^ d)
                at = pl.multiple_of(to * chunk, 16)
                out[(d, b) if clip_first else (b, d)] = acc[pl.ds(at, chunk), :].astype(bf16)


class Plan:
    def __init__(self, clips):
        self.clips = clips
        self.segs = lax.axis_size("seg")
        self.frames = lax.axis_size("frame")
        self.rings = lax.axis_size("clip")
        self.layout = (self.segs, self.frames, self.rings)
        self.devices = self.segs * self.frames * self.rings

    def chunk(self, rows):
        share = -(-rows // self.devices)
        return -(-share // 16) * 16

    def packet(self, rows, width, clip_first=False):
        chunk = self.chunk(rows)
        shape = (self.frames, self.rings, chunk, width)
        if clip_first:
            shape = (self.rings, self.frames, chunk, width)
        return chunk * self.devices, [full(shape)] * 2, [shape_of(shape, bf16)] * 2


def swap(x, axis, k):
    count = lax.axis_size(axis)
    return lax.ppermute(x, axis, [(i, i ^ k) for i in range(count)])


def total(terms):
    return functools.reduce(jnp.add, [t.astype(f32) for t in terms]).astype(bf16)


def behind(x, *others):
    return lax.optimization_barrier((x, others))[0]


def reduce_seg(keep, send):
    return [keep, swap(send, "seg", 1)]


def frame_sends(terms):
    return [total([t[b] for t in terms]) for b in range(1, terms[0].shape[0])]


def reduce_frame(terms, sends):
    return [t[0] for t in terms] + [swap(x, "frame", b + 1) for b, x in enumerate(sends)]


def clip_bits():
    count = lax.axis_size("clip")
    return [1 << j for j in range(count.bit_length() - 1)]


def clip_send(terms):
    paired = [t.reshape((-1, 2) + t.shape[1:]) for t in terms]
    return [p[:, 0] for p in paired], total([p[:, 1] for p in paired])


def clip_reduce(terms, bits):
    for bit in bits:
        terms, send = clip_send(terms)
        terms = terms + [swap(send, "clip", bit)]
    return terms


def clip_gather(held, bits):
    for bit in reversed(bits):
        both = jnp.stack([held, swap(held, "clip", bit)], axis=1)
        held = both.reshape((-1,) + held.shape[1:])
    return held


def gather_frame(held):
    return [held] + [swap(held, "frame", b) for b in range(1, lax.axis_size("frame"))]


def clip_all(own):
    return jnp.stack([own] + [swap(own, "clip", d) for d in range(1, lax.axis_size("clip"))])


def tree(terms):
    terms = [t.astype(f32) for t in terms]
    while len(terms) > 1:
        terms = [a + b for a, b in zip(terms[::2], terms[1::2])]
    return terms[0].astype(bf16)


def gather_seg(held):
    return held + [swap(h, "seg", 1) for h in held]


def place(layout, where_ref, piece, whole, chunk, absolute=False):
    segs, frames, clips = layout
    me_f, me_s, me_c = where_ref[0], where_ref[1], where_ref[2]
    for a in range(segs):
        for b in range(frames):
            for d in range(clips):
                f = b if absolute else me_f ^ b
                of = ((me_s ^ a) * frames + f) * clips + (me_c ^ d)
                whole[pl.ds(pl.multiple_of(of * chunk, 16), chunk), :] = piece(a, b, d)


def unpack_kernel(layout, where_ref, *refs):
    segs, frames, clips = layout
    main, side = refs[:segs], refs[segs : 2 * segs]
    up_ref, down_ref, big_ref, out_ref, whole, more = refs[2 * segs :]
    width, ff = up_ref.shape
    wide = whole.shape[1]
    place(layout, where_ref, lambda a, b, d: main[a][b * clips + d], whole, main[0].shape[1])
    chunk = more.shape[0] // (segs * frames * clips)
    place(layout, where_ref, lambda a, b, d: side[a][d, b, :chunk, :], more, chunk, True)
    blocks = ff // wide
    for c in range(blocks):
        span = slice(c * wide, (c + 1) * wide)
        up_ref[:, span] = whole[c * width : (c + 1) * width, :].astype(f32)
        other = whole[(blocks + c) * width : (blocks + c + 1) * width, :]
        down_ref[span, :] = other.astype(f32).T
    for j in range(3):
        big_ref[0, j] = more[j * width : (j + 1) * width, :].astype(f32)
    out_ref[0] = more[3 * width : 4 * width, :].astype(f32)


def unpack(where, main, side, width, ff, plan, slots):
    chunk, wide = main[0].shape[1:]
    return pl.pallas_call(
        functools.partial(unpack_kernel, plan.layout),
        grid=(1,),
        in_specs=[scalars()] + [full(x.shape) for x in main + side],
        out_specs=[
            full((width, ff)),
            full((ff, width)),
            pl.BlockSpec((1, 3, width, width), lambda i: (2, 0, 0, 0)),
            pl.BlockSpec((1, width, width), lambda i: (2, 0, 0)),
        ],
        out_shape=[
            shape_of((width, ff), f32),
            shape_of((ff, width), f32),
            shape_of((3, 3, width, width), f32),
            shape_of((3, width, width), f32),
        ],
        scratch_shapes=[
            pltpu.VMEM((plan.devices * chunk, wide), bf16),
            pltpu.VMEM((plan.devices * (side[0].shape[2] - slots), width), bf16),
        ],
        compiler_params=params(56),
        cost_estimate=cost(2e9, 12e6),
        name="unpack",
    )(where, *main, *side)


def last_rows_kernel(gain_a, gain_b, gain_c, dmsg_ref, out_ref):
    slots, width = dmsg_ref.shape
    rows = [
        dmsg_ref[0 : slots - 6, :],
        jnp.zeros((2, width), f32),
        gain_a[0:1, :],
        gain_b[0:1, :],
        gain_b[1:2, :],
        gain_c[0:1, :],
    ]
    out_ref[...] = jnp.concatenate(rows, axis=0).astype(bf16)


def last_rows(gain_a, gain_b, gain_c, dmsg):
    return pl.pallas_call(
        last_rows_kernel,
        out_shape=shape_of(dmsg.shape, bf16),
        name="last_rows",
    )(gain_a, gain_b, gain_c, dmsg)


def local(
    video, captions, caption_lengths, message_weight, message_gain, qkv_weights, out_weights,
    mlp_up, mlp_down, gains, video_cot, caption_cot,
):
    micro, clips, per_frame, patch, width = video.shape
    count = micro * clips * per_frame
    ff = mlp_up.shape[1]
    plan = Plan(clips)
    tokens = patch + 1
    rows = -(-tokens // 16) * 16
    slots = -(-(count + 6) // 16) * 16
    where = jnp.stack(
        [lax.axis_index("frame"), lax.axis_index("seg"), lax.axis_index("clip")]
    ).astype(jnp.int32)
    frames = video.reshape(count, patch, width)
    cots = video_cot.reshape(count, patch, width)
    caps = captions.reshape(-1, width)
    cap_cots = caption_cot.reshape(-1, width)
    lengths = caption_lengths.reshape(micro, -1)
    gain = message_gain.reshape(1, width)

    classes = class_rows(video, slots)
    gathered = gather_frame(classes)
    normed, kv = norm_tokens(frames, gains, qkv_weights, rows)
    message, nmsg, kvmsg, visual, final = first_rows(
        gathered, message_weight, gain, qkv_weights, out_weights, mlp_up, mlp_down, gains,
        kv, tokens,
    )
    visuals = gather_frame(visual)
    results = captions_step(
        where, lengths, visuals, caps, cap_cots, qkv_weights, out_weights, gains, plan
    )
    caption_out, caption_grad, gain_c = results[:3]
    parts = list(results[3:-2])
    parts = [parts[0]] + [swap(parts[b], "frame", b) for b in range(1, plan.frames)]
    bits = clip_bits()
    side = reduce_seg(*results[-2:])
    side, side_send = clip_send(side)
    resid, ctx, lse = attend(
        normed, kv, frames, message, nmsg, kvmsg, qkv_weights, out_weights, tokens, [side_send]
    )
    side = side + [swap(side_send, "clip", bits[0])]
    side, parts, resid = behind((side, parts, resid))
    side, side_send = clip_send(side)
    video_out, dresid, gain_b, keep, send = mlp_step(
        where, resid, cots, final, gains, mlp_up, mlp_down, parts, plan, [side_send]
    )
    side = side + [swap(side_send, "clip", bits[1])]
    side, video_out, dresid, keep, send = behind((side, video_out, dresid, keep, send))
    side = total([t[0] for t in clip_reduce(side, bits[2:])])
    main = reduce_seg(keep, send)
    side = gather_frame(side)
    turned = video_out.reshape(video.shape).transpose(1, 2, 3, 0, 4)
    main, dresid, turned, side = behind((main, dresid, turned, side))
    video_out = turned.transpose(3, 0, 1, 2, 4)
    sends = frame_sends(main)
    side = jnp.concatenate([tree(side), jnp.stack(gathered)], axis=1)[None]
    sends, dresid, side = behind((sends, dresid, side))
    batch = share_of(count, 2)
    steps = count // batch
    late_steps = 2
    back = functools.partial(
        attend_back, where, normed, kv, frames, message, nmsg, kvmsg, ctx, lse, dresid, gains,
        qkv_weights, out_weights, plan, batch,
    )
    carried = back(0, steps - late_steps)
    main = reduce_frame(main, sends)
    side = clip_gather(side, bits[1:])
    carried, main, side = behind((carried, main, side))
    main, send = clip_send(main)
    send, carried, side = behind((send, carried, side))
    got = swap(send, "clip", bits[0])
    side = clip_gather(side, bits[:1])
    grad, dmsg, dcls, gain_a, keep, send = back(steps - late_steps, late_steps, carried)
    main, side, keep, send, gain_a = behind((main + [got], side, keep, send, gain_a))

    late = reduce_seg(keep, send)
    main = clip_reduce(main, bits[1:])
    side = gather_seg([side])
    rest = last_rows(gain_a, gain_b, gain_c, dmsg)
    late, main, rest, side = behind((late, main, rest, side))
    late = reduce_frame(late, frame_sends(late))
    held = clip_gather(total(main), bits)
    held, late, side = behind((held, late, side))
    frames_n, half = plan.frames, max(1, plan.frames // 2)
    first = [swap(held, "frame", b) for b in range(frames_n - 1, frames_n - 1 - half // 2, -1)]
    late_sum = total(late)
    late = [late_sum[0]] + [swap(late_sum[d], "clip", d) for d in range(1, plan.rings)]
    held, late, first = behind((held, late, first))
    rest_b = range(frames_n - 1 - half // 2, 0, -1)
    second = [swap(held, "frame", b) for b in rest_b]
    late = clip_all(jnp.concatenate([total(late), rest], axis=0))
    held, late, first, second = behind((held, late, first, second))
    held = [held] + (first + second)[::-1]
    held = gather_seg([jnp.concatenate(held, axis=0)])
    late = gather_frame(late)
    up_grad, down_grad, big, out = unpack(where, held, side, width, ff, plan, slots)
    late, up_grad = behind((late, up_grad))
    late = gather_seg(late)
    big, out, mw_grad, mg_grad, gains_grad, dclass = message_back(
        where, late, side, message_weight, gain, qkv_weights, out_weights, big, out, plan.layout,
        slots,
    )
    fixed = (dclass + dcls)[:count].astype(bf16).reshape(micro, clips, per_frame, 1, width)
    grad = lax.dynamic_update_slice(grad.reshape(video.shape), fixed, (0, 0, 0, 0, 0))
    return (
        video_out.reshape(video.shape),
        caption_out.reshape(captions.shape),
        grad,
        caption_grad.reshape(captions.shape),
        mw_grad,
        mg_grad,
        big,
        out,
        up_grad,
        down_grad,
        gains_grad,
    )


def solution(mesh):
    rows = P(None, ("clip", "seg"), "frame", None, None)
    caps = P(None, ("clip", "seg"), "frame", None)
    return jax.shard_map(
        local,
        mesh=mesh,
        in_specs=(rows, caps, P(None, ("clip", "seg"), None)) + (P(),) * 7 + (rows, caps),
        out_specs=(rows, caps, rows, caps) + (P(),) * 7,
        check_vma=False,
    )
```

```python
import functools

import jax
import jax.numpy as jnp
from jax import lax
from jax.experimental import pallas as pl
from jax.experimental.pallas import tpu as pltpu
from jax.sharding import PartitionSpec as P

HEADS = 6
HEAD_DIM = 64
EPS = 1e-05
SCALE = 0.125
MASKED = -1e30

f32 = jnp.float32
bf16 = jnp.bfloat16


def nn(a, b):
    return lax.dot_general(a, b, (((1,), (0,)), ((), ())), preferred_element_type=f32)


def nt(a, b):
    return lax.dot_general(a, b, (((1,), (1,)), ((), ())), preferred_element_type=f32)


def tn(a, b):
    return lax.dot_general(a, b, (((0,), (0,)), ((), ())), preferred_element_type=f32)


def exact(a, b):
    return lax.dot_general(
        a, b, (((1,), (0,)), ((), ())), precision=lax.Precision.HIGHEST, preferred_element_type=f32
    )


def unit_norm(x):
    center = x - jnp.mean(x, axis=-1, keepdims=True)
    inv = lax.rsqrt(jnp.mean(center * center, axis=-1, keepdims=True) + EPS)
    return center * inv, inv


def norm_back(unit, inv, gain, dy):
    du = dy * gain
    mean_du = jnp.mean(du, axis=-1, keepdims=True)
    mean_dot = jnp.mean(du * unit, axis=-1, keepdims=True)
    return inv * (du - mean_du - unit * mean_dot)


def row_sum(x):
    return jnp.sum(x, axis=0, keepdims=True)


def sigmoid(x):
    return 0.5 + 0.5 * jnp.tanh(0.5 * x)


def head_mask(shape, lane_dim, head):
    lane = lax.broadcasted_iota(jnp.int32, shape, lane_dim)
    return (lane >= head * HEAD_DIM) & (lane < (head + 1) * HEAD_DIM)


def head_columns(width):
    lane = lax.broadcasted_iota(jnp.int32, (width, 128), 0)
    col = lax.broadcasted_iota(jnp.int32, (width, 128), 1)
    return ((lane >= col * HEAD_DIM) & (lane < (col + 1) * HEAD_DIM)).astype(f32)


def head_rows(width):
    col = lax.broadcasted_iota(jnp.int32, (128, width), 0)
    lane = lax.broadcasted_iota(jnp.int32, (128, width), 1)
    return ((lane >= col * HEAD_DIM) & (lane < (col + 1) * HEAD_DIM)).astype(f32)


def pad_rows(x, rows):
    if x.shape[0] == rows:
        return x
    return jnp.concatenate([x, jnp.zeros((rows - x.shape[0], x.shape[1]), x.dtype)], axis=0)


def put_row(block, at, row):
    top = at // 16 * 16
    tail = block[top : top + 16]
    index = lax.broadcasted_iota(jnp.int32, tail.shape, 0)
    tail = jnp.where(index == at - top, row, tail)
    pieces = [tail]
    if top:
        pieces.insert(0, block[:top])
    if top + 16 < block.shape[0]:
        pieces.append(block[top + 16 :])
    return jnp.concatenate(pieces, axis=0) if len(pieces) > 1 else tail


def full(shape):
    return pl.BlockSpec(shape, lambda *_: (0,) * len(shape))


def frame_block(shape):
    return pl.BlockSpec((1,) + shape, lambda i, *_: (i, 0, 0))


def frames_block(batch, shape):
    return pl.BlockSpec((batch,) + shape, lambda i, *_: (i, 0, 0))


def stagger(jobs, stages, gap):
    for at in range(len(jobs) + (len(stages) - 1) * gap):
        for k, stage in enumerate(stages):
            j = at - k * gap
            if 0 <= j < len(jobs):
                stage(jobs[j])


def share_of(count, most):
    return max(b for b in range(1, most + 1) if count % b == 0)


def square(width, *at):
    return pl.BlockSpec((None,) * len(at) + (width, width), lambda *_: at + (0, 0))


def scalars():
    return pl.BlockSpec(memory_space=pltpu.SMEM)


def shape_of(shape, dtype):
    return jax.ShapeDtypeStruct(shape, dtype)


def params(mib):
    return pltpu.CompilerParams(vmem_limit_bytes=mib * 1024 * 1024)


def cost(flops, nbytes):
    return pl.CostEstimate(flops=int(flops), bytes_accessed=int(nbytes), transcendentals=0)


def class_kernel(video_ref, out_ref):
    clips, _, micro, width = video_ref.shape
    rows = [video_ref[c, 0, m : m + 1, :].astype(f32) for m in range(micro) for c in range(clips)]
    out_ref[...] = pad_rows(jnp.concatenate(rows, axis=0), out_ref.shape[0]).astype(bf16)


def class_rows(video, slots):
    micro, clips, per_frame, patch, width = video.shape
    turned = video.transpose(1, 2, 3, 0, 4).reshape(clips * per_frame, patch, micro, width)
    return pl.pallas_call(
        class_kernel,
        grid=(1,),
        in_specs=[pl.BlockSpec((clips * per_frame, 1, micro, width), lambda i: (0, 0, 0, 0))],
        out_specs=full((slots, width)),
        out_shape=shape_of((slots, width), bf16),
        name="class_rows",
    )(turned)


def norm_kernel(video_ref, gains_ref, wk_ref, wv_ref, normed_ref, kv_ref, wkv):
    batch, rows, width = normed_ref.shape

    @pl.when(pl.program_id(0) == 0)
    def _():
        wkv[:, :width] = wk_ref[...]
        wkv[:, width:] = wv_ref[...]

    parts = []
    for i in range(batch):
        unit, _ = unit_norm(video_ref[i].astype(f32))
        parts.append(pad_rows(unit * gains_ref[0:1, :], rows).astype(bf16))
        normed_ref[i] = parts[i]
    normed = jnp.concatenate(parts, axis=0)
    kv_ref[...] = nn(normed, wkv[...]).astype(bf16).reshape(batch, rows, 2 * width)


def norm_tokens(video, gains, qkv, rows):
    count, patch, width = video.shape
    batch = share_of(count, 5)
    return pl.pallas_call(
        norm_kernel,
        grid=(count // batch,),
        in_specs=[
            frames_block(batch, (patch, width)),
            full(gains.shape),
            square(width, 1, 1),
            square(width, 1, 2),
        ],
        out_specs=[
            frames_block(batch, (rows, width)),
            frames_block(batch, (rows, 2 * width)),
        ],
        out_shape=[
            shape_of((count, rows, width), bf16),
            shape_of((count, rows, 2 * width), bf16),
        ],
        scratch_shapes=[pltpu.VMEM((width, 2 * width), bf16)],
        compiler_params=params(20),
        cost_estimate=cost(4 * count * rows * width * width, 8 * count * rows * width),
        name="norm_tokens",
    )(video, gains, qkv, qkv)


def message_scores(query, keys, columns):
    return [exact(query.astype(f32) * key.astype(f32), columns) * SCALE for key in keys]


def message_probs(scores):
    top = functools.reduce(jnp.maximum, scores)
    expo = [jnp.exp(score - top) for score in scores]
    total = functools.reduce(jnp.add, expo)
    return [e / total for e in expo]


def first_kernel(
    pieces, count, tokens, *refs
):
    gathered = refs[:pieces]
    (
        mw_ref, mg_ref, qkv_ref, outw_ref, up_ref, down_ref, gains_ref, kv_ref,
        message_ref, nmsg_ref, kvmsg_ref, visual_ref, final_ref, ctx,
    ) = refs[pieces:]
    width = mw_ref.shape[0]
    slots = gathered[0].shape[0]
    rows = kv_ref.shape[1]
    classes = jnp.concatenate([g[...] for g in gathered], axis=0)
    start = nn(classes, mw_ref[...]).astype(bf16)
    unit, _ = unit_norm(start.astype(f32))
    normed = (unit * mg_ref[...]).astype(bf16)
    keys = nn(normed, qkv_ref[0, 1]).astype(bf16)
    values = nn(normed, qkv_ref[0, 2]).astype(bf16)
    query = nn(normed[:slots], qkv_ref[0, 0]).astype(bf16)
    columns, spread = head_columns(width), head_rows(width).astype(bf16)
    cut = [slice(g * slots, (g + 1) * slots) for g in range(pieces)]
    probs = message_probs(message_scores(query, [keys[c] for c in cut], columns))
    context = functools.reduce(
        jnp.add,
        [nn(p.astype(bf16), spread) * values[c].astype(f32) for p, c in zip(probs, cut)],
    ).astype(bf16)
    message = start[:slots].astype(f32) + nn(context, outw_ref[0])
    message_ref[...] = message
    unit, _ = unit_norm(message)
    nmsg = (unit * gains_ref[0:1, :]).astype(bf16)
    nmsg_ref[...] = nmsg.astype(f32)
    kmsg = nn(nmsg, qkv_ref[1, 1]).astype(bf16).astype(f32)
    vmsg = nn(nmsg, qkv_ref[1, 2]).astype(bf16).astype(f32)

    own = gathered[0][...].astype(f32)
    unit, _ = unit_norm(own)
    qcls = nn((unit * gains_ref[0:1, :]).astype(bf16), qkv_ref[1, 0]).astype(bf16).astype(f32) * SCALE
    head = lax.broadcasted_iota(jnp.int32, (16, width), 0)
    lane = lax.broadcasted_iota(jnp.int32, (16, width), 1)
    mine = (lane >= head * HEAD_DIM) & (lane < (head + 1) * HEAD_DIM)
    token = lax.broadcasted_iota(jnp.int32, (16, rows), 1)
    ctx[...] = jnp.zeros(ctx.shape, f32)
    kvmsg_ref[:, :width] = kmsg
    kvmsg_ref[:, width:] = vmsg
    queries = [jnp.where(mine, qcls[i : i + 1], 0.0) for i in range(count)]
    scores = [nt(queries[i].astype(bf16), kv_ref[i, :, :width]) for i in range(count)]
    probs = []
    for i in range(count):
        last = jnp.sum(queries[i] * kmsg[i : i + 1], axis=1, keepdims=True)
        score = jnp.where(token == tokens - 1, last, scores[i])
        score = jnp.where(token < tokens, score, MASKED)
        expo = jnp.exp(score - jnp.max(score, axis=1, keepdims=True))
        probs.append((expo / jnp.sum(expo, axis=1, keepdims=True)).astype(bf16))
    outs = [nn(probs[i], kv_ref[i, :, width:]) for i in range(count)]
    for i in range(count):
        extra = jnp.sum(
            jnp.where(token == tokens - 1, probs[i].astype(f32), 0.0), axis=1, keepdims=True
        )
        out = outs[i] + extra * vmsg[i : i + 1]
        ctx[i : i + 1, :] = row_sum(jnp.where(mine, out, 0.0))
    resid = own + nn(ctx[...].astype(bf16), outw_ref[1])
    unit, _ = unit_norm(resid)
    hidden = nn((unit * gains_ref[1:2, :]).astype(bf16), up_ref[...])
    active = (hidden * sigmoid(1.702 * hidden)).astype(bf16)
    final = resid + nn(active, down_ref[...])
    final_ref[...] = final
    unit, _ = unit_norm(final)
    visual_ref[...] = (unit * gains_ref[2:3, :]).astype(bf16)


def first_rows(gathered, mw, mg, qkv, outw, up, down, gains, kv, tokens):
    count, width = kv.shape[0], mw.shape[0]
    slots = gathered[0].shape[0]
    operands = list(gathered) + [mw, mg, qkv, outw, up, down, gains, kv]
    return pl.pallas_call(
        functools.partial(first_kernel, len(gathered), count, tokens),
        grid=(1,),
        in_specs=[full(x.shape) for x in gathered]
        + [
            full(mw.shape),
            full(mg.shape),
            pl.BlockSpec((2, 3, width, width), lambda i: (0, 0, 0, 0)),
            pl.BlockSpec((2, width, width), lambda i: (0, 0, 0)),
            full(up.shape),
            full(down.shape),
            full(gains.shape),
            full(kv.shape),
        ],
        out_specs=[full((slots, width))] * 2 + [full((slots, 2 * width))] + [full((slots, width))] * 2,
        out_shape=[
            shape_of((slots, width), f32),
            shape_of((slots, width), f32),
            shape_of((slots, 2 * width), f32),
            shape_of((slots, width), bf16),
            shape_of((slots, width), f32),
        ],
        scratch_shapes=[pltpu.VMEM((slots, width), f32)],
        compiler_params=params(16),
        cost_estimate=cost(4e9, 12e6),
        name="first_rows",
    )(*operands)


def with_message(block, rows_ref, tokens, frame):
    top = (tokens - 1) // 16 * 16
    tail = block[top : top + 16].astype(f32)
    index = lax.broadcasted_iota(jnp.int32, tail.shape, 0)
    tail = jnp.where(index == tokens - 1 - top, rows_ref[pl.ds(frame, 1), :], tail).astype(bf16)
    pieces = [block[:top], tail]
    if top + 16 < block.shape[0]:
        pieces.append(block[top + 16 :])
    return jnp.concatenate(pieces, axis=0)


def masked_tail(scores, tokens):
    top = tokens // 16 * 16
    if top >= scores.shape[0]:
        return scores
    tail = scores[top:]
    index = lax.broadcasted_iota(jnp.int32, tail.shape, 0)
    return jnp.concatenate([scores[:top], jnp.where(index < tokens - top, tail, MASKED)], axis=0)


def half_pair(block_t, head):
    own = block_t[head * HEAD_DIM : (head + 1) * HEAD_DIM]
    none = jnp.zeros(own.shape, own.dtype)
    return jnp.concatenate([own, none] if head % 2 == 0 else [none, own], axis=0)


def pair_lanes(block, head):
    at = head // 2 * 2 * HEAD_DIM
    return block[:, at : at + 2 * HEAD_DIM]


def attend_kernel(
    tokens, normed_ref, kv_ref, video_ref, message_ref, nmsg_ref, kvmsg_ref, wq_ref, wv_ref, wo_ref,
    *refs,
):
    resid_ref, ctx_ref, lse_ref, wqt, wvt = refs[-5:]
    step = pl.program_id(0)

    @pl.when(step == 0)
    def _():
        wqt[...] = wq_ref[...].T
        wvt[...] = wv_ref[...].T

    batch, rows, width = normed_ref.shape
    normed, keys = [], []
    for i in range(batch):
        frame = step * batch + i
        normed.append(with_message(normed_ref[i], nmsg_ref, tokens, frame))
        keys.append(with_message(kv_ref[i], kvmsg_ref, tokens, frame))
    queries_t = [nt(wqt[...], n).astype(bf16) * jnp.bfloat16(SCALE) for n in normed]
    values_t = [nt(wvt[...], n).astype(bf16) for n in normed]
    jobs = [(i, h) for i in range(batch) for h in range(HEADS)]
    contexts, stats, scores, expos, totals = {}, {}, {}, {}, {}

    def score(job):
        i, head = job
        scores[job] = nn(pair_lanes(keys[i], head), half_pair(queries_t[i], head))

    def soften(job):
        one = masked_tail(scores.pop(job), tokens)
        top = jnp.max(one, axis=0, keepdims=True)
        expo = jnp.exp(one - top)
        totals[job] = row_sum(expo)
        expos[job] = expo.astype(bf16)
        stats[job] = top + jnp.log(totals[job])

    def mix(job):
        i, head = job
        own = values_t[i][head * HEAD_DIM : (head + 1) * HEAD_DIM]
        contexts[job] = nn(own, expos.pop(job)) * (1.0 / totals[job])

    stagger(jobs, [score, soften, mix], 3)
    for i in range(batch):
        context_t = jnp.concatenate([contexts[i, h] for h in range(HEADS)], axis=0).astype(bf16)
        ctx_ref[i] = context_t
        pad = [jnp.zeros((8 - HEADS, rows), f32)]
        lse_ref[i] = jnp.concatenate([stats[i, h] for h in range(HEADS)] + pad, axis=0)
        row = message_ref[pl.ds(step * batch + i, 1), :]
        base = put_row(pad_rows(video_ref[i].astype(f32), rows), tokens - 1, row)
        resid_ref[i] = base + tn(context_t, wo_ref[...])


def attend(normed, kv, video, message, nmsg, kvmsg, qkv, outw, tokens, after=()):
    count, rows, width = normed.shape
    slots = message.shape[0]
    batch = share_of(count, 2)
    return pl.pallas_call(
        functools.partial(attend_kernel, tokens),
        grid=(count // batch,),
        in_specs=[
            frames_block(batch, (rows, width)),
            frames_block(batch, (rows, 2 * width)),
            frames_block(batch, video.shape[1:]),
            full((slots, width)),
            full((slots, width)),
            full((slots, 2 * width)),
            square(width, 1, 0),
            square(width, 1, 2),
            square(width, 1),
        ]
        + [pl.BlockSpec(memory_space=pl.ANY)] * len(after),
        out_specs=[
            frames_block(batch, (rows, width)),
            frames_block(batch, (width, rows)),
            frames_block(batch, (8, rows)),
        ],
        out_shape=[
            shape_of((count, rows, width), f32),
            shape_of((count, width, rows), bf16),
            shape_of((count, 8, rows), f32),
        ],
        scratch_shapes=[pltpu.VMEM((width, width), bf16)] * 2,
        compiler_params=params(20),
        cost_estimate=cost(14e9, 10e6),
        name="attend",
    )(normed, kv, video, message, nmsg, kvmsg, qkv, qkv, outw, *after)


def caption_kernel(
    pieces, groups, clips, local, where_ref, lengths_ref, *refs
):
    gathered = refs[:pieces]
    caps_ref, cot_ref, qkv_ref, outw_ref, gains_ref = refs[pieces : pieces + 5]
    out_ref, grad_ref, gain_ref = refs[pieces + 5 : pieces + 8]
    part_refs = refs[pieces + 8 : pieces + 8 + pieces]
    keep_ref, send_ref, acc = refs[pieces + 8 + pieces :]
    width = caps_ref.shape[1]
    slots = gathered[0].shape[0]
    count = caps_ref.shape[0]
    keys_n = pieces * slots
    runs = lengths_ref.shape[1]

    token = lax.broadcasted_iota(jnp.int32, (count, keys_n), 0)
    key = lax.broadcasted_iota(jnp.int32, (count, keys_n), 1)
    slot = key % slots
    group = token // local
    position = token - group * local + where_ref[0] * local
    document = jnp.zeros((count, keys_n), jnp.int32)
    for m in range(groups):
        end = jnp.int32(0)
        for j in range(runs):
            end = end + lengths_ref[m, j]
            document = document + jnp.where((group == m) & (position >= end), 1, 0)
    allowed = slot == group * clips + document % clips
    valid = (document[:, 0:1] < runs - 1).astype(f32)

    pack = caps_ref[...].astype(f32)
    unit, inv = unit_norm(pack)
    gain = gains_ref[3:4, :]
    normed = (unit * gain).astype(bf16)
    visual = jnp.concatenate([g[...] for g in gathered], axis=0)
    queries = nn(normed, qkv_ref[0, 0]).astype(bf16)
    keys = nn(visual, qkv_ref[0, 1]).astype(bf16)
    values = nn(visual, qkv_ref[0, 2]).astype(bf16)

    masks = [head_mask((count, width), 1, h) for h in range(HEADS)]
    zero = jnp.zeros((count, width), bf16)

    def by_head(x):
        return jnp.concatenate([jnp.where(m, x, zero) for m in masks], axis=0)

    def merge(x):
        cut = [x[h * count : (h + 1) * count] for h in range(HEADS)]
        return functools.reduce(jnp.add, [jnp.where(m, c, 0.0) for m, c in zip(masks, cut)])

    allowed_all = jnp.concatenate([allowed.astype(jnp.int32)] * HEADS, axis=0) > 0
    split_q = by_head(queries)
    scores = jnp.where(allowed_all, nt(split_q, keys) * SCALE, MASKED)
    expo = jnp.exp(scores - jnp.max(scores, axis=1, keepdims=True))
    probs = expo / jnp.sum(expo, axis=1, keepdims=True)
    low = probs.astype(bf16)
    context = merge(nn(low, values)).astype(bf16)
    out_ref[...] = (pack + valid * nn(context, outw_ref[0])).astype(bf16)

    cot = cot_ref[...].astype(f32)
    branch = (cot * valid).astype(bf16)
    split_d = by_head(nt(branch, outw_ref[0]).astype(bf16))
    dvalues = tn(low, split_d)
    dprobs = nt(split_d, values)
    dscores = probs * (dprobs - jnp.sum(dprobs * probs, axis=1, keepdims=True))
    dscores = jnp.where(allowed_all, dscores, 0.0).astype(bf16)
    dqueries = (merge(nn(dscores, keys)) * SCALE).astype(bf16)
    dkeys = tn(dscores, split_q) * SCALE
    dnormed = nt(dqueries, qkv_ref[0, 0])
    grad_ref[...] = (cot + norm_back(unit, inv, gain, dnormed)).astype(bf16)
    gain_ref[...] = jnp.concatenate([row_sum(dnormed * unit), jnp.zeros((7, width), f32)], axis=0)
    low_k, low_v = dkeys.astype(bf16), dvalues.astype(bf16)
    part = nt(low_k, qkv_ref[0, 1]) + nt(low_v, qkv_ref[0, 2])
    for g in range(pieces):
        part_refs[g][...] = part[g * slots : (g + 1) * slots]
    if acc.shape[0] > 4 * width:
        acc[...] = jnp.zeros(acc.shape, f32)
    acc[0:width, :] = tn(normed, dqueries)
    acc[width : 2 * width, :] = tn(visual, low_k)
    acc[2 * width : 3 * width, :] = tn(visual, low_v)
    acc[3 * width : 4 * width, :] = tn(context, branch)
    emit(where_ref, acc, keep_ref, send_ref)


def captions_step(where, lengths, gathered, caps, cot, qkv, outw, gains, plan):
    count, width = caps.shape
    groups = lengths.shape[0]
    pieces = len(gathered)
    slots = gathered[0].shape[0]
    operands = list(gathered) + [caps, cot, qkv, outw, gains]
    acc_rows, packet_specs, packet_shapes = plan.packet(4 * width, width)
    return pl.pallas_call(
        functools.partial(caption_kernel, pieces, groups, plan.clips, count // groups),
        grid=(1,),
        in_specs=[scalars(), scalars()]
        + [full(x.shape) for x in operands[:-3]]
        + [
            pl.BlockSpec((1, 3, width, width), lambda i: (2, 0, 0, 0)),
            pl.BlockSpec((1, width, width), lambda i: (2, 0, 0)),
            full(gains.shape),
        ],
        out_specs=[full((count, width))] * 2
        + [full((8, width))]
        + [full((slots, width))] * pieces
        + packet_specs,
        out_shape=[shape_of((count, width), bf16)] * 2
        + [shape_of((8, width), f32)]
        + [shape_of((slots, width), f32)] * pieces
        + packet_shapes,
        scratch_shapes=[pltpu.VMEM((acc_rows, width), f32)],
        compiler_params=params(12),
        cost_estimate=cost(4e9, 8e6),
        name="captions_step",
    )(where, lengths, *operands)


def mlp_kernel(
    pieces, patch, ff, where_ref, resid_ref, cot_ref, final_ref, gains_ref, up_ref, down_ref, *refs
):
    parts = refs[:pieces]
    out_ref, dresid_ref, gain_ref, keep_ref, send_ref, acc, dcls = refs[-7:]
    step = pl.program_id(0)
    batch, rows, width = resid_ref.shape
    wide = acc.shape[1]
    blocks = ff // wide

    @pl.when(step == 0)
    def _():
        acc[...] = jnp.zeros(acc.shape, f32)
        dvisual = functools.reduce(jnp.add, [p[...] for p in parts])
        unit, inv = unit_norm(final_ref[...])
        dcls[...] = norm_back(unit, inv, gains_ref[2:3, :], dvisual)
        gain_ref[...] = jnp.concatenate(
            [jnp.zeros((1, width), f32), row_sum(dvisual * unit), jnp.zeros((6, width), f32)],
            axis=0,
        )

    resid = resid_ref[...].reshape(batch * rows, width)
    gain = gains_ref[1:2, :]
    unit, inv = unit_norm(resid)
    normed32 = unit * gain
    normed = normed32.astype(bf16)
    normed_t = normed32.T.astype(bf16)
    pieces_d = []
    for i in range(batch):
        one = pad_rows(cot_ref[i].astype(f32), rows)
        pieces_d.append(put_row(one, 0, one[0:1] + dcls[pl.ds(step * batch + i, 1), :]))
    dfinal = jnp.concatenate(pieces_d, axis=0)
    branch = dfinal.astype(bf16)
    branch_t = dfinal.T.astype(bf16)
    final = resid
    dnormed = jnp.zeros((batch * rows, width), f32)
    for c in range(blocks):
        span = slice(c * wide, (c + 1) * wide)
        hidden = nn(normed, up_ref[:, span])
        gate = sigmoid(1.702 * hidden)
        active = (hidden * gate).astype(bf16)
        final = final + nn(active, down_ref[span, :])
        dactive = nt(branch, down_ref[span, :])
        dhidden = (dactive * gate * (1.0 + 1.702 * hidden * (1.0 - gate))).astype(bf16)
        dnormed = dnormed + nt(dhidden, up_ref[:, span])
        acc[c * width : (c + 1) * width, :] += nn(normed_t, dhidden)
        acc[(blocks + c) * width : (blocks + c + 1) * width, :] += nn(branch_t, active)
    for i in range(batch):
        out_ref[i] = final[i * rows : i * rows + patch].astype(bf16)
    dresid = dfinal + norm_back(unit, inv, gain, dnormed)
    dresid_ref[...] = dresid.reshape(batch, rows, width)
    gain_ref[0:1, :] += row_sum(dnormed * unit)

    @pl.when(step == pl.num_programs(0) - 1)
    def _():
        emit(where_ref, acc, keep_ref, send_ref)


def mlp_step(where, resid, cot, final, gains, up, down, parts, plan, after=()):
    count, rows, width = resid.shape
    patch = cot.shape[1]
    ff = up.shape[1]
    slots = final.shape[0]
    batch = share_of(count, 2)
    wide = 2 * width
    acc_rows, packet_specs, packet_shapes = plan.packet(2 * ff * width // wide, wide)
    return pl.pallas_call(
        functools.partial(mlp_kernel, len(parts), patch, ff),
        grid=(count // batch,),
        in_specs=[
            scalars(),
            frames_block(batch, (rows, width)),
            frames_block(batch, (patch, width)),
            full((slots, width)),
            full(gains.shape),
            full(up.shape),
            full(down.shape),
        ]
        + [full((slots, width))] * len(parts)
        + [pl.BlockSpec(memory_space=pl.ANY)] * len(after),
        out_specs=[
            frames_block(batch, (patch, width)),
            frames_block(batch, (rows, width)),
            full((8, width)),
        ]
        + packet_specs,
        out_shape=[
            shape_of((count, patch, width), bf16),
            shape_of((count, rows, width), f32),
            shape_of((8, width), f32),
        ]
        + packet_shapes,
        scratch_shapes=[pltpu.VMEM((acc_rows, wide), f32), pltpu.VMEM((slots, width), f32)],
        compiler_params=params(36),
        cost_estimate=cost(20e9, 20e6),
        name="mlp_step",
    )(where, resid, cot, final, gains, up, down, *parts, *after)


def attend_back_kernel(tokens, first, last, waits, where_ref, normed_ref, kv_ref, *refs):
    (
        video_ref, message_ref, nmsg_ref, kvmsg_ref, ctx_ref, lse_ref, dresid_ref, gains_ref,
        wq_ref, wk_ref, wv_ref, wo_ref,
    ) = refs[:12]
    refs = refs[12:]
    if first:
        carried, refs = refs[1:5], refs[5:]
    refs = refs[waits:]
    outs = refs[: 6 if last else 5]
    grad_ref, dmsg_ref, dcls_ref, gain_ref = outs[:4]
    acc, wqt, wkt, wall = refs[len(outs) :]
    here = pl.program_id(0)
    step = here + first
    batch, rows, width = dresid_ref.shape
    patch = tokens - 1

    @pl.when(here == 0)
    def _():
        wqt[...] = wq_ref[...].T
        wkt[...] = wk_ref[...].T
        wall[:, 0:width] = wq_ref[...]
        wall[:, width : 2 * width] = wk_ref[...]
        wall[:, 2 * width : 3 * width] = wv_ref[...]
        for k, ref in enumerate((dmsg_ref, dcls_ref, gain_ref, acc)):
            ref[...] = carried[k][...] if first else jnp.zeros(ref.shape, f32)

    frames = range(batch)
    normed, kv = [], []
    for i in frames:
        normed.append(with_message(normed_ref[i], nmsg_ref, tokens, step * batch + i))
        kv.append(with_message(kv_ref[i], kvmsg_ref, tokens, step * batch + i))
    branch = [dresid_ref[i].astype(bf16) for i in frames]
    queries_t = [nt(wqt[...], n).astype(bf16) * jnp.bfloat16(SCALE) for n in normed]
    dcontext_t = [nt(wo_ref[...], b).astype(bf16) for b in branch]
    keys_t = [nt(wkt[...], n).astype(bf16) for n in normed]
    acc[3 * width : 4 * width, :] += functools.reduce(
        jnp.add, [nn(ctx_ref[i], branch[i]) for i in frames]
    )
    jobs = [(i, h) for i in frames for h in range(HEADS)]
    own = [slice(h * HEAD_DIM, (h + 1) * HEAD_DIM) for h in range(HEADS)]
    scores, dprobs, low, dscores, dq, dk, dv = {}, {}, {}, {}, {}, {}, {}

    def score(job):
        i, h = job
        scores[job] = nn(pair_lanes(kv[i], h), half_pair(queries_t[i], h))
        dprobs[job] = nn(pair_lanes(kv[i], HEADS + h), half_pair(dcontext_t[i], h))

    def soften(job):
        i, h = job
        probs = jnp.exp(masked_tail(scores.pop(job), tokens) - lse_ref[i, h : h + 1, :])
        low[job] = probs.astype(bf16)
        weighted = dprobs.pop(job) * probs
        dscores[job] = (weighted - probs * row_sum(weighted)).astype(bf16)

    def mix(job):
        i, h = job
        dq[job] = nn(keys_t[i][own[h]], dscores[job]) * SCALE
        dk[job] = nt(queries_t[i][own[h]], dscores.pop(job))
        dv[job] = nt(dcontext_t[i][own[h]], low.pop(job))

    stagger(jobs, [score, soften, mix], 2)
    dall = []
    for i in frames:
        parts = [d[i, h] for d in (dq, dk, dv) for h in range(HEADS)]
        dall.append(jnp.concatenate(parts, axis=0).astype(bf16))
    acc[0 : 3 * width, :] += functools.reduce(
        jnp.add, [nn(dall[i], normed[i]) for i in frames]
    )
    gain_sum = jnp.zeros((1, width), f32)
    for i in frames:
        dnormed = nn(wall[...], dall[i]).T
        at = pl.ds(step * batch + i, 1)
        base = put_row(pad_rows(video_ref[i].astype(f32), rows), tokens - 1, message_ref[at, :])
        unit, inv = unit_norm(base)
        dtokens = dresid_ref[i] + norm_back(unit, inv, gains_ref[0:1, :], dnormed)
        gain_sum = gain_sum + row_sum(dnormed * unit)
        grad_ref[i] = dtokens[:patch].astype(bf16)
        dcls_ref[at, :] = dtokens[0:1]
        dmsg_ref[at, :] = dtokens[patch : patch + 1]
    gain_ref[0:1, :] += gain_sum

    @pl.when(here == pl.num_programs(0) - 1)
    def _():
        if last:
            emit(where_ref, acc, *outs[4:])
        else:
            outs[4][...] = acc[...]


def attend_back(
    where, normed, kv, video, message, nmsg, kvmsg, ctx, lse, dresid, gains, qkv, outw, plan,
    batch, first, steps, carried=(), after=(),
):
    count, rows, width = normed.shape
    patch = video.shape[1]
    slots = message.shape[0]
    last = (first + steps) * batch == count
    acc_rows, packet_specs, packet_shapes = plan.packet(4 * width, width)
    if not last:
        packet_specs, packet_shapes = [full((acc_rows, width))], [shape_of((acc_rows, width), f32)]

    def block(shape):
        return pl.BlockSpec((batch,) + shape, lambda i, *_: (i + first, 0, 0))

    anywhere = pl.BlockSpec(memory_space=pl.ANY)
    carry_specs = [anywhere] + [full(x.shape) for x in carried[1:]] if carried else []
    return pl.pallas_call(
        functools.partial(attend_back_kernel, patch + 1, first, last, len(after)),
        grid=(steps,),
        in_specs=[
            scalars(),
            block((rows, width)),
            block((rows, 2 * width)),
            block((patch, width)),
            full((slots, width)),
            full((slots, width)),
            full((slots, 2 * width)),
            block((width, rows)),
            block((8, rows)),
            block((rows, width)),
            full(gains.shape),
            square(width, 1, 0),
            square(width, 1, 1),
            square(width, 1, 2),
            square(width, 1),
        ]
        + carry_specs
        + [anywhere] * len(after),
        out_specs=[block((patch, width))]
        + [full((slots, width))] * 2
        + [full((8, width))]
        + packet_specs,
        out_shape=[shape_of((count, patch, width), bf16)]
        + [shape_of((slots, width), f32)] * 2
        + [shape_of((8, width), f32)]
        + packet_shapes,
        input_output_aliases={15: 0} if carried else {},
        scratch_shapes=[
            pltpu.VMEM((acc_rows, width), f32),
            pltpu.VMEM((width, width), bf16),
            pltpu.VMEM((width, width), bf16),
            pltpu.VMEM((width, 3 * width), bf16),
        ],
        compiler_params=params(26),
        cost_estimate=cost(4.5e9 * steps, 4e6 * steps),
        name="attend_back",
    )(
        where, normed, kv, video, message, nmsg, kvmsg, ctx, lse, dresid, gains, qkv, qkv, qkv,
        outw, *carried, *after,
    )


class Groups:
    def __init__(self, layout, slots):
        self.segs, self.frames, self.clips = layout
        self.slots = slots
        self.groups = self.segs * self.clips
        self.together = max(1, min(self.groups, 512 // (self.frames * slots)))
        self.steps = self.groups // self.together
        self.rows = self.frames * self.together * slots
        per_group = self.frames * slots
        self.side = per_group * max(1, min(self.together, 128 // per_group))
        self.blocks = [slice(at, at + self.side) for at in range(0, self.rows, self.side)]
        self.jobs = [(i, h) for i in range(len(self.blocks)) for h in range(HEADS)]

    def row_of(self, s, f, c):
        group = s * self.clips + c
        step, inside = group // self.together, group % self.together
        return step, pl.multiple_of((inside * self.frames + f) * self.slots, 16)

    def every(self, where_ref):
        me_f, me_s, me_c = where_ref[0], where_ref[1], where_ref[2]
        for a in range(self.segs):
            for b in range(self.frames):
                for d in range(self.clips):
                    yield a, b, d, *self.row_of(me_s ^ a, me_f ^ b, me_c ^ d)

    def run(self, batch):
        def first(ref, at, value):
            ref[at] = value

        def again(ref, at, value):
            ref[at] += value

        batch(0, first)
        if self.steps > 1:
            pl.loop(1, self.steps)(lambda step: batch(step, again))


def join(groups, *parts):
    lanes = [
        jnp.concatenate([p[i, h] for p in parts for h in range(HEADS)], axis=0)
        for i in range(len(groups.blocks))
    ]
    return (jnp.concatenate(lanes, axis=1) if len(lanes) > 1 else lanes[0]).astype(bf16)


OWN = [slice(h * HEAD_DIM, (h + 1) * HEAD_DIM) for h in range(HEADS)]


def message_forward_kernel(groups, where_ref, *refs):
    side = refs[: groups.segs]
    (
        mw_ref, mg_ref, qkv_ref, classes_ref, start_ref, values_ref, qt_ref, kt_ref, probs_ref,
        ctx_ref, wqt, wkt, wvt,
    ) = refs[groups.segs :]
    for a, b, d, step, row in groups.every(where_ref):
        classes_ref[step, pl.ds(row, groups.slots), :] = side[a][d, b]
    wqt[...] = qkv_ref[0, 0].T
    wkt[...] = qkv_ref[0, 1].T
    wvt[...] = qkv_ref[0, 2].T
    edge = (groups.side, groups.side)
    key, query = lax.broadcasted_iota(jnp.int32, edge, 0), lax.broadcasted_iota(jnp.int32, edge, 1)
    per_group = groups.frames * groups.slots
    same = (key % groups.slots == query % groups.slots) & (key // per_group == query // per_group)

    def batch(step, put):
        del put
        start = nn(classes_ref[step], mw_ref[...]).astype(bf16)
        start_ref[step] = start
        unit, _ = unit_norm(start.astype(f32))
        normed = (unit * mg_ref[...]).astype(bf16)
        keys = nn(normed, qkv_ref[0, 1]).astype(bf16)
        values_ref[step] = nn(normed, qkv_ref[0, 2]).astype(bf16)
        queries_t = nt(wqt[...], normed).astype(bf16) * jnp.bfloat16(SCALE)
        values_t = nt(wvt[...], normed).astype(bf16)
        qt_ref[step] = queries_t
        kt_ref[step] = nt(wkt[...], normed).astype(bf16)
        scores, low, ctx = {}, {}, {}

        def score(job):
            i, h = job
            at = groups.blocks[i]
            scores[job] = nn(pair_lanes(keys[at], h), half_pair(queries_t[:, at], h))

        def soften(job):
            i, h = job
            one = jnp.where(same, scores.pop(job), MASKED)
            expo = jnp.exp(one - jnp.max(one, axis=0, keepdims=True))
            probs = expo * (1.0 / row_sum(expo))
            probs_ref[step, i * HEADS + h] = probs.astype(probs_ref.dtype)
            low[job] = probs.astype(bf16)

        def mix(job):
            i, h = job
            ctx[job] = nn(values_t[OWN[h], groups.blocks[i]], low.pop(job))

        stagger(groups.jobs, [score, soften, mix], 3)
        ctx_ref[step] = join(groups, ctx)

    groups.run(batch)


def message_forward(where, side, mw, mg, qkv, groups):
    width = mw.shape[0]
    rows, steps = groups.rows, groups.steps
    outs = [
        shape_of((steps, rows, width), bf16),
        shape_of((steps, rows, width), bf16),
        shape_of((steps, rows, width), bf16),
        shape_of((steps, width, rows), bf16),
        shape_of((steps, width, rows), bf16),
        shape_of((steps, len(groups.jobs), groups.side, groups.side), f32 if steps == 1 else bf16),
        shape_of((steps, width, rows), bf16),
    ]
    return pl.pallas_call(
        functools.partial(message_forward_kernel, groups),
        grid=(1,),
        in_specs=[scalars()]
        + [full(x.shape) for x in side]
        + [
            full(mw.shape),
            full(mg.shape),
            pl.BlockSpec((1, 3, width, width), lambda i: (0, 0, 0, 0)),
        ],
        out_specs=[full(x.shape) for x in outs],
        out_shape=outs,
        scratch_shapes=[pltpu.VMEM((width, width), bf16)] * 3,
        compiler_params=params(56),
        cost_estimate=cost(3e9, 6e6),
        name="message_forward",
    )(where, *side, mw, mg, qkv)


def message_back_kernel(layout, groups, where_ref, *refs):
    @pl.when(pl.program_id(0) == 0)
    def _():
        frame_part(layout, where_ref, *refs)

    @pl.when(pl.program_id(0) == 1)
    def _():
        message_part(groups, where_ref, *refs)


def frame_part(layout, where_ref, *refs):
    segs, frames, clips = layout
    pieces, refs = refs[: segs * frames], refs[segs * frames + 7 :]
    big_ref, out_ref, whole = refs[6], refs[7], refs[12]
    width = out_ref.shape[-1]
    chunk = whole.shape[0] // (segs * frames * clips)
    place(
        layout,
        where_ref,
        lambda a, b, d: pieces[a * frames + b][d * chunk : (d + 1) * chunk, :],
        whole,
        chunk,
    )
    for j in range(3):
        big_ref[0, j] = whole[j * width : (j + 1) * width, :].astype(f32).T
    out_ref[0] = whole[3 * width : 4 * width, :].astype(f32)


def message_part(groups, where_ref, *refs):
    count = groups.segs * groups.frames
    pieces, refs = refs[:count], refs[count:]
    classes_ref, start_ref, values_ref, qt_ref, kt_ref, probs_ref, ctx_ref = refs[:7]
    mw_ref, mg_ref, qkv_ref, outw_ref = refs[7:11]
    big_ref, out_ref, mwg_ref, gain_ref, gains_ref, dclass_ref, _, dmsgs, dstart, wall = refs[13:]
    width, slots = mw_ref.shape[0], groups.slots
    for a, b, d, step, row in groups.every(where_ref):
        piece = pieces[a * groups.frames + b]
        at = piece.shape[0] - (groups.clips - d) * slots
        dmsgs[step, pl.ds(row, slots), :] = piece[at : at + slots, :]
    gain_total = jnp.zeros((slots, width), f32)
    for i in range(groups.frames * groups.together):
        for step in range(groups.steps):
            gain_total += dmsgs[step, i * slots : (i + 1) * slots, :].astype(f32)
    gains_ref[...] = gain_total[slots - 4 : slots]
    for j in range(3):
        wall[:, j * width : (j + 1) * width] = qkv_ref[0, j]
    index = lax.broadcasted_iota(jnp.int32, (groups.rows, 1), 0) % slots
    my_step, my_row = groups.row_of(where_ref[1], where_ref[0], where_ref[2])

    def batch(step, put):
        dm = jnp.where(index < slots - 6, dmsgs[step].astype(f32), 0.0).astype(bf16)
        unit, inv = unit_norm(start_ref[step].astype(f32))
        normed = (unit * mg_ref[...]).astype(bf16)
        dcontext_t = nt(outw_ref[0], dm).astype(bf16)
        values, queries_t, keys_t = values_ref[step], qt_ref[step], kt_ref[step]
        dprobs, low, dscores, dq, dk, dv = {}, {}, {}, {}, {}, {}

        def score(job):
            i, h = job
            at = groups.blocks[i]
            dprobs[job] = nn(pair_lanes(values[at], h), half_pair(dcontext_t[:, at], h))

        def soften(job):
            i, h = job
            probs = probs_ref[step, i * HEADS + h].astype(f32)
            low[job] = probs.astype(bf16)
            weighted = dprobs.pop(job) * probs
            dscores[job] = (weighted - probs * row_sum(weighted)).astype(bf16)

        def mix(job):
            i, h = job
            at = groups.blocks[i]
            dq[job] = nn(keys_t[OWN[h], at], dscores[job]) * SCALE
            dk[job] = nt(queries_t[OWN[h], at], dscores.pop(job))
            dv[job] = nt(dcontext_t[OWN[h], at], low.pop(job))

        stagger(groups.jobs, [score, soften, mix], 2)
        put(out_ref, 0, nn(ctx_ref[step], dm))
        dall = join(groups, dq, dk, dv)
        grads = nn(dall, normed)
        for j in range(3):
            put(big_ref, (0, j), grads[j * width : (j + 1) * width].T)
        dnormed = nn(wall[...], dall).T
        put(gain_ref, ..., jnp.sum(dnormed * unit, axis=0))
        ds = norm_back(unit, inv, mg_ref[...], dnormed) + dm.astype(f32)
        dstart[...] = ds
        put(mwg_ref, ..., tn(classes_ref[step], ds.astype(bf16)))

        @pl.when(my_step == step)
        def _():
            dclass_ref[...] = nt(dstart[pl.ds(my_row, slots), :].astype(bf16), mw_ref[...])

    groups.run(batch)


def message_back(where, pieces, forward, mw, mg, qkv, outw, big, out, layout, groups):
    width = mw.shape[0]
    operands = list(pieces) + list(forward) + [mw, mg]
    chunk = pieces[0].shape[0] // groups.clips - groups.slots
    return pl.pallas_call(
        functools.partial(message_back_kernel, layout, groups),
        grid=(2,),
        in_specs=[scalars()]
        + [full(x.shape) for x in operands]
        + [
            pl.BlockSpec((1, 3, width, width), lambda i: (0, 0, 0, 0)),
            pl.BlockSpec((1, width, width), lambda i: (0, 0, 0)),
            pl.BlockSpec(memory_space=pl.ANY),
            pl.BlockSpec(memory_space=pl.ANY),
        ],
        out_specs=[
            pl.BlockSpec((1, 3, width, width), lambda i: (1 - i, 0, 0, 0)),
            pl.BlockSpec((1, width, width), lambda i: (1 - i, 0, 0)),
            full((width, width)),
            full((width,)),
            full((4, width)),
            full((groups.slots, width)),
        ],
        out_shape=[
            shape_of((3, 3, width, width), f32),
            shape_of((3, width, width), f32),
            shape_of((width, width), f32),
            shape_of((width,), f32),
            shape_of((4, width), f32),
            shape_of((groups.slots, width), f32),
        ],
        input_output_aliases={len(operands) + 3: 0, len(operands) + 4: 1},
        scratch_shapes=[
            pltpu.VMEM((groups.groups * groups.frames * chunk, width), bf16),
            pltpu.VMEM((groups.steps, groups.rows, width), bf16),
            pltpu.VMEM((groups.rows, width), f32),
            pltpu.VMEM((width, 3 * width), bf16),
        ],
        compiler_params=params(30 if groups.steps == 1 else 60),
        cost_estimate=cost(4e9, 12e6),
        name="message_back",
    )(where, *operands, qkv, outw, big, out)


def emit(where_ref, acc, keep_ref, send_ref):
    frames, clips, chunk = keep_ref.shape[:3]
    me_f, me_s = where_ref[0], where_ref[1]
    for a, out in enumerate((keep_ref, send_ref)):
        for b in range(frames):
            for d in range(clips):
                to = ((me_s ^ a) * frames + (me_f ^ b)) * clips + d
                at = pl.multiple_of(to * chunk, 16)
                out[b, d] = acc[pl.ds(at, chunk), :].astype(bf16)


class Plan:
    def __init__(self, clips):
        self.clips = clips
        self.segs = lax.axis_size("seg")
        self.frames = lax.axis_size("frame")
        self.rings = lax.axis_size("clip")
        self.layout = (self.segs, self.frames, self.rings)
        self.devices = self.segs * self.frames * self.rings

    def chunk(self, rows):
        share = -(-rows // self.devices)
        return -(-share // 16) * 16

    def packet(self, rows, width):
        chunk = self.chunk(rows)
        shape = (self.frames, self.rings, chunk, width)
        return chunk * self.devices, [full(shape)] * 2, [shape_of(shape, bf16)] * 2


def swap(x, axis, k):
    count = lax.axis_size(axis)
    return lax.ppermute(x, axis, [(i, i ^ k) for i in range(count)])


def behind(x, *others):
    return lax.optimization_barrier((x, others))[0]


class Sum:
    def __init__(self, arrays, views=None):
        self.arrays = list(arrays)
        self.views = list(views or [()] * len(self.arrays))

    def part(self, view):
        return Sum(self.arrays, [v + (view,) for v in self.views])

    def plus(self, *arrays):
        return Sum(self.arrays + list(arrays), self.views + [()] * len(arrays))

    def value(self):
        terms = []
        for x, views in zip(self.arrays, self.views):
            for view in views:
                x = view(x)
            terms.append(x.astype(f32))
        return functools.reduce(jnp.add, terms).astype(bf16)


jax.tree_util.register_pytree_node(
    Sum, lambda s: (s.arrays, s.views), lambda views, arrays: Sum(arrays, views)
)


def at(k):
    return lambda x: x[k]


def total(one, two):
    return (one.astype(f32) + two.astype(f32)).astype(bf16)


def reduce_seg(keep, send):
    return Sum([keep, swap(send, "seg", 1)])


def frame_sends(terms):
    return [terms.part(at(b)).value() for b in range(1, lax.axis_size("frame"))]


def reduce_frame(terms, sends):
    return terms.part(at(0)).plus(*[swap(x, "frame", b + 1) for b, x in enumerate(sends)])


def clip_bits():
    count = lax.axis_size("clip")
    return [1 << j for j in range(count.bit_length() - 1)]


def swap_two(one, two, axis, k):
    width = one.shape[-1]
    rows = one.size // width
    got = swap(jnp.concatenate([one.reshape(-1, width), two.reshape(-1, width)]), axis, k)
    return got[:rows].reshape(one.shape), got[rows:].reshape(two.shape)


def exchange(part, rows, bit):
    got, got_rows = swap_two(part, rows, "clip", bit)
    return total(part, got), jnp.concatenate([rows, got_rows])


def gather_frame(held):
    return [held] + [swap(held, "frame", b) for b in range(1, lax.axis_size("frame"))]


def gather_seg(held):
    return held + [swap(h, "seg", 1) for h in held]


def place(layout, where_ref, piece, whole, chunk):
    segs, frames, clips = layout
    me_f, me_s = where_ref[0], where_ref[1]
    for a in range(segs):
        for b in range(frames):
            for d in range(clips):
                of = ((me_s ^ a) * frames + (me_f ^ b)) * clips + d
                whole[pl.ds(pl.multiple_of(of * chunk, 16), chunk), :] = piece(a, b, d)


def unpack_kernel(layout, where_ref, *refs):
    segs, frames, clips = layout
    main = refs[:segs]
    up_ref, down_ref, whole = refs[segs:]
    width, ff = up_ref.shape
    wide = whole.shape[1]
    place(layout, where_ref, lambda a, b, d: main[a][b * clips + d], whole, main[0].shape[1])
    blocks = ff // wide
    for c in range(blocks):
        span = slice(c * wide, (c + 1) * wide)
        up_ref[:, span] = whole[c * width : (c + 1) * width, :].astype(f32)
        other = whole[(blocks + c) * width : (blocks + c + 1) * width, :]
        down_ref[span, :] = other.astype(f32).T


def unpack(where, main, width, ff, plan):
    chunk, wide = main[0].shape[1:]
    return pl.pallas_call(
        functools.partial(unpack_kernel, plan.layout),
        grid=(1,),
        in_specs=[scalars()] + [full(x.shape) for x in main],
        out_specs=[full((width, ff)), full((ff, width))],
        out_shape=[shape_of((width, ff), f32), shape_of((ff, width), f32)],
        scratch_shapes=[pltpu.VMEM((plan.devices * chunk, wide), bf16)],
        compiler_params=params(40),
        cost_estimate=cost(2e9, 10e6),
        name="unpack",
    )(where, *main)


def unpack_side_kernel(layout, where_ref, *refs):
    segs = layout[0]
    side = refs[:segs]
    big_ref, out_ref, whole = refs[segs:]
    width = out_ref.shape[-1]
    place(layout, where_ref, lambda a, b, d: side[a][b, d], whole, side[0].shape[2])
    for j in range(3):
        big_ref[0, j] = whole[j * width : (j + 1) * width, :].astype(f32)
    out_ref[0] = whole[3 * width : 4 * width, :].astype(f32)


def unpack_side(where, side, plan):
    rows, width = side[0].shape[2:]
    return pl.pallas_call(
        functools.partial(unpack_side_kernel, plan.layout),
        grid=(1,),
        in_specs=[scalars()] + [full(x.shape) for x in side],
        out_specs=[
            pl.BlockSpec((1, 3, width, width), lambda i: (2, 0, 0, 0)),
            pl.BlockSpec((1, width, width), lambda i: (2, 0, 0)),
        ],
        out_shape=[shape_of((3, 3, width, width), f32), shape_of((3, width, width), f32)],
        scratch_shapes=[pltpu.VMEM((plan.devices * rows, width), bf16)],
        compiler_params=params(30),
        cost_estimate=cost(1e9, 4e6),
        name="unpack_side",
    )(where, *side)


def last_rows_kernel(gain_a, gain_b, gain_c, dmsg_ref, out_ref):
    slots, width = dmsg_ref.shape
    rows = [
        dmsg_ref[0 : slots - 6, :],
        jnp.zeros((2, width), f32),
        gain_a[0:1, :],
        gain_b[0:1, :],
        gain_b[1:2, :],
        gain_c[0:1, :],
    ]
    out_ref[...] = jnp.concatenate(rows, axis=0).astype(bf16)


def last_rows(gain_a, gain_b, gain_c, dmsg):
    return pl.pallas_call(
        last_rows_kernel,
        out_shape=shape_of(dmsg.shape, bf16),
        name="last_rows",
    )(gain_a, gain_b, gain_c, dmsg)


def local(
    video, captions, caption_lengths, message_weight, message_gain, qkv_weights, out_weights,
    mlp_up, mlp_down, gains, video_cot, caption_cot,
):
    micro, clips, per_frame, patch, width = video.shape
    count = micro * clips * per_frame
    ff = mlp_up.shape[1]
    plan = Plan(clips)
    tokens = patch + 1
    rows = -(-tokens // 16) * 16
    slots = -(-(count + 6) // 16) * 16
    where = jnp.stack(
        [lax.axis_index("frame"), lax.axis_index("seg"), lax.axis_index("clip")]
    ).astype(jnp.int32)
    frames = video.reshape(count, patch, width)
    cots = video_cot.reshape(count, patch, width)
    caps = captions.reshape(-1, width)
    cap_cots = caption_cot.reshape(-1, width)
    lengths = caption_lengths.reshape(micro, -1)
    gain = message_gain.reshape(1, width)

    classes = class_rows(video, slots)
    gathered = gather_frame(classes)
    normed, kv = norm_tokens(frames, gains, qkv_weights, rows)
    message, nmsg, kvmsg, visual, final = first_rows(
        gathered, message_weight, gain, qkv_weights, out_weights, mlp_up, mlp_down, gains,
        kv, tokens,
    )
    visuals = gather_frame(visual)
    results = captions_step(
        where, lengths, visuals, caps, cap_cots, qkv_weights, out_weights, gains, plan
    )
    caption_out, caption_grad, gain_c = results[:3]
    parts = list(results[3:-2])
    parts = [parts[0]] + [swap(parts[b], "frame", b) for b in range(1, plan.frames)]
    bits = clip_bits()
    rows_all = jnp.stack(gathered)[None]
    side = reduce_seg(*results[-2:])
    side = behind(side, results[3])
    sends = frame_sends(side)
    resid, ctx, lse = attend(
        normed, kv, frames, message, nmsg, kvmsg, qkv_weights, out_weights, tokens, sends
    )
    side = reduce_frame(side, sends)
    parts, resid, side = behind((parts, resid, side))
    side = side.value()
    side, resid = behind((side, resid))
    video_out, dresid, gain_b, keep, send = mlp_step(
        where, resid, cots, final, gains, mlp_up, mlp_down, parts, plan
    )
    for bit in bits[:-1]:
        side, rows_all = exchange(side, rows_all, bit)
    side, rows_all, video_out, dresid, keep, send = behind(
        (side, rows_all, video_out, dresid, keep, send)
    )
    main = reduce_seg(keep, send)
    turned = video_out.reshape(video.shape).transpose(1, 2, 3, 0, 4)
    main, dresid, turned = behind((main, dresid, turned))
    video_out = turned.transpose(3, 0, 1, 2, 4)
    sends = frame_sends(main)
    sends, dresid, side, rows_all = behind((sends, dresid, side, rows_all))
    batch = share_of(count, 2)
    steps = count // batch
    late_steps = 2
    back = functools.partial(
        attend_back, where, normed, kv, frames, message, nmsg, kvmsg, ctx, lse, dresid, gains,
        qkv_weights, out_weights, plan, batch,
    )
    carried = back(0, steps - late_steps)
    main = reduce_frame(main, sends)
    side, rows_all = exchange(side, rows_all, bits[-1])
    carried, main, side, rows_all = behind((carried, main, side, rows_all))
    main = main.value()
    main, carried, side = behind((main, carried, side))
    for bit in bits[:-1]:
        main = total(main, swap(main, "clip", bit))
    side = gather_frame(side)
    grad, dmsg, dcls, gain_a, keep, send = back(steps - late_steps, late_steps, carried)
    main, side, keep, send, gain_a, dmsg = behind((main, side, keep, send, gain_a, dmsg))

    main = total(main, swap(main, "clip", bits[-1]))
    late = reduce_seg(keep, send)
    rest = last_rows(gain_a, gain_b, gain_c, dmsg)
    side = jnp.stack(side)
    other, other_rows = swap_two(side, rows_all, "seg", 1)
    late, rest = behind((late, rest))
    late = reduce_frame(late, frame_sends(late))
    main, late, other, other_rows = behind((main, late, other, other_rows))

    held = gather_frame(main)
    late, rest = late.value(), rest[None]
    for bit in bits:
        late, rest = exchange(late, rest, bit)
    big, out = unpack_side(where, [side, other], plan)
    groups = Groups(plan.layout, slots)
    forward = message_forward(
        where, [rows_all, other_rows], message_weight, gain, qkv_weights, groups
    )
    held, late, rest, big, forward = behind((held, late, rest, big, forward))

    late = gather_frame(jnp.concatenate([late.reshape(-1, width), rest.reshape(-1, width)]))
    held = gather_seg([jnp.concatenate(held, axis=0)])
    up_grad, down_grad = unpack(where, held, width, ff, plan)
    late, up_grad = behind((late, up_grad))

    late = gather_seg(late)
    big, out, mw_grad, mg_grad, gains_grad, dclass = message_back(
        where, late, forward, message_weight, gain, qkv_weights, out_weights, big, out,
        plan.layout, groups,
    )
    fixed = (dclass + dcls)[:count].astype(bf16).reshape(micro, clips, per_frame, 1, width)
    grad = lax.dynamic_update_slice(grad.reshape(video.shape), fixed, (0, 0, 0, 0, 0))
    return (
        video_out.reshape(video.shape),
        caption_out.reshape(captions.shape),
        grad,
        caption_grad.reshape(captions.shape),
        mw_grad,
        mg_grad,
        big,
        out,
        up_grad,
        down_grad,
        gains_grad,
    )


def solution(mesh):
    rows = P(None, ("clip", "seg"), "frame", None, None)
    caps = P(None, ("clip", "seg"), "frame", None)
    return jax.shard_map(
        local,
        mesh=mesh,
        in_specs=(rows, caps, P(None, ("clip", "seg"), None)) + (P(),) * 7 + (rows, caps),
        out_specs=(rows, caps, rows, caps) + (P(),) * 7,
        check_vma=False,
    )
```

```python
import functools

import jax
import jax.numpy as jnp
from jax import lax
from jax.experimental import pallas as pl
from jax.experimental.pallas import tpu as pltpu
from jax.sharding import PartitionSpec as P

HEADS = 6
HEAD_DIM = 64
EPS = 1e-05
SCALE = 0.125
MASKED = -1e30

f32 = jnp.float32
bf16 = jnp.bfloat16


def nn(a, b):
    return lax.dot_general(a, b, (((1,), (0,)), ((), ())), preferred_element_type=f32)


def nt(a, b):
    return lax.dot_general(a, b, (((1,), (1,)), ((), ())), preferred_element_type=f32)


def tn(a, b):
    return lax.dot_general(a, b, (((0,), (0,)), ((), ())), preferred_element_type=f32)


def exact(a, b):
    return lax.dot_general(
        a, b, (((1,), (0,)), ((), ())), precision=lax.Precision.HIGHEST, preferred_element_type=f32
    )


def unit_norm(x):
    center = x - jnp.mean(x, axis=-1, keepdims=True)
    inv = lax.rsqrt(jnp.mean(center * center, axis=-1, keepdims=True) + EPS)
    return center * inv, inv


def norm_back(unit, inv, gain, dy):
    du = dy * gain
    mean_du = jnp.mean(du, axis=-1, keepdims=True)
    mean_dot = jnp.mean(du * unit, axis=-1, keepdims=True)
    return inv * (du - mean_du - unit * mean_dot)


def row_sum(x):
    return jnp.sum(x, axis=0, keepdims=True)


def sigmoid(x):
    return 0.5 + 0.5 * jnp.tanh(0.5 * x)


def head_mask(shape, lane_dim, head):
    lane = lax.broadcasted_iota(jnp.int32, shape, lane_dim)
    return (lane >= head * HEAD_DIM) & (lane < (head + 1) * HEAD_DIM)


def head_columns(width):
    lane = lax.broadcasted_iota(jnp.int32, (width, 128), 0)
    col = lax.broadcasted_iota(jnp.int32, (width, 128), 1)
    return ((lane >= col * HEAD_DIM) & (lane < (col + 1) * HEAD_DIM)).astype(f32)


def head_rows(width):
    col = lax.broadcasted_iota(jnp.int32, (128, width), 0)
    lane = lax.broadcasted_iota(jnp.int32, (128, width), 1)
    return ((lane >= col * HEAD_DIM) & (lane < (col + 1) * HEAD_DIM)).astype(f32)


def pad_rows(x, rows):
    if x.shape[0] == rows:
        return x
    return jnp.concatenate([x, jnp.zeros((rows - x.shape[0], x.shape[1]), x.dtype)], axis=0)


def put_row(block, at, row):
    top = at // 16 * 16
    tail = block[top : top + 16]
    index = lax.broadcasted_iota(jnp.int32, tail.shape, 0)
    tail = jnp.where(index == at - top, row, tail)
    pieces = [tail]
    if top:
        pieces.insert(0, block[:top])
    if top + 16 < block.shape[0]:
        pieces.append(block[top + 16 :])
    return jnp.concatenate(pieces, axis=0) if len(pieces) > 1 else tail


def full(shape):
    return pl.BlockSpec(shape, lambda *_: (0,) * len(shape))


def frame_block(shape):
    return pl.BlockSpec((1,) + shape, lambda i, *_: (i, 0, 0))


def frames_block(batch, shape):
    return pl.BlockSpec((batch,) + shape, lambda i, *_: (i, 0, 0))


def stagger(jobs, stages, gap):
    for at in range(len(jobs) + (len(stages) - 1) * gap):
        for k, stage in enumerate(stages):
            j = at - k * gap
            if 0 <= j < len(jobs):
                stage(jobs[j])


def share_of(count, most):
    return max(b for b in range(1, most + 1) if count % b == 0)


def square(width, *at):
    return pl.BlockSpec((None,) * len(at) + (width, width), lambda *_: at + (0, 0))


def scalars():
    return pl.BlockSpec(memory_space=pltpu.SMEM)


def shape_of(shape, dtype):
    return jax.ShapeDtypeStruct(shape, dtype)


def params(mib):
    return pltpu.CompilerParams(vmem_limit_bytes=mib * 1024 * 1024)


def cost(flops, nbytes):
    return pl.CostEstimate(flops=int(flops), bytes_accessed=int(nbytes), transcendentals=0)


def class_kernel(video_ref, out_ref):
    clips, _, micro, width = video_ref.shape
    rows = [video_ref[c, 0, m : m + 1, :].astype(f32) for m in range(micro) for c in range(clips)]
    out_ref[...] = pad_rows(jnp.concatenate(rows, axis=0), out_ref.shape[0]).astype(bf16)


def class_rows(video, slots):
    micro, clips, per_frame, patch, width = video.shape
    turned = video.transpose(1, 2, 3, 0, 4).reshape(clips * per_frame, patch, micro, width)
    return pl.pallas_call(
        class_kernel,
        grid=(1,),
        in_specs=[pl.BlockSpec((clips * per_frame, 1, micro, width), lambda i: (0, 0, 0, 0))],
        out_specs=full((slots, width)),
        out_shape=shape_of((slots, width), bf16),
        name="class_rows",
    )(turned)


def norm_kernel(video_ref, gains_ref, wk_ref, wv_ref, normed_ref, kv_ref, wkv):
    batch, rows, width = normed_ref.shape

    @pl.when(pl.program_id(0) == 0)
    def _():
        wkv[:, :width] = wk_ref[...]
        wkv[:, width:] = wv_ref[...]

    parts = []
    for i in range(batch):
        unit, _ = unit_norm(video_ref[i].astype(f32))
        parts.append(pad_rows(unit * gains_ref[0:1, :], rows).astype(bf16))
        normed_ref[i] = parts[i]
    normed = jnp.concatenate(parts, axis=0)
    kv_ref[...] = nn(normed, wkv[...]).astype(bf16).reshape(batch, rows, 2 * width)


def norm_tokens(video, gains, qkv, rows):
    count, patch, width = video.shape
    batch = share_of(count, 5)
    return pl.pallas_call(
        norm_kernel,
        grid=(count // batch,),
        in_specs=[
            frames_block(batch, (patch, width)),
            full(gains.shape),
            square(width, 1, 1),
            square(width, 1, 2),
        ],
        out_specs=[
            frames_block(batch, (rows, width)),
            frames_block(batch, (rows, 2 * width)),
        ],
        out_shape=[
            shape_of((count, rows, width), bf16),
            shape_of((count, rows, 2 * width), bf16),
        ],
        scratch_shapes=[pltpu.VMEM((width, 2 * width), bf16)],
        compiler_params=params(20),
        cost_estimate=cost(4 * count * rows * width * width, 8 * count * rows * width),
        name="norm_tokens",
    )(video, gains, qkv, qkv)


def message_scores(query, keys, columns):
    return [exact(query.astype(f32) * key.astype(f32), columns) * SCALE for key in keys]


def message_probs(scores):
    top = functools.reduce(jnp.maximum, scores)
    expo = [jnp.exp(score - top) for score in scores]
    total = functools.reduce(jnp.add, expo)
    return [e / total for e in expo]


def first_kernel(
    pieces, count, tokens, *refs
):
    gathered = refs[:pieces]
    (
        mw_ref, mg_ref, qkv_ref, outw_ref, up_ref, down_ref, gains_ref, kv_ref,
        message_ref, nmsg_ref, kvmsg_ref, visual_ref, final_ref, ctx,
    ) = refs[pieces:]
    width = mw_ref.shape[0]
    slots = gathered[0].shape[0]
    rows = kv_ref.shape[1]
    classes = jnp.concatenate([g[...] for g in gathered], axis=0)
    start = nn(classes, mw_ref[...]).astype(bf16)
    unit, _ = unit_norm(start.astype(f32))
    normed = (unit * mg_ref[...]).astype(bf16)
    keys = nn(normed, qkv_ref[0, 1]).astype(bf16)
    values = nn(normed, qkv_ref[0, 2]).astype(bf16)
    query = nn(normed[:slots], qkv_ref[0, 0]).astype(bf16)
    columns, spread = head_columns(width), head_rows(width).astype(bf16)
    cut = [slice(g * slots, (g + 1) * slots) for g in range(pieces)]
    probs = message_probs(message_scores(query, [keys[c] for c in cut], columns))
    context = functools.reduce(
        jnp.add,
        [nn(p.astype(bf16), spread) * values[c].astype(f32) for p, c in zip(probs, cut)],
    ).astype(bf16)
    message = start[:slots].astype(f32) + nn(context, outw_ref[0])
    message_ref[...] = message
    unit, _ = unit_norm(message)
    nmsg = (unit * gains_ref[0:1, :]).astype(bf16)
    nmsg_ref[...] = nmsg.astype(f32)
    kmsg = nn(nmsg, qkv_ref[1, 1]).astype(bf16).astype(f32)
    vmsg = nn(nmsg, qkv_ref[1, 2]).astype(bf16).astype(f32)

    own = gathered[0][...].astype(f32)
    unit, _ = unit_norm(own)
    qcls = nn((unit * gains_ref[0:1, :]).astype(bf16), qkv_ref[1, 0]).astype(bf16).astype(f32) * SCALE
    head = lax.broadcasted_iota(jnp.int32, (16, width), 0)
    lane = lax.broadcasted_iota(jnp.int32, (16, width), 1)
    mine = (lane >= head * HEAD_DIM) & (lane < (head + 1) * HEAD_DIM)
    token = lax.broadcasted_iota(jnp.int32, (16, rows), 1)
    ctx[...] = jnp.zeros(ctx.shape, f32)
    kvmsg_ref[:, :width] = kmsg
    kvmsg_ref[:, width:] = vmsg
    queries = [jnp.where(mine, qcls[i : i + 1], 0.0) for i in range(count)]
    scores = [nt(queries[i].astype(bf16), kv_ref[i, :, :width]) for i in range(count)]
    probs = []
    for i in range(count):
        last = jnp.sum(queries[i] * kmsg[i : i + 1], axis=1, keepdims=True)
        score = jnp.where(token == tokens - 1, last, scores[i])
        score = jnp.where(token < tokens, score, MASKED)
        expo = jnp.exp(score - jnp.max(score, axis=1, keepdims=True))
        probs.append((expo / jnp.sum(expo, axis=1, keepdims=True)).astype(bf16))
    outs = [nn(probs[i], kv_ref[i, :, width:]) for i in range(count)]
    for i in range(count):
        extra = jnp.sum(
            jnp.where(token == tokens - 1, probs[i].astype(f32), 0.0), axis=1, keepdims=True
        )
        out = outs[i] + extra * vmsg[i : i + 1]
        ctx[i : i + 1, :] = row_sum(jnp.where(mine, out, 0.0))
    resid = own + nn(ctx[...].astype(bf16), outw_ref[1])
    unit, _ = unit_norm(resid)
    hidden = nn((unit * gains_ref[1:2, :]).astype(bf16), up_ref[...])
    active = (hidden * sigmoid(1.702 * hidden)).astype(bf16)
    final = resid + nn(active, down_ref[...])
    final_ref[...] = final
    unit, _ = unit_norm(final)
    visual_ref[...] = (unit * gains_ref[2:3, :]).astype(bf16)


def first_rows(gathered, mw, mg, qkv, outw, up, down, gains, kv, tokens):
    count, width = kv.shape[0], mw.shape[0]
    slots = gathered[0].shape[0]
    operands = list(gathered) + [mw, mg, qkv, outw, up, down, gains, kv]
    return pl.pallas_call(
        functools.partial(first_kernel, len(gathered), count, tokens),
        grid=(1,),
        in_specs=[full(x.shape) for x in gathered]
        + [
            full(mw.shape),
            full(mg.shape),
            pl.BlockSpec((2, 3, width, width), lambda i: (0, 0, 0, 0)),
            pl.BlockSpec((2, width, width), lambda i: (0, 0, 0)),
            full(up.shape),
            full(down.shape),
            full(gains.shape),
            full(kv.shape),
        ],
        out_specs=[full((slots, width))] * 2 + [full((slots, 2 * width))] + [full((slots, width))] * 2,
        out_shape=[
            shape_of((slots, width), f32),
            shape_of((slots, width), f32),
            shape_of((slots, 2 * width), f32),
            shape_of((slots, width), bf16),
            shape_of((slots, width), f32),
        ],
        scratch_shapes=[pltpu.VMEM((slots, width), f32)],
        compiler_params=params(16),
        cost_estimate=cost(4e9, 12e6),
        name="first_rows",
    )(*operands)


def with_message(block, rows_ref, tokens, frame):
    top = (tokens - 1) // 16 * 16
    tail = block[top : top + 16].astype(f32)
    index = lax.broadcasted_iota(jnp.int32, tail.shape, 0)
    tail = jnp.where(index == tokens - 1 - top, rows_ref[pl.ds(frame, 1), :], tail).astype(bf16)
    pieces = [block[:top], tail]
    if top + 16 < block.shape[0]:
        pieces.append(block[top + 16 :])
    return jnp.concatenate(pieces, axis=0)


def masked_tail(scores, tokens):
    top = tokens // 16 * 16
    if top >= scores.shape[0]:
        return scores
    tail = scores[top:]
    index = lax.broadcasted_iota(jnp.int32, tail.shape, 0)
    return jnp.concatenate([scores[:top], jnp.where(index < tokens - top, tail, MASKED)], axis=0)


def half_pair(block_t, head):
    own = block_t[head * HEAD_DIM : (head + 1) * HEAD_DIM]
    none = jnp.zeros(own.shape, own.dtype)
    return jnp.concatenate([own, none] if head % 2 == 0 else [none, own], axis=0)


def pair_lanes(block, head):
    at = head // 2 * 2 * HEAD_DIM
    return block[:, at : at + 2 * HEAD_DIM]


def attend_kernel(
    tokens, normed_ref, kv_ref, video_ref, message_ref, nmsg_ref, kvmsg_ref, wq_ref, wv_ref, wo_ref,
    *refs,
):
    resid_ref, ctx_ref, lse_ref, wqt, wvt = refs[-5:]
    step = pl.program_id(0)

    @pl.when(step == 0)
    def _():
        wqt[...] = wq_ref[...].T
        wvt[...] = wv_ref[...].T

    batch, rows, width = normed_ref.shape
    normed, keys = [], []
    for i in range(batch):
        frame = step * batch + i
        normed.append(with_message(normed_ref[i], nmsg_ref, tokens, frame))
        keys.append(with_message(kv_ref[i], kvmsg_ref, tokens, frame))
    queries_t = [nt(wqt[...], n).astype(bf16) * jnp.bfloat16(SCALE) for n in normed]
    values_t = [nt(wvt[...], n).astype(bf16) for n in normed]
    jobs = [(i, h) for i in range(batch) for h in range(HEADS)]
    contexts, stats, scores, expos, totals = {}, {}, {}, {}, {}

    def score(job):
        i, head = job
        scores[job] = nn(pair_lanes(keys[i], head), half_pair(queries_t[i], head))

    def soften(job):
        one = masked_tail(scores.pop(job), tokens)
        top = jnp.max(one, axis=0, keepdims=True)
        expo = jnp.exp(one - top)
        totals[job] = row_sum(expo)
        expos[job] = expo.astype(bf16)
        stats[job] = top + jnp.log(totals[job])

    def mix(job):
        i, head = job
        own = values_t[i][head * HEAD_DIM : (head + 1) * HEAD_DIM]
        contexts[job] = nn(own, expos.pop(job)) * (1.0 / totals[job])

    stagger(jobs, [score, soften, mix], 3)
    for i in range(batch):
        context_t = jnp.concatenate([contexts[i, h] for h in range(HEADS)], axis=0).astype(bf16)
        ctx_ref[i] = context_t
        pad = [jnp.zeros((8 - HEADS, rows), f32)]
        lse_ref[i] = jnp.concatenate([stats[i, h] for h in range(HEADS)] + pad, axis=0)
        row = message_ref[pl.ds(step * batch + i, 1), :]
        base = put_row(pad_rows(video_ref[i].astype(f32), rows), tokens - 1, row)
        resid_ref[i] = base + tn(context_t, wo_ref[...])


def attend(normed, kv, video, message, nmsg, kvmsg, qkv, outw, tokens, after=()):
    count, rows, width = normed.shape
    slots = message.shape[0]
    batch = share_of(count, 2)
    return pl.pallas_call(
        functools.partial(attend_kernel, tokens),
        grid=(count // batch,),
        in_specs=[
            frames_block(batch, (rows, width)),
            frames_block(batch, (rows, 2 * width)),
            frames_block(batch, video.shape[1:]),
            full((slots, width)),
            full((slots, width)),
            full((slots, 2 * width)),
            square(width, 1, 0),
            square(width, 1, 2),
            square(width, 1),
        ]
        + [pl.BlockSpec(memory_space=pl.ANY)] * len(after),
        out_specs=[
            frames_block(batch, (rows, width)),
            frames_block(batch, (width, rows)),
            frames_block(batch, (8, rows)),
        ],
        out_shape=[
            shape_of((count, rows, width), f32),
            shape_of((count, width, rows), bf16),
            shape_of((count, 8, rows), f32),
        ],
        scratch_shapes=[pltpu.VMEM((width, width), bf16)] * 2,
        compiler_params=params(20),
        cost_estimate=cost(14e9, 10e6),
        name="attend",
    )(normed, kv, video, message, nmsg, kvmsg, qkv, qkv, outw, *after)


def caption_kernel(
    pieces, groups, clips, local, where_ref, lengths_ref, *refs
):
    gathered = refs[:pieces]
    caps_ref, cot_ref, qkv_ref, outw_ref, gains_ref = refs[pieces : pieces + 5]
    out_ref, grad_ref, gain_ref = refs[pieces + 5 : pieces + 8]
    part_refs = refs[pieces + 8 : pieces + 8 + pieces]
    keep_ref, send_ref, acc = refs[pieces + 8 + pieces :]
    width = caps_ref.shape[1]
    slots = gathered[0].shape[0]
    count = caps_ref.shape[0]
    keys_n = pieces * slots
    runs = lengths_ref.shape[1]

    token = lax.broadcasted_iota(jnp.int32, (count, keys_n), 0)
    key = lax.broadcasted_iota(jnp.int32, (count, keys_n), 1)
    slot = key % slots
    group = token // local
    position = token - group * local + where_ref[0] * local
    document = jnp.zeros((count, keys_n), jnp.int32)
    for m in range(groups):
        end = jnp.int32(0)
        for j in range(runs):
            end = end + lengths_ref[m, j]
            document = document + jnp.where((group == m) & (position >= end), 1, 0)
    allowed = slot == group * clips + document % clips
    valid = (document[:, 0:1] < runs - 1).astype(f32)

    pack = caps_ref[...].astype(f32)
    unit, inv = unit_norm(pack)
    gain = gains_ref[3:4, :]
    normed = (unit * gain).astype(bf16)
    visual = jnp.concatenate([g[...] for g in gathered], axis=0)
    queries = nn(normed, qkv_ref[0, 0]).astype(bf16)
    keys = nn(visual, qkv_ref[0, 1]).astype(bf16)
    values = nn(visual, qkv_ref[0, 2]).astype(bf16)

    masks = [head_mask((count, width), 1, h) for h in range(HEADS)]
    zero = jnp.zeros((count, width), bf16)

    def by_head(x):
        return jnp.concatenate([jnp.where(m, x, zero) for m in masks], axis=0)

    def merge(x):
        cut = [x[h * count : (h + 1) * count] for h in range(HEADS)]
        return functools.reduce(jnp.add, [jnp.where(m, c, 0.0) for m, c in zip(masks, cut)])

    allowed_all = jnp.concatenate([allowed.astype(jnp.int32)] * HEADS, axis=0) > 0
    split_q = by_head(queries)
    scores = jnp.where(allowed_all, nt(split_q, keys) * SCALE, MASKED)
    expo = jnp.exp(scores - jnp.max(scores, axis=1, keepdims=True))
    probs = expo / jnp.sum(expo, axis=1, keepdims=True)
    low = probs.astype(bf16)
    context = merge(nn(low, values)).astype(bf16)
    out_ref[...] = (pack + valid * nn(context, outw_ref[0])).astype(bf16)

    cot = cot_ref[...].astype(f32)
    branch = (cot * valid).astype(bf16)
    split_d = by_head(nt(branch, outw_ref[0]).astype(bf16))
    dvalues = tn(low, split_d)
    dprobs = nt(split_d, values)
    dscores = probs * (dprobs - jnp.sum(dprobs * probs, axis=1, keepdims=True))
    dscores = jnp.where(allowed_all, dscores, 0.0).astype(bf16)
    dqueries = (merge(nn(dscores, keys)) * SCALE).astype(bf16)
    dkeys = tn(dscores, split_q) * SCALE
    dnormed = nt(dqueries, qkv_ref[0, 0])
    grad_ref[...] = (cot + norm_back(unit, inv, gain, dnormed)).astype(bf16)
    gain_ref[...] = jnp.concatenate([row_sum(dnormed * unit), jnp.zeros((7, width), f32)], axis=0)
    low_k, low_v = dkeys.astype(bf16), dvalues.astype(bf16)
    part = nt(low_k, qkv_ref[0, 1]) + nt(low_v, qkv_ref[0, 2])
    for g in range(pieces):
        part_refs[g][...] = part[g * slots : (g + 1) * slots]
    if acc.shape[0] > 4 * width:
        acc[...] = jnp.zeros(acc.shape, f32)
    acc[0:width, :] = tn(normed, dqueries)
    acc[width : 2 * width, :] = tn(visual, low_k)
    acc[2 * width : 3 * width, :] = tn(visual, low_v)
    acc[3 * width : 4 * width, :] = tn(context, branch)
    emit(where_ref, acc, keep_ref, send_ref)


def captions_step(where, lengths, gathered, caps, cot, qkv, outw, gains, plan):
    count, width = caps.shape
    groups = lengths.shape[0]
    pieces = len(gathered)
    slots = gathered[0].shape[0]
    operands = list(gathered) + [caps, cot, qkv, outw, gains]
    acc_rows, packet_specs, packet_shapes = plan.packet(4 * width, width)
    return pl.pallas_call(
        functools.partial(caption_kernel, pieces, groups, plan.clips, count // groups),
        grid=(1,),
        in_specs=[scalars(), scalars()]
        + [full(x.shape) for x in operands[:-3]]
        + [
            pl.BlockSpec((1, 3, width, width), lambda i: (2, 0, 0, 0)),
            pl.BlockSpec((1, width, width), lambda i: (2, 0, 0)),
            full(gains.shape),
        ],
        out_specs=[full((count, width))] * 2
        + [full((8, width))]
        + [full((slots, width))] * pieces
        + packet_specs,
        out_shape=[shape_of((count, width), bf16)] * 2
        + [shape_of((8, width), f32)]
        + [shape_of((slots, width), f32)] * pieces
        + packet_shapes,
        scratch_shapes=[pltpu.VMEM((acc_rows, width), f32)],
        compiler_params=params(12),
        cost_estimate=cost(4e9, 8e6),
        name="captions_step",
    )(where, lengths, *operands)


def mlp_kernel(
    pieces, patch, ff, where_ref, resid_ref, cot_ref, final_ref, gains_ref, up_ref, down_ref, *refs
):
    parts = refs[:pieces]
    out_ref, dresid_ref, gain_ref, keep_ref, send_ref, acc, dcls = refs[-7:]
    step = pl.program_id(0)
    batch, rows, width = resid_ref.shape
    wide = acc.shape[1]
    blocks = ff // wide

    @pl.when(step == 0)
    def _():
        acc[...] = jnp.zeros(acc.shape, f32)
        dvisual = functools.reduce(jnp.add, [p[...] for p in parts])
        unit, inv = unit_norm(final_ref[...])
        dcls[...] = norm_back(unit, inv, gains_ref[2:3, :], dvisual)
        gain_ref[...] = jnp.concatenate(
            [jnp.zeros((1, width), f32), row_sum(dvisual * unit), jnp.zeros((6, width), f32)],
            axis=0,
        )

    resid = resid_ref[...].reshape(batch * rows, width)
    gain = gains_ref[1:2, :]
    unit, inv = unit_norm(resid)
    normed32 = unit * gain
    normed = normed32.astype(bf16)
    normed_t = normed32.T.astype(bf16)
    pieces_d = []
    for i in range(batch):
        one = pad_rows(cot_ref[i].astype(f32), rows)
        pieces_d.append(put_row(one, 0, one[0:1] + dcls[pl.ds(step * batch + i, 1), :]))
    dfinal = jnp.concatenate(pieces_d, axis=0)
    branch = dfinal.astype(bf16)
    branch_t = dfinal.T.astype(bf16)
    final = resid
    dnormed = jnp.zeros((batch * rows, width), f32)
    for c in range(blocks):
        span = slice(c * wide, (c + 1) * wide)
        hidden = nn(normed, up_ref[:, span])
        gate = sigmoid(1.702 * hidden)
        active = (hidden * gate).astype(bf16)
        final = final + nn(active, down_ref[span, :])
        dactive = nt(branch, down_ref[span, :])
        dhidden = (dactive * gate * (1.0 + 1.702 * hidden * (1.0 - gate))).astype(bf16)
        dnormed = dnormed + nt(dhidden, up_ref[:, span])
        acc[c * width : (c + 1) * width, :] += nn(normed_t, dhidden)
        acc[(blocks + c) * width : (blocks + c + 1) * width, :] += nn(branch_t, active)
    for i in range(batch):
        out_ref[i] = final[i * rows : i * rows + patch].astype(bf16)
    dresid = dfinal + norm_back(unit, inv, gain, dnormed)
    dresid_ref[...] = dresid.reshape(batch, rows, width)
    gain_ref[0:1, :] += row_sum(dnormed * unit)

    @pl.when(step == pl.num_programs(0) - 1)
    def _():
        emit(where_ref, acc, keep_ref, send_ref)


def mlp_step(where, resid, cot, final, gains, up, down, parts, plan, after=()):
    count, rows, width = resid.shape
    patch = cot.shape[1]
    ff = up.shape[1]
    slots = final.shape[0]
    batch = share_of(count, 2)
    wide = 2 * width
    acc_rows, packet_specs, packet_shapes = plan.packet(2 * ff * width // wide, wide)
    return pl.pallas_call(
        functools.partial(mlp_kernel, len(parts), patch, ff),
        grid=(count // batch,),
        in_specs=[
            scalars(),
            frames_block(batch, (rows, width)),
            frames_block(batch, (patch, width)),
            full((slots, width)),
            full(gains.shape),
            full(up.shape),
            full(down.shape),
        ]
        + [full((slots, width))] * len(parts)
        + [pl.BlockSpec(memory_space=pl.ANY)] * len(after),
        out_specs=[
            frames_block(batch, (patch, width)),
            frames_block(batch, (rows, width)),
            full((8, width)),
        ]
        + packet_specs,
        out_shape=[
            shape_of((count, patch, width), bf16),
            shape_of((count, rows, width), f32),
            shape_of((8, width), f32),
        ]
        + packet_shapes,
        scratch_shapes=[pltpu.VMEM((acc_rows, wide), f32), pltpu.VMEM((slots, width), f32)],
        compiler_params=params(36),
        cost_estimate=cost(20e9, 20e6),
        name="mlp_step",
    )(where, resid, cot, final, gains, up, down, *parts, *after)


def attend_back_kernel(tokens, first, last, waits, where_ref, normed_ref, kv_ref, *refs):
    (
        video_ref, message_ref, nmsg_ref, kvmsg_ref, ctx_ref, lse_ref, dresid_ref, gains_ref,
        wq_ref, wk_ref, wv_ref, wo_ref,
    ) = refs[:12]
    refs = refs[12:]
    if first:
        carried, refs = refs[1:5], refs[5:]
    refs = refs[waits:]
    outs = refs[: 6 if last else 5]
    grad_ref, dmsg_ref, dcls_ref, gain_ref = outs[:4]
    acc, wqt, wkt, wall = refs[len(outs) :]
    here = pl.program_id(0)
    step = here + first
    batch, rows, width = dresid_ref.shape
    patch = tokens - 1

    @pl.when(here == 0)
    def _():
        wqt[...] = wq_ref[...].T
        wkt[...] = wk_ref[...].T
        wall[:, 0:width] = wq_ref[...]
        wall[:, width : 2 * width] = wk_ref[...]
        wall[:, 2 * width : 3 * width] = wv_ref[...]
        for k, ref in enumerate((dmsg_ref, dcls_ref, gain_ref, acc)):
            ref[...] = carried[k][...] if first else jnp.zeros(ref.shape, f32)

    frames = range(batch)
    normed, kv = [], []
    for i in frames:
        normed.append(with_message(normed_ref[i], nmsg_ref, tokens, step * batch + i))
        kv.append(with_message(kv_ref[i], kvmsg_ref, tokens, step * batch + i))
    branch = [dresid_ref[i].astype(bf16) for i in frames]
    queries_t = [nt(wqt[...], n).astype(bf16) * jnp.bfloat16(SCALE) for n in normed]
    dcontext_t = [nt(wo_ref[...], b).astype(bf16) for b in branch]
    keys_t = [nt(wkt[...], n).astype(bf16) for n in normed]
    acc[3 * width : 4 * width, :] += functools.reduce(
        jnp.add, [nn(ctx_ref[i], branch[i]) for i in frames]
    )
    jobs = [(i, h) for i in frames for h in range(HEADS)]
    own = [slice(h * HEAD_DIM, (h + 1) * HEAD_DIM) for h in range(HEADS)]
    scores, dprobs, low, dscores, dq, dk, dv = {}, {}, {}, {}, {}, {}, {}

    def score(job):
        i, h = job
        scores[job] = nn(pair_lanes(kv[i], h), half_pair(queries_t[i], h))
        dprobs[job] = nn(pair_lanes(kv[i], HEADS + h), half_pair(dcontext_t[i], h))

    def soften(job):
        i, h = job
        probs = jnp.exp(masked_tail(scores.pop(job), tokens) - lse_ref[i, h : h + 1, :])
        low[job] = probs.astype(bf16)
        weighted = dprobs.pop(job) * probs
        dscores[job] = (weighted - probs * row_sum(weighted)).astype(bf16)

    def mix(job):
        i, h = job
        dq[job] = nn(keys_t[i][own[h]], dscores[job]) * SCALE
        dk[job] = nt(queries_t[i][own[h]], dscores.pop(job))
        dv[job] = nt(dcontext_t[i][own[h]], low.pop(job))

    stagger(jobs, [score, soften, mix], 2)
    dall = []
    for i in frames:
        parts = [d[i, h] for d in (dq, dk, dv) for h in range(HEADS)]
        dall.append(jnp.concatenate(parts, axis=0).astype(bf16))
    acc[0 : 3 * width, :] += functools.reduce(
        jnp.add, [nn(dall[i], normed[i]) for i in frames]
    )
    gain_sum = jnp.zeros((1, width), f32)
    for i in frames:
        dnormed = nn(wall[...], dall[i]).T
        at = pl.ds(step * batch + i, 1)
        base = put_row(pad_rows(video_ref[i].astype(f32), rows), tokens - 1, message_ref[at, :])
        unit, inv = unit_norm(base)
        dtokens = dresid_ref[i] + norm_back(unit, inv, gains_ref[0:1, :], dnormed)
        gain_sum = gain_sum + row_sum(dnormed * unit)
        grad_ref[i] = dtokens[:patch].astype(bf16)
        dcls_ref[at, :] = dtokens[0:1]
        dmsg_ref[at, :] = dtokens[patch : patch + 1]
    gain_ref[0:1, :] += gain_sum

    @pl.when(here == pl.num_programs(0) - 1)
    def _():
        if last:
            emit(where_ref, acc, *outs[4:])
        else:
            outs[4][...] = acc[...]


def attend_back(
    where, normed, kv, video, message, nmsg, kvmsg, ctx, lse, dresid, gains, qkv, outw, plan,
    batch, first, steps, carried=(), after=(),
):
    count, rows, width = normed.shape
    patch = video.shape[1]
    slots = message.shape[0]
    last = (first + steps) * batch == count
    acc_rows, packet_specs, packet_shapes = plan.packet(4 * width, width)
    if not last:
        packet_specs, packet_shapes = [full((acc_rows, width))], [shape_of((acc_rows, width), f32)]

    def block(shape):
        return pl.BlockSpec((batch,) + shape, lambda i, *_: (i + first, 0, 0))

    anywhere = pl.BlockSpec(memory_space=pl.ANY)
    carry_specs = [anywhere] + [full(x.shape) for x in carried[1:]] if carried else []
    return pl.pallas_call(
        functools.partial(attend_back_kernel, patch + 1, first, last, len(after)),
        grid=(steps,),
        in_specs=[
            scalars(),
            block((rows, width)),
            block((rows, 2 * width)),
            block((patch, width)),
            full((slots, width)),
            full((slots, width)),
            full((slots, 2 * width)),
            block((width, rows)),
            block((8, rows)),
            block((rows, width)),
            full(gains.shape),
            square(width, 1, 0),
            square(width, 1, 1),
            square(width, 1, 2),
            square(width, 1),
        ]
        + carry_specs
        + [anywhere] * len(after),
        out_specs=[block((patch, width))]
        + [full((slots, width))] * 2
        + [full((8, width))]
        + packet_specs,
        out_shape=[shape_of((count, patch, width), bf16)]
        + [shape_of((slots, width), f32)] * 2
        + [shape_of((8, width), f32)]
        + packet_shapes,
        input_output_aliases={15: 0} if carried else {},
        scratch_shapes=[
            pltpu.VMEM((acc_rows, width), f32),
            pltpu.VMEM((width, width), bf16),
            pltpu.VMEM((width, width), bf16),
            pltpu.VMEM((width, 3 * width), bf16),
        ],
        compiler_params=params(26),
        cost_estimate=cost(4.5e9 * steps, 4e6 * steps),
        name="attend_back",
    )(
        where, normed, kv, video, message, nmsg, kvmsg, ctx, lse, dresid, gains, qkv, qkv, qkv,
        outw, *carried, *after,
    )


class Groups:
    def __init__(self, layout, slots):
        self.segs, self.frames, self.clips = layout
        self.slots = slots
        self.groups = self.segs * self.clips
        self.together = max(1, min(self.groups, 512 // (self.frames * slots)))
        self.steps = self.groups // self.together
        self.rows = self.frames * self.together * slots
        per_group = self.frames * slots
        self.side = per_group * max(1, min(self.together, 128 // per_group))
        self.blocks = [slice(at, at + self.side) for at in range(0, self.rows, self.side)]
        self.jobs = [(i, h) for i in range(len(self.blocks)) for h in range(HEADS)]

    def row_of(self, s, f, c):
        group = s * self.clips + c
        step, inside = group // self.together, group % self.together
        return step, pl.multiple_of((inside * self.frames + f) * self.slots, 16)

    def every(self, where_ref):
        me_f, me_s, me_c = where_ref[0], where_ref[1], where_ref[2]
        for a in range(self.segs):
            for b in range(self.frames):
                for d in range(self.clips):
                    yield a, b, d, *self.row_of(me_s ^ a, me_f ^ b, me_c ^ d)

    def run(self, batch):
        def first(ref, at, value):
            ref[at] = value

        def again(ref, at, value):
            ref[at] += value

        batch(0, first)
        if self.steps > 1:
            pl.loop(1, self.steps)(lambda step: batch(step, again))


def join(groups, *parts):
    lanes = [
        jnp.concatenate([p[i, h] for p in parts for h in range(HEADS)], axis=0)
        for i in range(len(groups.blocks))
    ]
    return (jnp.concatenate(lanes, axis=1) if len(lanes) > 1 else lanes[0]).astype(bf16)


OWN = [slice(h * HEAD_DIM, (h + 1) * HEAD_DIM) for h in range(HEADS)]


def message_forward_kernel(groups, where_ref, *refs):
    side = refs[: groups.segs]
    (
        mw_ref, mg_ref, qkv_ref, classes_ref, start_ref, values_ref, qt_ref, kt_ref, probs_ref,
        ctx_ref, wqt, wkt, wvt,
    ) = refs[groups.segs :]
    for a, b, d, step, row in groups.every(where_ref):
        classes_ref[step, pl.ds(row, groups.slots), :] = side[a][d, b]
    wqt[...] = qkv_ref[0, 0].T
    wkt[...] = qkv_ref[0, 1].T
    wvt[...] = qkv_ref[0, 2].T
    edge = (groups.side, groups.side)
    key, query = lax.broadcasted_iota(jnp.int32, edge, 0), lax.broadcasted_iota(jnp.int32, edge, 1)
    per_group = groups.frames * groups.slots
    same = (key % groups.slots == query % groups.slots) & (key // per_group == query // per_group)

    def batch(step, put):
        del put
        start = nn(classes_ref[step], mw_ref[...]).astype(bf16)
        start_ref[step] = start
        unit, _ = unit_norm(start.astype(f32))
        normed = (unit * mg_ref[...]).astype(bf16)
        keys = nn(normed, qkv_ref[0, 1]).astype(bf16)
        values_ref[step] = nn(normed, qkv_ref[0, 2]).astype(bf16)
        queries_t = nt(wqt[...], normed).astype(bf16) * jnp.bfloat16(SCALE)
        values_t = nt(wvt[...], normed).astype(bf16)
        qt_ref[step] = queries_t
        kt_ref[step] = nt(wkt[...], normed).astype(bf16)
        scores, low, ctx = {}, {}, {}

        def score(job):
            i, h = job
            at = groups.blocks[i]
            scores[job] = nn(pair_lanes(keys[at], h), half_pair(queries_t[:, at], h))

        def soften(job):
            i, h = job
            one = jnp.where(same, scores.pop(job), MASKED)
            expo = jnp.exp(one - jnp.max(one, axis=0, keepdims=True))
            probs = expo * (1.0 / row_sum(expo))
            probs_ref[step, i * HEADS + h] = probs.astype(probs_ref.dtype)
            low[job] = probs.astype(bf16)

        def mix(job):
            i, h = job
            ctx[job] = nn(values_t[OWN[h], groups.blocks[i]], low.pop(job))

        stagger(groups.jobs, [score, soften, mix], 3)
        ctx_ref[step] = join(groups, ctx)

    groups.run(batch)


def message_forward(where, side, mw, mg, qkv, groups):
    width = mw.shape[0]
    rows, steps = groups.rows, groups.steps
    outs = [
        shape_of((steps, rows, width), bf16),
        shape_of((steps, rows, width), bf16),
        shape_of((steps, rows, width), bf16),
        shape_of((steps, width, rows), bf16),
        shape_of((steps, width, rows), bf16),
        shape_of((steps, len(groups.jobs), groups.side, groups.side), f32 if steps == 1 else bf16),
        shape_of((steps, width, rows), bf16),
    ]
    return pl.pallas_call(
        functools.partial(message_forward_kernel, groups),
        grid=(1,),
        in_specs=[scalars()]
        + [full(x.shape) for x in side]
        + [
            full(mw.shape),
            full(mg.shape),
            pl.BlockSpec((1, 3, width, width), lambda i: (0, 0, 0, 0)),
        ],
        out_specs=[full(x.shape) for x in outs],
        out_shape=outs,
        scratch_shapes=[pltpu.VMEM((width, width), bf16)] * 3,
        compiler_params=params(56),
        cost_estimate=cost(3e9, 6e6),
        name="message_forward",
    )(where, *side, mw, mg, qkv)


def message_back_kernel(layout, groups, where_ref, *refs):
    frame_part(layout, where_ref, *refs)
    message_part(groups, where_ref, *refs)


def frame_part(layout, where_ref, *refs):
    segs, frames, clips = layout
    pieces, refs = refs[: segs * frames], refs[segs * frames + 7 :]
    big_ref, out_ref, whole = refs[6], refs[7], refs[12]
    width = out_ref.shape[-1]
    chunk = whole.shape[0] // (segs * frames * clips)
    place(
        layout,
        where_ref,
        lambda a, b, d: pieces[a * frames + b][d * chunk : (d + 1) * chunk, :],
        whole,
        chunk,
    )
    for j in range(3):
        big_ref[1, j] = whole[j * width : (j + 1) * width, :].astype(f32).T
    out_ref[1] = whole[3 * width : 4 * width, :].astype(f32)


def message_part(groups, where_ref, *refs):
    count = groups.segs * groups.frames
    pieces, refs = refs[:count], refs[count:]
    classes_ref, start_ref, values_ref, qt_ref, kt_ref, probs_ref, ctx_ref = refs[:7]
    mw_ref, mg_ref, qkv_ref, outw_ref = refs[7:11]
    big_ref, out_ref, mwg_ref, gain_ref, gains_ref, dclass_ref, _, dmsgs, dstart, wall = refs[13:]
    width, slots = mw_ref.shape[0], groups.slots
    for a, b, d, step, row in groups.every(where_ref):
        piece = pieces[a * groups.frames + b]
        at = piece.shape[0] - (groups.clips - d) * slots
        dmsgs[step, pl.ds(row, slots), :] = piece[at : at + slots, :]
    gain_total = jnp.zeros((slots, width), f32)
    for i in range(groups.frames * groups.together):
        for step in range(groups.steps):
            gain_total += dmsgs[step, i * slots : (i + 1) * slots, :].astype(f32)
    gains_ref[...] = gain_total[slots - 4 : slots]
    for j in range(3):
        wall[:, j * width : (j + 1) * width] = qkv_ref[0, j]
    index = lax.broadcasted_iota(jnp.int32, (groups.rows, 1), 0) % slots
    my_step, my_row = groups.row_of(where_ref[1], where_ref[0], where_ref[2])

    def batch(step, put):
        dm = jnp.where(index < slots - 6, dmsgs[step].astype(f32), 0.0).astype(bf16)
        unit, inv = unit_norm(start_ref[step].astype(f32))
        normed = (unit * mg_ref[...]).astype(bf16)
        dcontext_t = nt(outw_ref[0], dm).astype(bf16)
        values, queries_t, keys_t = values_ref[step], qt_ref[step], kt_ref[step]
        dprobs, low, dscores, dq, dk, dv = {}, {}, {}, {}, {}, {}

        def score(job):
            i, h = job
            at = groups.blocks[i]
            dprobs[job] = nn(pair_lanes(values[at], h), half_pair(dcontext_t[:, at], h))

        def soften(job):
            i, h = job
            probs = probs_ref[step, i * HEADS + h].astype(f32)
            low[job] = probs.astype(bf16)
            weighted = dprobs.pop(job) * probs
            dscores[job] = (weighted - probs * row_sum(weighted)).astype(bf16)

        def mix(job):
            i, h = job
            at = groups.blocks[i]
            dq[job] = nn(keys_t[OWN[h], at], dscores[job]) * SCALE
            dk[job] = nt(queries_t[OWN[h], at], dscores.pop(job))
            dv[job] = nt(dcontext_t[OWN[h], at], low.pop(job))

        stagger(groups.jobs, [score, soften, mix], 2)
        put(out_ref, 0, nn(ctx_ref[step], dm))
        dall = join(groups, dq, dk, dv)
        grads = nn(dall, normed)
        for j in range(3):
            put(big_ref, (0, j), grads[j * width : (j + 1) * width].T)
        dnormed = nn(wall[...], dall).T
        put(gain_ref, ..., jnp.sum(dnormed * unit, axis=0))
        ds = norm_back(unit, inv, mg_ref[...], dnormed) + dm.astype(f32)
        dstart[...] = ds
        put(mwg_ref, ..., tn(classes_ref[step], ds.astype(bf16)))

        @pl.when(my_step == step)
        def _():
            dclass_ref[...] = nt(dstart[pl.ds(my_row, slots), :].astype(bf16), mw_ref[...])

    groups.run(batch)


def message_back(where, pieces, forward, mw, mg, qkv, outw, big, out, layout, groups):
    width = mw.shape[0]
    operands = list(pieces) + list(forward) + [mw, mg]
    chunk = pieces[0].shape[0] // groups.clips - groups.slots
    return pl.pallas_call(
        functools.partial(message_back_kernel, layout, groups),
        grid=(1,),
        in_specs=[scalars()]
        + [full(x.shape) for x in operands]
        + [
            pl.BlockSpec((1, 3, width, width), lambda i: (0, 0, 0, 0)),
            pl.BlockSpec((1, width, width), lambda i: (0, 0, 0)),
            pl.BlockSpec(memory_space=pl.ANY),
            pl.BlockSpec(memory_space=pl.ANY),
        ],
        out_specs=[
            pl.BlockSpec((2, 3, width, width), lambda i: (0, 0, 0, 0)),
            pl.BlockSpec((2, width, width), lambda i: (0, 0, 0)),
            full((width, width)),
            full((width,)),
            full((4, width)),
            full((groups.slots, width)),
        ],
        out_shape=[
            shape_of((3, 3, width, width), f32),
            shape_of((3, width, width), f32),
            shape_of((width, width), f32),
            shape_of((width,), f32),
            shape_of((4, width), f32),
            shape_of((groups.slots, width), f32),
        ],
        input_output_aliases={len(operands) + 3: 0, len(operands) + 4: 1},
        scratch_shapes=[
            pltpu.VMEM((groups.groups * groups.frames * chunk, width), bf16),
            pltpu.VMEM((groups.steps, groups.rows, width), bf16),
            pltpu.VMEM((groups.rows, width), f32),
            pltpu.VMEM((width, 3 * width), bf16),
        ],
        compiler_params=params(30 if groups.steps == 1 else 60),
        cost_estimate=cost(4e9, 12e6),
        name="message_back",
    )(where, *operands, qkv, outw, big, out)


def emit(where_ref, acc, keep_ref, send_ref):
    frames, clips, chunk = keep_ref.shape[:3]
    me_f, me_s = where_ref[0], where_ref[1]
    for a, out in enumerate((keep_ref, send_ref)):
        for b in range(frames):
            for d in range(clips):
                to = ((me_s ^ a) * frames + (me_f ^ b)) * clips + d
                at = pl.multiple_of(to * chunk, 16)
                out[b, d] = acc[pl.ds(at, chunk), :].astype(bf16)


class Plan:
    def __init__(self, clips):
        self.clips = clips
        self.segs = lax.axis_size("seg")
        self.frames = lax.axis_size("frame")
        self.rings = lax.axis_size("clip")
        self.layout = (self.segs, self.frames, self.rings)
        self.devices = self.segs * self.frames * self.rings

    def chunk(self, rows):
        share = -(-rows // self.devices)
        return -(-share // 16) * 16

    def packet(self, rows, width):
        chunk = self.chunk(rows)
        shape = (self.frames, self.rings, chunk, width)
        return chunk * self.devices, [full(shape)] * 2, [shape_of(shape, bf16)] * 2


def swap(x, axis, k):
    count = lax.axis_size(axis)
    return lax.ppermute(x, axis, [(i, i ^ k) for i in range(count)])


def behind(x, *others):
    return lax.optimization_barrier((x, others))[0]


class Sum:
    def __init__(self, arrays, views=None):
        self.arrays = list(arrays)
        self.views = list(views or [()] * len(self.arrays))

    def part(self, view):
        return Sum(self.arrays, [v + (view,) for v in self.views])

    def plus(self, *arrays):
        return Sum(self.arrays + list(arrays), self.views + [()] * len(arrays))

    def value(self):
        terms = []
        for x, views in zip(self.arrays, self.views):
            for view in views:
                x = view(x)
            terms.append(x.astype(f32))
        return functools.reduce(jnp.add, terms).astype(bf16)


jax.tree_util.register_pytree_node(
    Sum, lambda s: (s.arrays, s.views), lambda views, arrays: Sum(arrays, views)
)


def at(k):
    return lambda x: x[k]


def total(one, two):
    return (one.astype(f32) + two.astype(f32)).astype(bf16)


def reduce_seg(keep, send):
    return Sum([keep, swap(send, "seg", 1)])


def frame_sends(terms):
    return [terms.part(at(b)).value() for b in range(1, lax.axis_size("frame"))]


def reduce_frame(terms, sends):
    return terms.part(at(0)).plus(*[swap(x, "frame", b + 1) for b, x in enumerate(sends)])


def clip_bits():
    count = lax.axis_size("clip")
    return [1 << j for j in range(count.bit_length() - 1)]


def swap_two(one, two, axis, k):
    width = one.shape[-1]
    rows = one.size // width
    got = swap(jnp.concatenate([one.reshape(-1, width), two.reshape(-1, width)]), axis, k)
    return got[:rows].reshape(one.shape), got[rows:].reshape(two.shape)


def exchange(part, rows, bit):
    got, got_rows = swap_two(part, rows, "clip", bit)
    return total(part, got), jnp.concatenate([rows, got_rows])


def gather_frame(held):
    return [held] + [swap(held, "frame", b) for b in range(1, lax.axis_size("frame"))]


def gather_seg(held):
    return held + [swap(h, "seg", 1) for h in held]


def place(layout, where_ref, piece, whole, chunk):
    segs, frames, clips = layout
    me_f, me_s = where_ref[0], where_ref[1]
    for a in range(segs):
        for b in range(frames):
            for d in range(clips):
                of = ((me_s ^ a) * frames + (me_f ^ b)) * clips + d
                whole[pl.ds(pl.multiple_of(of * chunk, 16), chunk), :] = piece(a, b, d)


def unpack_kernel(layout, where_ref, *refs):
    segs, frames, clips = layout
    main = refs[:segs]
    up_ref, down_ref, whole = refs[segs:]
    width, ff = up_ref.shape
    wide = whole.shape[1]
    place(layout, where_ref, lambda a, b, d: main[a][b * clips + d], whole, main[0].shape[1])
    blocks = ff // wide
    for c in range(blocks):
        span = slice(c * wide, (c + 1) * wide)
        up_ref[:, span] = whole[c * width : (c + 1) * width, :].astype(f32)
        other = whole[(blocks + c) * width : (blocks + c + 1) * width, :]
        down_ref[span, :] = other.astype(f32).T


def unpack(where, main, width, ff, plan):
    chunk, wide = main[0].shape[1:]
    return pl.pallas_call(
        functools.partial(unpack_kernel, plan.layout),
        grid=(1,),
        in_specs=[scalars()] + [full(x.shape) for x in main],
        out_specs=[full((width, ff)), full((ff, width))],
        out_shape=[shape_of((width, ff), f32), shape_of((ff, width), f32)],
        scratch_shapes=[pltpu.VMEM((plan.devices * chunk, wide), bf16)],
        compiler_params=params(40),
        cost_estimate=cost(2e9, 10e6),
        name="unpack",
    )(where, *main)


def unpack_side_kernel(layout, where_ref, *refs):
    segs = layout[0]
    side = refs[:segs]
    big_ref, out_ref, whole = refs[segs:]
    width = out_ref.shape[-1]
    place(layout, where_ref, lambda a, b, d: side[a][b, d], whole, side[0].shape[2])
    for j in range(3):
        big_ref[0, j] = whole[j * width : (j + 1) * width, :].astype(f32)
    out_ref[0] = whole[3 * width : 4 * width, :].astype(f32)


def unpack_side(where, side, plan):
    rows, width = side[0].shape[2:]
    return pl.pallas_call(
        functools.partial(unpack_side_kernel, plan.layout),
        grid=(1,),
        in_specs=[scalars()] + [full(x.shape) for x in side],
        out_specs=[
            pl.BlockSpec((1, 3, width, width), lambda i: (2, 0, 0, 0)),
            pl.BlockSpec((1, width, width), lambda i: (2, 0, 0)),
        ],
        out_shape=[shape_of((3, 3, width, width), f32), shape_of((3, width, width), f32)],
        scratch_shapes=[pltpu.VMEM((plan.devices * rows, width), bf16)],
        compiler_params=params(30),
        cost_estimate=cost(1e9, 4e6),
        name="unpack_side",
    )(where, *side)


def last_rows_kernel(gain_a, gain_b, gain_c, dmsg_ref, out_ref):
    slots, width = dmsg_ref.shape
    rows = [
        dmsg_ref[0 : slots - 6, :],
        jnp.zeros((2, width), f32),
        gain_a[0:1, :],
        gain_b[0:1, :],
        gain_b[1:2, :],
        gain_c[0:1, :],
    ]
    out_ref[...] = jnp.concatenate(rows, axis=0).astype(bf16)


def last_rows(gain_a, gain_b, gain_c, dmsg):
    return pl.pallas_call(
        last_rows_kernel,
        out_shape=shape_of(dmsg.shape, bf16),
        name="last_rows",
    )(gain_a, gain_b, gain_c, dmsg)


def local(
    video, captions, caption_lengths, message_weight, message_gain, qkv_weights, out_weights,
    mlp_up, mlp_down, gains, video_cot, caption_cot,
):
    micro, clips, per_frame, patch, width = video.shape
    count = micro * clips * per_frame
    ff = mlp_up.shape[1]
    plan = Plan(clips)
    tokens = patch + 1
    rows = -(-tokens // 16) * 16
    slots = -(-(count + 6) // 16) * 16
    where = jnp.stack(
        [lax.axis_index("frame"), lax.axis_index("seg"), lax.axis_index("clip")]
    ).astype(jnp.int32)
    frames = video.reshape(count, patch, width)
    cots = video_cot.reshape(count, patch, width)
    caps = captions.reshape(-1, width)
    cap_cots = caption_cot.reshape(-1, width)
    lengths = caption_lengths.reshape(micro, -1)
    gain = message_gain.reshape(1, width)

    classes = class_rows(video, slots)
    gathered = gather_frame(classes)
    normed, kv = norm_tokens(frames, gains, qkv_weights, rows)
    message, nmsg, kvmsg, visual, final = first_rows(
        gathered, message_weight, gain, qkv_weights, out_weights, mlp_up, mlp_down, gains,
        kv, tokens,
    )
    visuals = gather_frame(visual)
    results = captions_step(
        where, lengths, visuals, caps, cap_cots, qkv_weights, out_weights, gains, plan
    )
    caption_out, caption_grad, gain_c = results[:3]
    parts = list(results[3:-2])
    parts = [parts[0]] + [swap(parts[b], "frame", b) for b in range(1, plan.frames)]
    bits = clip_bits()
    rows_all = jnp.stack(gathered)[None]
    side = reduce_seg(*results[-2:])
    side = behind(side, results[3])
    sends = frame_sends(side)
    resid, ctx, lse = attend(
        normed, kv, frames, message, nmsg, kvmsg, qkv_weights, out_weights, tokens, sends
    )
    side = reduce_frame(side, sends)
    parts, resid, side = behind((parts, resid, side))
    side = side.value()
    side, resid = behind((side, resid))
    video_out, dresid, gain_b, keep, send = mlp_step(
        where, resid, cots, final, gains, mlp_up, mlp_down, parts, plan
    )
    for bit in bits[:-1]:
        side, rows_all = exchange(side, rows_all, bit)
    side, rows_all, video_out, dresid, keep, send = behind(
        (side, rows_all, video_out, dresid, keep, send)
    )
    main = reduce_seg(keep, send)
    turned = video_out.reshape(video.shape).transpose(1, 2, 3, 0, 4)
    main, dresid, turned = behind((main, dresid, turned))
    video_out = turned.transpose(3, 0, 1, 2, 4)
    sends = frame_sends(main)
    sends, dresid, side, rows_all = behind((sends, dresid, side, rows_all))
    batch = share_of(count, 2)
    steps = count // batch
    late_steps = 2
    back = functools.partial(
        attend_back, where, normed, kv, frames, message, nmsg, kvmsg, ctx, lse, dresid, gains,
        qkv_weights, out_weights, plan, batch,
    )
    carried = back(0, steps - late_steps)
    main = reduce_frame(main, sends)
    side, rows_all = exchange(side, rows_all, bits[-1])
    carried, main, side, rows_all = behind((carried, main, side, rows_all))
    main = main.value()
    main, carried, side = behind((main, carried, side))
    for bit in bits[:-1]:
        main = total(main, swap(main, "clip", bit))
    side = gather_frame(side)
    grad, dmsg, dcls, gain_a, keep, send = back(steps - late_steps, late_steps, carried)
    main, side, keep, send, gain_a, dmsg = behind((main, side, keep, send, gain_a, dmsg))

    main = total(main, swap(main, "clip", bits[-1]))
    late = reduce_seg(keep, send)
    rest = last_rows(gain_a, gain_b, gain_c, dmsg)
    side = jnp.stack(side)
    other, other_rows = swap_two(side, rows_all, "seg", 1)
    late, rest = behind((late, rest))
    late = reduce_frame(late, frame_sends(late))
    main, late, other, other_rows = behind((main, late, other, other_rows))

    held = gather_frame(main)
    late, rest = late.value(), rest[None]
    for bit in bits:
        late, rest = exchange(late, rest, bit)
    big, out = unpack_side(where, [side, other], plan)
    groups = Groups(plan.layout, slots)
    forward = message_forward(
        where, [rows_all, other_rows], message_weight, gain, qkv_weights, groups
    )
    held, late, rest, big, forward = behind((held, late, rest, big, forward))

    late = gather_frame(jnp.concatenate([late.reshape(-1, width), rest.reshape(-1, width)]))
    held = gather_seg([jnp.concatenate(held, axis=0)])
    up_grad, down_grad = unpack(where, held, width, ff, plan)
    late, up_grad = behind((late, up_grad))

    late = gather_seg(late)
    big, out, mw_grad, mg_grad, gains_grad, dclass = message_back(
        where, late, forward, message_weight, gain, qkv_weights, out_weights, big, out,
        plan.layout, groups,
    )
    fixed = (dclass + dcls)[:count].astype(bf16).reshape(micro, clips, per_frame, 1, width)
    grad = lax.dynamic_update_slice(grad.reshape(video.shape), fixed, (0, 0, 0, 0, 0))
    return (
        video_out.reshape(video.shape),
        caption_out.reshape(captions.shape),
        grad,
        caption_grad.reshape(captions.shape),
        mw_grad,
        mg_grad,
        big,
        out,
        up_grad,
        down_grad,
        gains_grad,
    )


def solution(mesh):
    rows = P(None, ("clip", "seg"), "frame", None, None)
    caps = P(None, ("clip", "seg"), "frame", None)
    return jax.shard_map(
        local,
        mesh=mesh,
        in_specs=(rows, caps, P(None, ("clip", "seg"), None)) + (P(),) * 7 + (rows, caps),
        out_specs=(rows, caps, rows, caps) + (P(),) * 7,
        check_vma=False,
    )
```

```python
import functools

import jax
import jax.numpy as jnp
from jax import lax
from jax.experimental import pallas as pl
from jax.experimental.pallas import tpu as pltpu
from jax.sharding import PartitionSpec as P

HEADS = 6
HEAD_DIM = 64
EPS = 1e-05
SCALE = 0.125
MASKED = -1e30

f32 = jnp.float32
bf16 = jnp.bfloat16


def nn(a, b):
    return lax.dot_general(a, b, (((1,), (0,)), ((), ())), preferred_element_type=f32)


def nt(a, b):
    return lax.dot_general(a, b, (((1,), (1,)), ((), ())), preferred_element_type=f32)


def tn(a, b):
    return lax.dot_general(a, b, (((0,), (0,)), ((), ())), preferred_element_type=f32)


def exact(a, b):
    return lax.dot_general(
        a, b, (((1,), (0,)), ((), ())), precision=lax.Precision.HIGHEST, preferred_element_type=f32
    )


def unit_norm(x):
    center = x - jnp.mean(x, axis=-1, keepdims=True)
    inv = lax.rsqrt(jnp.mean(center * center, axis=-1, keepdims=True) + EPS)
    return center * inv, inv


def norm_back(unit, inv, gain, dy):
    du = dy * gain
    mean_du = jnp.mean(du, axis=-1, keepdims=True)
    mean_dot = jnp.mean(du * unit, axis=-1, keepdims=True)
    return inv * (du - mean_du - unit * mean_dot)


def row_sum(x):
    return jnp.sum(x, axis=0, keepdims=True)


def sigmoid(x):
    return 0.5 + 0.5 * jnp.tanh(0.5 * x)


def head_mask(shape, lane_dim, head):
    lane = lax.broadcasted_iota(jnp.int32, shape, lane_dim)
    return (lane >= head * HEAD_DIM) & (lane < (head + 1) * HEAD_DIM)


def head_columns(width):
    lane = lax.broadcasted_iota(jnp.int32, (width, 128), 0)
    col = lax.broadcasted_iota(jnp.int32, (width, 128), 1)
    return ((lane >= col * HEAD_DIM) & (lane < (col + 1) * HEAD_DIM)).astype(f32)


def head_rows(width):
    col = lax.broadcasted_iota(jnp.int32, (128, width), 0)
    lane = lax.broadcasted_iota(jnp.int32, (128, width), 1)
    return ((lane >= col * HEAD_DIM) & (lane < (col + 1) * HEAD_DIM)).astype(f32)


def pad_rows(x, rows):
    if x.shape[0] == rows:
        return x
    return jnp.concatenate([x, jnp.zeros((rows - x.shape[0], x.shape[1]), x.dtype)], axis=0)


def put_row(block, at, row):
    top = at // 16 * 16
    tail = block[top : top + 16]
    index = lax.broadcasted_iota(jnp.int32, tail.shape, 0)
    tail = jnp.where(index == at - top, row, tail)
    pieces = [tail]
    if top:
        pieces.insert(0, block[:top])
    if top + 16 < block.shape[0]:
        pieces.append(block[top + 16 :])
    return jnp.concatenate(pieces, axis=0) if len(pieces) > 1 else tail


def full(shape):
    return pl.BlockSpec(shape, lambda *_: (0,) * len(shape))


def frame_block(shape):
    return pl.BlockSpec((1,) + shape, lambda i, *_: (i, 0, 0))


def frames_block(batch, shape):
    return pl.BlockSpec((batch,) + shape, lambda i, *_: (i, 0, 0))


def stagger(jobs, stages, gap):
    for at in range(len(jobs) + (len(stages) - 1) * gap):
        for k, stage in enumerate(stages):
            j = at - k * gap
            if 0 <= j < len(jobs):
                stage(jobs[j])


def share_of(count, most):
    return max(b for b in range(1, most + 1) if count % b == 0)


def square(width, *at):
    return pl.BlockSpec((None,) * len(at) + (width, width), lambda *_: at + (0, 0))


def scalars():
    return pl.BlockSpec(memory_space=pltpu.SMEM)


def shape_of(shape, dtype):
    return jax.ShapeDtypeStruct(shape, dtype)


def params(mib):
    return pltpu.CompilerParams(vmem_limit_bytes=mib * 1024 * 1024)


def cost(flops, nbytes):
    return pl.CostEstimate(flops=int(flops), bytes_accessed=int(nbytes), transcendentals=0)


def class_kernel(video_ref, out_ref):
    clips, _, micro, width = video_ref.shape
    rows = [video_ref[c, 0, m : m + 1, :].astype(f32) for m in range(micro) for c in range(clips)]
    out_ref[...] = pad_rows(jnp.concatenate(rows, axis=0), out_ref.shape[0]).astype(bf16)


def class_rows(video, slots):
    micro, clips, per_frame, patch, width = video.shape
    turned = video.transpose(1, 2, 3, 0, 4).reshape(clips * per_frame, patch, micro, width)
    return pl.pallas_call(
        class_kernel,
        grid=(1,),
        in_specs=[pl.BlockSpec((clips * per_frame, 1, micro, width), lambda i: (0, 0, 0, 0))],
        out_specs=full((slots, width)),
        out_shape=shape_of((slots, width), bf16),
        name="class_rows",
    )(turned)


def norm_kernel(video_ref, gains_ref, wk_ref, wv_ref, normed_ref, kv_ref, wkv):
    batch, rows, width = normed_ref.shape

    @pl.when(pl.program_id(0) == 0)
    def _():
        wkv[:, :width] = wk_ref[...]
        wkv[:, width:] = wv_ref[...]

    parts = []
    for i in range(batch):
        unit, _ = unit_norm(video_ref[i].astype(f32))
        parts.append(pad_rows(unit * gains_ref[0:1, :], rows).astype(bf16))
        normed_ref[i] = parts[i]
    normed = jnp.concatenate(parts, axis=0)
    kv_ref[...] = nn(normed, wkv[...]).astype(bf16).reshape(batch, rows, 2 * width)


def norm_tokens(video, gains, qkv, rows):
    count, patch, width = video.shape
    batch = share_of(count, 5)
    return pl.pallas_call(
        norm_kernel,
        grid=(count // batch,),
        in_specs=[
            frames_block(batch, (patch, width)),
            full(gains.shape),
            square(width, 1, 1),
            square(width, 1, 2),
        ],
        out_specs=[
            frames_block(batch, (rows, width)),
            frames_block(batch, (rows, 2 * width)),
        ],
        out_shape=[
            shape_of((count, rows, width), bf16),
            shape_of((count, rows, 2 * width), bf16),
        ],
        scratch_shapes=[pltpu.VMEM((width, 2 * width), bf16)],
        compiler_params=params(20),
        cost_estimate=cost(4 * count * rows * width * width, 8 * count * rows * width),
        name="norm_tokens",
    )(video, gains, qkv, qkv)


def message_scores(query, keys, columns):
    return [exact(query.astype(f32) * key.astype(f32), columns) * SCALE for key in keys]


def message_probs(scores):
    top = functools.reduce(jnp.maximum, scores)
    expo = [jnp.exp(score - top) for score in scores]
    total = functools.reduce(jnp.add, expo)
    return [e / total for e in expo]


def first_kernel(
    pieces, count, tokens, *refs
):
    gathered = refs[:pieces]
    (
        mw_ref, mg_ref, qkv_ref, outw_ref, up_ref, down_ref, gains_ref, kv_ref,
        message_ref, nmsg_ref, kvmsg_ref, visual_ref, final_ref, ctx,
    ) = refs[pieces:]
    width = mw_ref.shape[0]
    slots = gathered[0].shape[0]
    rows = kv_ref.shape[1]
    classes = jnp.concatenate([g[...] for g in gathered], axis=0)
    start = nn(classes, mw_ref[...]).astype(bf16)
    unit, _ = unit_norm(start.astype(f32))
    normed = (unit * mg_ref[...]).astype(bf16)
    keys = nn(normed, qkv_ref[0, 1]).astype(bf16)
    values = nn(normed, qkv_ref[0, 2]).astype(bf16)
    query = nn(normed[:slots], qkv_ref[0, 0]).astype(bf16)
    columns, spread = head_columns(width), head_rows(width).astype(bf16)
    cut = [slice(g * slots, (g + 1) * slots) for g in range(pieces)]
    probs = message_probs(message_scores(query, [keys[c] for c in cut], columns))
    context = functools.reduce(
        jnp.add,
        [nn(p.astype(bf16), spread) * values[c].astype(f32) for p, c in zip(probs, cut)],
    ).astype(bf16)
    message = start[:slots].astype(f32) + nn(context, outw_ref[0])
    message_ref[...] = message
    unit, _ = unit_norm(message)
    nmsg = (unit * gains_ref[0:1, :]).astype(bf16)
    nmsg_ref[...] = nmsg.astype(f32)
    kmsg = nn(nmsg, qkv_ref[1, 1]).astype(bf16).astype(f32)
    vmsg = nn(nmsg, qkv_ref[1, 2]).astype(bf16).astype(f32)

    own = gathered[0][...].astype(f32)
    unit, _ = unit_norm(own)
    qcls = nn((unit * gains_ref[0:1, :]).astype(bf16), qkv_ref[1, 0]).astype(bf16).astype(f32) * SCALE
    head = lax.broadcasted_iota(jnp.int32, (16, width), 0)
    lane = lax.broadcasted_iota(jnp.int32, (16, width), 1)
    mine = (lane >= head * HEAD_DIM) & (lane < (head + 1) * HEAD_DIM)
    token = lax.broadcasted_iota(jnp.int32, (16, rows), 1)
    ctx[...] = jnp.zeros(ctx.shape, f32)
    kvmsg_ref[:, :width] = kmsg
    kvmsg_ref[:, width:] = vmsg
    queries = [jnp.where(mine, qcls[i : i + 1], 0.0) for i in range(count)]
    scores = [nt(queries[i].astype(bf16), kv_ref[i, :, :width]) for i in range(count)]
    probs = []
    for i in range(count):
        last = jnp.sum(queries[i] * kmsg[i : i + 1], axis=1, keepdims=True)
        score = jnp.where(token == tokens - 1, last, scores[i])
        score = jnp.where(token < tokens, score, MASKED)
        expo = jnp.exp(score - jnp.max(score, axis=1, keepdims=True))
        probs.append((expo / jnp.sum(expo, axis=1, keepdims=True)).astype(bf16))
    outs = [nn(probs[i], kv_ref[i, :, width:]) for i in range(count)]
    for i in range(count):
        extra = jnp.sum(
            jnp.where(token == tokens - 1, probs[i].astype(f32), 0.0), axis=1, keepdims=True
        )
        out = outs[i] + extra * vmsg[i : i + 1]
        ctx[i : i + 1, :] = row_sum(jnp.where(mine, out, 0.0))
    resid = own + nn(ctx[...].astype(bf16), outw_ref[1])
    unit, _ = unit_norm(resid)
    hidden = nn((unit * gains_ref[1:2, :]).astype(bf16), up_ref[...])
    active = (hidden * sigmoid(1.702 * hidden)).astype(bf16)
    final = resid + nn(active, down_ref[...])
    final_ref[...] = final
    unit, _ = unit_norm(final)
    visual_ref[...] = (unit * gains_ref[2:3, :]).astype(bf16)


def first_rows(gathered, mw, mg, qkv, outw, up, down, gains, kv, tokens):
    count, width = kv.shape[0], mw.shape[0]
    slots = gathered[0].shape[0]
    operands = list(gathered) + [mw, mg, qkv, outw, up, down, gains, kv]
    return pl.pallas_call(
        functools.partial(first_kernel, len(gathered), count, tokens),
        grid=(1,),
        in_specs=[full(x.shape) for x in gathered]
        + [
            full(mw.shape),
            full(mg.shape),
            pl.BlockSpec((2, 3, width, width), lambda i: (0, 0, 0, 0)),
            pl.BlockSpec((2, width, width), lambda i: (0, 0, 0)),
            full(up.shape),
            full(down.shape),
            full(gains.shape),
            full(kv.shape),
        ],
        out_specs=[full((slots, width))] * 2 + [full((slots, 2 * width))] + [full((slots, width))] * 2,
        out_shape=[
            shape_of((slots, width), f32),
            shape_of((slots, width), f32),
            shape_of((slots, 2 * width), f32),
            shape_of((slots, width), bf16),
            shape_of((slots, width), f32),
        ],
        scratch_shapes=[pltpu.VMEM((slots, width), f32)],
        compiler_params=params(56),
        cost_estimate=cost(4e9, 12e6),
        name="first_rows",
    )(*operands)


def with_message(block, rows_ref, tokens, frame):
    top = (tokens - 1) // 16 * 16
    tail = block[top : top + 16].astype(f32)
    index = lax.broadcasted_iota(jnp.int32, tail.shape, 0)
    tail = jnp.where(index == tokens - 1 - top, rows_ref[pl.ds(frame, 1), :], tail).astype(bf16)
    pieces = [block[:top], tail]
    if top + 16 < block.shape[0]:
        pieces.append(block[top + 16 :])
    return jnp.concatenate(pieces, axis=0)


def masked_tail(scores, tokens):
    top = tokens // 16 * 16
    if top >= scores.shape[0]:
        return scores
    tail = scores[top:]
    index = lax.broadcasted_iota(jnp.int32, tail.shape, 0)
    return jnp.concatenate([scores[:top], jnp.where(index < tokens - top, tail, MASKED)], axis=0)


def half_pair(block_t, head):
    own = block_t[head * HEAD_DIM : (head + 1) * HEAD_DIM]
    none = jnp.zeros(own.shape, own.dtype)
    return jnp.concatenate([own, none] if head % 2 == 0 else [none, own], axis=0)


def pair_lanes(block, head):
    at = head // 2 * 2 * HEAD_DIM
    return block[:, at : at + 2 * HEAD_DIM]


def attend_kernel(
    tokens, normed_ref, kv_ref, video_ref, message_ref, nmsg_ref, kvmsg_ref, wq_ref, wv_ref, wo_ref,
    *refs,
):
    resid_ref, ctx_ref, lse_ref, wqt, wvt = refs[-5:]
    step = pl.program_id(0)

    @pl.when(step == 0)
    def _():
        wqt[...] = wq_ref[...].T
        wvt[...] = wv_ref[...].T

    batch, rows, width = normed_ref.shape
    normed, keys = [], []
    for i in range(batch):
        frame = step * batch + i
        normed.append(with_message(normed_ref[i], nmsg_ref, tokens, frame))
        keys.append(with_message(kv_ref[i], kvmsg_ref, tokens, frame))
    queries_t = [nt(wqt[...], n).astype(bf16) * jnp.bfloat16(SCALE) for n in normed]
    values_t = [nt(wvt[...], n).astype(bf16) for n in normed]
    jobs = [(i, h) for i in range(batch) for h in range(HEADS)]
    contexts, stats, scores, expos, totals = {}, {}, {}, {}, {}

    def score(job):
        i, head = job
        scores[job] = nn(pair_lanes(keys[i], head), half_pair(queries_t[i], head))

    def soften(job):
        one = masked_tail(scores.pop(job), tokens)
        top = jnp.max(one, axis=0, keepdims=True)
        expo = jnp.exp(one - top)
        totals[job] = row_sum(expo)
        expos[job] = expo.astype(bf16)
        stats[job] = top + jnp.log(totals[job])

    def mix(job):
        i, head = job
        own = values_t[i][head * HEAD_DIM : (head + 1) * HEAD_DIM]
        contexts[job] = nn(own, expos.pop(job)) * (1.0 / totals[job])

    stagger(jobs, [score, soften, mix], 3)
    for i in range(batch):
        context_t = jnp.concatenate([contexts[i, h] for h in range(HEADS)], axis=0).astype(bf16)
        ctx_ref[i] = context_t
        pad = [jnp.zeros((8 - HEADS, rows), f32)]
        lse_ref[i] = jnp.concatenate([stats[i, h] for h in range(HEADS)] + pad, axis=0)
        row = message_ref[pl.ds(step * batch + i, 1), :]
        base = put_row(pad_rows(video_ref[i].astype(f32), rows), tokens - 1, row)
        resid_ref[i] = base + tn(context_t, wo_ref[...])


def attend(normed, kv, video, message, nmsg, kvmsg, qkv, outw, tokens, after=()):
    count, rows, width = normed.shape
    slots = message.shape[0]
    batch = share_of(count, 2)
    return pl.pallas_call(
        functools.partial(attend_kernel, tokens),
        grid=(count // batch,),
        in_specs=[
            frames_block(batch, (rows, width)),
            frames_block(batch, (rows, 2 * width)),
            frames_block(batch, video.shape[1:]),
            full((slots, width)),
            full((slots, width)),
            full((slots, 2 * width)),
            square(width, 1, 0),
            square(width, 1, 2),
            square(width, 1),
        ]
        + [pl.BlockSpec(memory_space=pl.ANY)] * len(after),
        out_specs=[
            frames_block(batch, (rows, width)),
            frames_block(batch, (width, rows)),
            frames_block(batch, (8, rows)),
        ],
        out_shape=[
            shape_of((count, rows, width), f32),
            shape_of((count, width, rows), bf16),
            shape_of((count, 8, rows), f32),
        ],
        scratch_shapes=[pltpu.VMEM((width, width), bf16)] * 2,
        compiler_params=params(20),
        cost_estimate=cost(14e9, 10e6),
        name="attend",
    )(normed, kv, video, message, nmsg, kvmsg, qkv, qkv, outw, *after)


def caption_kernel(
    pieces, groups, clips, local, where_ref, lengths_ref, *refs
):
    gathered = refs[:pieces]
    caps_ref, cot_ref, qkv_ref, outw_ref, gains_ref = refs[pieces : pieces + 5]
    out_ref, grad_ref, gain_ref = refs[pieces + 5 : pieces + 8]
    part_refs = refs[pieces + 8 : pieces + 8 + pieces]
    keep_ref, send_ref, acc = refs[pieces + 8 + pieces :]
    width = caps_ref.shape[1]
    slots = gathered[0].shape[0]
    count = caps_ref.shape[0]
    keys_n = pieces * slots
    runs = lengths_ref.shape[1]

    token = lax.broadcasted_iota(jnp.int32, (count, keys_n), 0)
    key = lax.broadcasted_iota(jnp.int32, (count, keys_n), 1)
    slot = key % slots
    group = token // local
    position = token - group * local + where_ref[0] * local
    document = jnp.zeros((count, keys_n), jnp.int32)
    for m in range(groups):
        end = jnp.int32(0)
        for j in range(runs):
            end = end + lengths_ref[m, j]
            document = document + jnp.where((group == m) & (position >= end), 1, 0)
    allowed = slot == group * clips + document % clips
    valid = (document[:, 0:1] < runs - 1).astype(f32)

    pack = caps_ref[...].astype(f32)
    unit, inv = unit_norm(pack)
    gain = gains_ref[3:4, :]
    normed = (unit * gain).astype(bf16)
    visual = jnp.concatenate([g[...] for g in gathered], axis=0)
    queries = nn(normed, qkv_ref[0, 0]).astype(bf16)
    keys = nn(visual, qkv_ref[0, 1]).astype(bf16)
    values = nn(visual, qkv_ref[0, 2]).astype(bf16)

    masks = [head_mask((count, width), 1, h) for h in range(HEADS)]
    zero = jnp.zeros((count, width), bf16)

    def by_head(x):
        return jnp.concatenate([jnp.where(m, x, zero) for m in masks], axis=0)

    def merge(x):
        cut = [x[h * count : (h + 1) * count] for h in range(HEADS)]
        return functools.reduce(jnp.add, [jnp.where(m, c, 0.0) for m, c in zip(masks, cut)])

    allowed_all = jnp.concatenate([allowed.astype(jnp.int32)] * HEADS, axis=0) > 0
    split_q = by_head(queries)
    scores = jnp.where(allowed_all, nt(split_q, keys) * SCALE, MASKED)
    expo = jnp.exp(scores - jnp.max(scores, axis=1, keepdims=True))
    probs = expo / jnp.sum(expo, axis=1, keepdims=True)
    low = probs.astype(bf16)
    context = merge(nn(low, values)).astype(bf16)
    out_ref[...] = (pack + valid * nn(context, outw_ref[0])).astype(bf16)

    cot = cot_ref[...].astype(f32)
    branch = (cot * valid).astype(bf16)
    split_d = by_head(nt(branch, outw_ref[0]).astype(bf16))
    dvalues = tn(low, split_d)
    dprobs = nt(split_d, values)
    dscores = probs * (dprobs - jnp.sum(dprobs * probs, axis=1, keepdims=True))
    dscores = jnp.where(allowed_all, dscores, 0.0).astype(bf16)
    dqueries = (merge(nn(dscores, keys)) * SCALE).astype(bf16)
    dkeys = tn(dscores, split_q) * SCALE
    dnormed = nt(dqueries, qkv_ref[0, 0])
    grad_ref[...] = (cot + norm_back(unit, inv, gain, dnormed)).astype(bf16)
    gain_ref[...] = jnp.concatenate([row_sum(dnormed * unit), jnp.zeros((7, width), f32)], axis=0)
    low_k, low_v = dkeys.astype(bf16), dvalues.astype(bf16)
    part = nt(low_k, qkv_ref[0, 1]) + nt(low_v, qkv_ref[0, 2])
    for g in range(pieces):
        part_refs[g][...] = part[g * slots : (g + 1) * slots]
    if acc.shape[0] > 4 * width:
        acc[...] = jnp.zeros(acc.shape, f32)
    acc[0:width, :] = tn(normed, dqueries)
    acc[width : 2 * width, :] = tn(visual, low_k)
    acc[2 * width : 3 * width, :] = tn(visual, low_v)
    acc[3 * width : 4 * width, :] = tn(context, branch)
    emit(where_ref, acc, keep_ref, send_ref)


def captions_step(where, lengths, gathered, caps, cot, qkv, outw, gains, plan):
    count, width = caps.shape
    groups = lengths.shape[0]
    pieces = len(gathered)
    slots = gathered[0].shape[0]
    operands = list(gathered) + [caps, cot, qkv, outw, gains]
    acc_rows, packet_specs, packet_shapes = plan.packet(4 * width, width)
    return pl.pallas_call(
        functools.partial(caption_kernel, pieces, groups, plan.clips, count // groups),
        grid=(1,),
        in_specs=[scalars(), scalars()]
        + [full(x.shape) for x in operands[:-3]]
        + [
            pl.BlockSpec((1, 3, width, width), lambda i: (2, 0, 0, 0)),
            pl.BlockSpec((1, width, width), lambda i: (2, 0, 0)),
            full(gains.shape),
        ],
        out_specs=[full((count, width))] * 2
        + [full((8, width))]
        + [full((slots, width))] * pieces
        + packet_specs,
        out_shape=[shape_of((count, width), bf16)] * 2
        + [shape_of((8, width), f32)]
        + [shape_of((slots, width), f32)] * pieces
        + packet_shapes,
        scratch_shapes=[pltpu.VMEM((acc_rows, width), f32)],
        compiler_params=params(12),
        cost_estimate=cost(4e9, 8e6),
        name="captions_step",
    )(where, lengths, *operands)


def mlp_kernel(
    pieces, patch, ff, where_ref, resid_ref, cot_ref, final_ref, gains_ref, up_ref, down_ref, *refs
):
    parts = refs[:pieces]
    out_ref, dresid_ref, gain_ref, keep_ref, send_ref, acc, dcls = refs[-7:]
    step = pl.program_id(0)
    batch, rows, width = resid_ref.shape
    wide = acc.shape[1]
    blocks = ff // wide

    @pl.when(step == 0)
    def _():
        acc[...] = jnp.zeros(acc.shape, f32)
        dvisual = functools.reduce(jnp.add, [p[...] for p in parts])
        unit, inv = unit_norm(final_ref[...])
        dcls[...] = norm_back(unit, inv, gains_ref[2:3, :], dvisual)
        gain_ref[...] = jnp.concatenate(
            [jnp.zeros((1, width), f32), row_sum(dvisual * unit), jnp.zeros((6, width), f32)],
            axis=0,
        )

    resid = resid_ref[...].reshape(batch * rows, width)
    gain = gains_ref[1:2, :]
    unit, inv = unit_norm(resid)
    normed32 = unit * gain
    normed = normed32.astype(bf16)
    normed_t = normed32.T.astype(bf16)
    pieces_d = []
    for i in range(batch):
        one = pad_rows(cot_ref[i].astype(f32), rows)
        pieces_d.append(put_row(one, 0, one[0:1] + dcls[pl.ds(step * batch + i, 1), :]))
    dfinal = jnp.concatenate(pieces_d, axis=0)
    branch = dfinal.astype(bf16)
    branch_t = dfinal.T.astype(bf16)
    final = resid
    dnormed = jnp.zeros((batch * rows, width), f32)
    for c in range(blocks):
        span = slice(c * wide, (c + 1) * wide)
        hidden = nn(normed, up_ref[:, span])
        gate = sigmoid(1.702 * hidden)
        active = (hidden * gate).astype(bf16)
        final = final + nn(active, down_ref[span, :])
        dactive = nt(branch, down_ref[span, :])
        dhidden = (dactive * gate * (1.0 + 1.702 * hidden * (1.0 - gate))).astype(bf16)
        dnormed = dnormed + nt(dhidden, up_ref[:, span])
        acc[c * width : (c + 1) * width, :] += nn(normed_t, dhidden)
        acc[(blocks + c) * width : (blocks + c + 1) * width, :] += nn(branch_t, active)
    for i in range(batch):
        out_ref[i] = final[i * rows : i * rows + patch].astype(bf16)
    dresid = dfinal + norm_back(unit, inv, gain, dnormed)
    dresid_ref[...] = dresid.reshape(batch, rows, width)
    gain_ref[0:1, :] += row_sum(dnormed * unit)

    @pl.when(step == pl.num_programs(0) - 1)
    def _():
        emit(where_ref, acc, keep_ref, send_ref)


def mlp_step(where, resid, cot, final, gains, up, down, parts, plan, after=()):
    count, rows, width = resid.shape
    patch = cot.shape[1]
    ff = up.shape[1]
    slots = final.shape[0]
    batch = share_of(count, 2)
    wide = 2 * width
    acc_rows, packet_specs, packet_shapes = plan.packet(2 * ff * width // wide, wide)
    return pl.pallas_call(
        functools.partial(mlp_kernel, len(parts), patch, ff),
        grid=(count // batch,),
        in_specs=[
            scalars(),
            frames_block(batch, (rows, width)),
            frames_block(batch, (patch, width)),
            full((slots, width)),
            full(gains.shape),
            full(up.shape),
            full(down.shape),
        ]
        + [full((slots, width))] * len(parts)
        + [pl.BlockSpec(memory_space=pl.ANY)] * len(after),
        out_specs=[
            frames_block(batch, (patch, width)),
            frames_block(batch, (rows, width)),
            full((8, width)),
        ]
        + packet_specs,
        out_shape=[
            shape_of((count, patch, width), bf16),
            shape_of((count, rows, width), f32),
            shape_of((8, width), f32),
        ]
        + packet_shapes,
        scratch_shapes=[pltpu.VMEM((acc_rows, wide), f32), pltpu.VMEM((slots, width), f32)],
        compiler_params=params(36),
        cost_estimate=cost(20e9, 20e6),
        name="mlp_step",
    )(where, resid, cot, final, gains, up, down, *parts, *after)


def attend_back_kernel(tokens, first, last, waits, where_ref, normed_ref, kv_ref, *refs):
    (
        video_ref, message_ref, nmsg_ref, kvmsg_ref, ctx_ref, lse_ref, dresid_ref, gains_ref,
        wq_ref, wk_ref, wv_ref, wo_ref,
    ) = refs[:12]
    refs = refs[12:]
    if first:
        carried, refs = refs[1:5], refs[5:]
    refs = refs[waits:]
    outs = refs[: 6 if last else 5]
    grad_ref, dmsg_ref, dcls_ref, gain_ref = outs[:4]
    acc, wqt, wkt, wall = refs[len(outs) :]
    here = pl.program_id(0)
    step = here + first
    batch, rows, width = dresid_ref.shape
    patch = tokens - 1

    @pl.when(here == 0)
    def _():
        wqt[...] = wq_ref[...].T
        wkt[...] = wk_ref[...].T
        wall[:, 0:width] = wq_ref[...]
        wall[:, width : 2 * width] = wk_ref[...]
        wall[:, 2 * width : 3 * width] = wv_ref[...]
        for k, ref in enumerate((dmsg_ref, dcls_ref, gain_ref, acc)):
            ref[...] = carried[k][...] if first else jnp.zeros(ref.shape, f32)

    frames = range(batch)
    normed, kv = [], []
    for i in frames:
        normed.append(with_message(normed_ref[i], nmsg_ref, tokens, step * batch + i))
        kv.append(with_message(kv_ref[i], kvmsg_ref, tokens, step * batch + i))
    branch = [dresid_ref[i].astype(bf16) for i in frames]
    queries_t = [nt(wqt[...], n).astype(bf16) * jnp.bfloat16(SCALE) for n in normed]
    dcontext_t = [nt(wo_ref[...], b).astype(bf16) for b in branch]
    keys_t = [nt(wkt[...], n).astype(bf16) for n in normed]
    acc[3 * width : 4 * width, :] += functools.reduce(
        jnp.add, [nn(ctx_ref[i], branch[i]) for i in frames]
    )
    jobs = [(i, h) for i in frames for h in range(HEADS)]
    own = [slice(h * HEAD_DIM, (h + 1) * HEAD_DIM) for h in range(HEADS)]
    scores, dprobs, low, dscores, dq, dk, dv = {}, {}, {}, {}, {}, {}, {}

    def score(job):
        i, h = job
        scores[job] = nn(pair_lanes(kv[i], h), half_pair(queries_t[i], h))
        dprobs[job] = nn(pair_lanes(kv[i], HEADS + h), half_pair(dcontext_t[i], h))

    def soften(job):
        i, h = job
        probs = jnp.exp(masked_tail(scores.pop(job), tokens) - lse_ref[i, h : h + 1, :])
        low[job] = probs.astype(bf16)
        weighted = dprobs.pop(job) * probs
        dscores[job] = (weighted - probs * row_sum(weighted)).astype(bf16)

    def mix(job):
        i, h = job
        dq[job] = nn(keys_t[i][own[h]], dscores[job]) * SCALE
        dk[job] = nt(queries_t[i][own[h]], dscores.pop(job))
        dv[job] = nt(dcontext_t[i][own[h]], low.pop(job))

    stagger(jobs, [score, soften, mix], 2)
    dall = []
    for i in frames:
        parts = [d[i, h] for d in (dq, dk, dv) for h in range(HEADS)]
        dall.append(jnp.concatenate(parts, axis=0).astype(bf16))
    acc[0 : 3 * width, :] += functools.reduce(
        jnp.add, [nn(dall[i], normed[i]) for i in frames]
    )
    gain_sum = jnp.zeros((1, width), f32)
    for i in frames:
        dnormed = nn(wall[...], dall[i]).T
        at = pl.ds(step * batch + i, 1)
        base = put_row(pad_rows(video_ref[i].astype(f32), rows), tokens - 1, message_ref[at, :])
        unit, inv = unit_norm(base)
        dtokens = dresid_ref[i] + norm_back(unit, inv, gains_ref[0:1, :], dnormed)
        gain_sum = gain_sum + row_sum(dnormed * unit)
        grad_ref[i] = dtokens[:patch].astype(bf16)
        dcls_ref[at, :] = dtokens[0:1]
        dmsg_ref[at, :] = dtokens[patch : patch + 1]
    gain_ref[0:1, :] += gain_sum

    @pl.when(here == pl.num_programs(0) - 1)
    def _():
        if last:
            emit(where_ref, acc, *outs[4:])
        else:
            outs[4][...] = acc[...]


def attend_back(
    where, normed, kv, video, message, nmsg, kvmsg, ctx, lse, dresid, gains, qkv, outw, plan,
    batch, first, steps, carried=(), after=(),
):
    count, rows, width = normed.shape
    patch = video.shape[1]
    slots = message.shape[0]
    last = (first + steps) * batch == count
    acc_rows, packet_specs, packet_shapes = plan.packet(4 * width, width)
    if not last:
        packet_specs, packet_shapes = [full((acc_rows, width))], [shape_of((acc_rows, width), f32)]

    def block(shape):
        return pl.BlockSpec((batch,) + shape, lambda i, *_: (i + first, 0, 0))

    anywhere = pl.BlockSpec(memory_space=pl.ANY)
    carry_specs = [anywhere] + [full(x.shape) for x in carried[1:]] if carried else []
    return pl.pallas_call(
        functools.partial(attend_back_kernel, patch + 1, first, last, len(after)),
        grid=(steps,),
        in_specs=[
            scalars(),
            block((rows, width)),
            block((rows, 2 * width)),
            block((patch, width)),
            full((slots, width)),
            full((slots, width)),
            full((slots, 2 * width)),
            block((width, rows)),
            block((8, rows)),
            block((rows, width)),
            full(gains.shape),
            square(width, 1, 0),
            square(width, 1, 1),
            square(width, 1, 2),
            square(width, 1),
        ]
        + carry_specs
        + [anywhere] * len(after),
        out_specs=[block((patch, width))]
        + [full((slots, width))] * 2
        + [full((8, width))]
        + packet_specs,
        out_shape=[shape_of((count, patch, width), bf16)]
        + [shape_of((slots, width), f32)] * 2
        + [shape_of((8, width), f32)]
        + packet_shapes,
        input_output_aliases={15: 0} if carried else {},
        scratch_shapes=[
            pltpu.VMEM((acc_rows, width), f32),
            pltpu.VMEM((width, width), bf16),
            pltpu.VMEM((width, width), bf16),
            pltpu.VMEM((width, 3 * width), bf16),
        ],
        compiler_params=params(26),
        cost_estimate=cost(4.5e9 * steps, 4e6 * steps),
        name="attend_back",
    )(
        where, normed, kv, video, message, nmsg, kvmsg, ctx, lse, dresid, gains, qkv, qkv, qkv,
        outw, *carried, *after,
    )


class Groups:
    def __init__(self, layout, slots):
        self.segs, self.frames, self.clips = layout
        self.slots = slots
        self.groups = self.segs * self.clips
        self.together = max(1, min(self.groups, 512 // (self.frames * slots)))
        self.steps = self.groups // self.together
        self.rows = self.frames * self.together * slots
        per_group = self.frames * slots
        self.side = per_group * max(1, min(self.together, 128 // per_group))
        self.blocks = [slice(at, at + self.side) for at in range(0, self.rows, self.side)]
        self.jobs = [(i, h) for i in range(len(self.blocks)) for h in range(HEADS)]

    def row_of(self, s, f, c):
        group = s * self.clips + c
        step, inside = group // self.together, group % self.together
        return step, pl.multiple_of((inside * self.frames + f) * self.slots, 16)

    def every(self, where_ref):
        me_f, me_s, me_c = where_ref[0], where_ref[1], where_ref[2]
        for a in range(self.segs):
            for b in range(self.frames):
                for d in range(self.clips):
                    yield a, b, d, *self.row_of(me_s ^ a, me_f ^ b, me_c ^ d)

    def run(self, batch):
        def first(ref, at, value):
            ref[at] = value

        def again(ref, at, value):
            ref[at] += value

        batch(0, first)
        if self.steps > 1:
            pl.loop(1, self.steps)(lambda step: batch(step, again))


def join(groups, *parts):
    lanes = [
        jnp.concatenate([p[i, h] for p in parts for h in range(HEADS)], axis=0)
        for i in range(len(groups.blocks))
    ]
    return (jnp.concatenate(lanes, axis=1) if len(lanes) > 1 else lanes[0]).astype(bf16)


OWN = [slice(h * HEAD_DIM, (h + 1) * HEAD_DIM) for h in range(HEADS)]


def message_forward_kernel(groups, where_ref, *refs):
    side = refs[: groups.segs]
    (
        mw_ref, mg_ref, qkv_ref, classes_ref, start_ref, values_ref, qt_ref, kt_ref, probs_ref,
        ctx_ref, wqt, wkt, wvt,
    ) = refs[groups.segs :]
    for a, b, d, step, row in groups.every(where_ref):
        classes_ref[step, pl.ds(row, groups.slots), :] = side[a][d, b]
    wqt[...] = qkv_ref[0, 0].T
    wkt[...] = qkv_ref[0, 1].T
    wvt[...] = qkv_ref[0, 2].T
    edge = (groups.side, groups.side)
    key, query = lax.broadcasted_iota(jnp.int32, edge, 0), lax.broadcasted_iota(jnp.int32, edge, 1)
    per_group = groups.frames * groups.slots
    same = (key % groups.slots == query % groups.slots) & (key // per_group == query // per_group)

    def batch(step, put):
        del put
        start = nn(classes_ref[step], mw_ref[...]).astype(bf16)
        start_ref[step] = start
        unit, _ = unit_norm(start.astype(f32))
        normed = (unit * mg_ref[...]).astype(bf16)
        keys = nn(normed, qkv_ref[0, 1]).astype(bf16)
        values_ref[step] = nn(normed, qkv_ref[0, 2]).astype(bf16)
        queries_t = nt(wqt[...], normed).astype(bf16) * jnp.bfloat16(SCALE)
        values_t = nt(wvt[...], normed).astype(bf16)
        qt_ref[step] = queries_t
        kt_ref[step] = nt(wkt[...], normed).astype(bf16)
        scores, low, ctx = {}, {}, {}

        def score(job):
            i, h = job
            at = groups.blocks[i]
            scores[job] = nn(pair_lanes(keys[at], h), half_pair(queries_t[:, at], h))

        def soften(job):
            i, h = job
            one = jnp.where(same, scores.pop(job), MASKED)
            expo = jnp.exp(one - jnp.max(one, axis=0, keepdims=True))
            probs = expo * (1.0 / row_sum(expo))
            probs_ref[step, i * HEADS + h] = probs.astype(probs_ref.dtype)
            low[job] = probs.astype(bf16)

        def mix(job):
            i, h = job
            ctx[job] = nn(values_t[OWN[h], groups.blocks[i]], low.pop(job))

        stagger(groups.jobs, [score, soften, mix], 3)
        ctx_ref[step] = join(groups, ctx)

    groups.run(batch)


def message_forward(where, side, mw, mg, qkv, groups):
    width = mw.shape[0]
    rows, steps = groups.rows, groups.steps
    outs = [
        shape_of((steps, rows, width), bf16),
        shape_of((steps, rows, width), bf16),
        shape_of((steps, rows, width), bf16),
        shape_of((steps, width, rows), bf16),
        shape_of((steps, width, rows), bf16),
        shape_of((steps, len(groups.jobs), groups.side, groups.side), f32 if steps == 1 else bf16),
        shape_of((steps, width, rows), bf16),
    ]
    return pl.pallas_call(
        functools.partial(message_forward_kernel, groups),
        grid=(1,),
        in_specs=[scalars()]
        + [full(x.shape) for x in side]
        + [
            full(mw.shape),
            full(mg.shape),
            pl.BlockSpec((1, 3, width, width), lambda i: (0, 0, 0, 0)),
        ],
        out_specs=[full(x.shape) for x in outs],
        out_shape=outs,
        scratch_shapes=[pltpu.VMEM((width, width), bf16)] * 3,
        compiler_params=params(56),
        cost_estimate=cost(3e9, 6e6),
        name="message_forward",
    )(where, *side, mw, mg, qkv)


def message_back_kernel(layout, groups, where_ref, *refs):
    frame_part(layout, where_ref, *refs)
    message_part(groups, where_ref, *refs)


def frame_part(layout, where_ref, *refs):
    segs, frames, clips = layout
    pieces, refs = refs[: segs * frames], refs[segs * frames + 7 :]
    big_ref, out_ref, whole = refs[6], refs[7], refs[12]
    width = out_ref.shape[-1]
    chunk = whole.shape[0] // (segs * frames * clips)
    place(
        layout,
        where_ref,
        lambda a, b, d: pieces[a * frames + b][d * chunk : (d + 1) * chunk, :],
        whole,
        chunk,
    )
    for j in range(3):
        big_ref[1, j] = whole[j * width : (j + 1) * width, :].astype(f32).T
    out_ref[1] = whole[3 * width : 4 * width, :].astype(f32)


def message_part(groups, where_ref, *refs):
    count = groups.segs * groups.frames
    pieces, refs = refs[:count], refs[count:]
    classes_ref, start_ref, values_ref, qt_ref, kt_ref, probs_ref, ctx_ref = refs[:7]
    mw_ref, mg_ref, qkv_ref, outw_ref = refs[7:11]
    big_ref, out_ref, mwg_ref, gain_ref, gains_ref, dclass_ref, _, dmsgs, dstart, wall = refs[13:]
    width, slots = mw_ref.shape[0], groups.slots
    for a, b, d, step, row in groups.every(where_ref):
        piece = pieces[a * groups.frames + b]
        at = piece.shape[0] - (groups.clips - d) * slots
        dmsgs[step, pl.ds(row, slots), :] = piece[at : at + slots, :]
    gain_total = jnp.zeros((slots, width), f32)
    for i in range(groups.frames * groups.together):
        for step in range(groups.steps):
            gain_total += dmsgs[step, i * slots : (i + 1) * slots, :].astype(f32)
    gains_ref[...] = gain_total[slots - 4 : slots]
    for j in range(3):
        wall[:, j * width : (j + 1) * width] = qkv_ref[0, j]
    index = lax.broadcasted_iota(jnp.int32, (groups.rows, 1), 0) % slots
    my_step, my_row = groups.row_of(where_ref[1], where_ref[0], where_ref[2])

    def batch(step, put):
        dm = jnp.where(index < slots - 6, dmsgs[step].astype(f32), 0.0).astype(bf16)
        unit, inv = unit_norm(start_ref[step].astype(f32))
        normed = (unit * mg_ref[...]).astype(bf16)
        dcontext_t = nt(outw_ref[0], dm).astype(bf16)
        values, queries_t, keys_t = values_ref[step], qt_ref[step], kt_ref[step]
        dprobs, low, dscores, dq, dk, dv = {}, {}, {}, {}, {}, {}

        def score(job):
            i, h = job
            at = groups.blocks[i]
            dprobs[job] = nn(pair_lanes(values[at], h), half_pair(dcontext_t[:, at], h))

        def soften(job):
            i, h = job
            probs = probs_ref[step, i * HEADS + h].astype(f32)
            low[job] = probs.astype(bf16)
            weighted = dprobs.pop(job) * probs
            dscores[job] = (weighted - probs * row_sum(weighted)).astype(bf16)

        def mix(job):
            i, h = job
            at = groups.blocks[i]
            dq[job] = nn(keys_t[OWN[h], at], dscores[job]) * SCALE
            dk[job] = nt(queries_t[OWN[h], at], dscores.pop(job))
            dv[job] = nt(dcontext_t[OWN[h], at], low.pop(job))

        stagger(groups.jobs, [score, soften, mix], 2)
        put(out_ref, 0, nn(ctx_ref[step], dm))
        dall = join(groups, dq, dk, dv)
        grads = nn(dall, normed)
        for j in range(3):
            put(big_ref, (0, j), grads[j * width : (j + 1) * width].T)
        dnormed = nn(wall[...], dall).T
        put(gain_ref, ..., jnp.sum(dnormed * unit, axis=0))
        ds = norm_back(unit, inv, mg_ref[...], dnormed) + dm.astype(f32)
        dstart[...] = ds
        put(mwg_ref, ..., tn(classes_ref[step], ds.astype(bf16)))

        @pl.when(my_step == step)
        def _():
            dclass_ref[...] = nt(dstart[pl.ds(my_row, slots), :].astype(bf16), mw_ref[...])

    groups.run(batch)


def message_back(where, pieces, forward, mw, mg, qkv, outw, big, out, layout, groups):
    width = mw.shape[0]
    operands = list(pieces) + list(forward) + [mw, mg]
    chunk = pieces[0].shape[0] // groups.clips - groups.slots
    return pl.pallas_call(
        functools.partial(message_back_kernel, layout, groups),
        grid=(1,),
        in_specs=[scalars()]
        + [full(x.shape) for x in operands]
        + [
            pl.BlockSpec((1, 3, width, width), lambda i: (0, 0, 0, 0)),
            pl.BlockSpec((1, width, width), lambda i: (0, 0, 0)),
            pl.BlockSpec(memory_space=pl.ANY),
            pl.BlockSpec(memory_space=pl.ANY),
        ],
        out_specs=[
            pl.BlockSpec((2, 3, width, width), lambda i: (0, 0, 0, 0)),
            pl.BlockSpec((2, width, width), lambda i: (0, 0, 0)),
            full((width, width)),
            full((width,)),
            full((4, width)),
            full((groups.slots, width)),
        ],
        out_shape=[
            shape_of((3, 3, width, width), f32),
            shape_of((3, width, width), f32),
            shape_of((width, width), f32),
            shape_of((width,), f32),
            shape_of((4, width), f32),
            shape_of((groups.slots, width), f32),
        ],
        input_output_aliases={len(operands) + 3: 0, len(operands) + 4: 1},
        scratch_shapes=[
            pltpu.VMEM((groups.groups * groups.frames * chunk, width), bf16),
            pltpu.VMEM((groups.steps, groups.rows, width), bf16),
            pltpu.VMEM((groups.rows, width), f32),
            pltpu.VMEM((width, 3 * width), bf16),
        ],
        compiler_params=params(30 if groups.steps == 1 else 60),
        cost_estimate=cost(4e9, 12e6),
        name="message_back",
    )(where, *operands, qkv, outw, big, out)


def emit(where_ref, acc, keep_ref, send_ref):
    frames, clips, chunk = keep_ref.shape[:3]
    me_f, me_s = where_ref[0], where_ref[1]
    for a, out in enumerate((keep_ref, send_ref)):
        for b in range(frames):
            for d in range(clips):
                to = ((me_s ^ a) * frames + (me_f ^ b)) * clips + d
                at = pl.multiple_of(to * chunk, 16)
                out[b, d] = acc[pl.ds(at, chunk), :].astype(bf16)


class Plan:
    def __init__(self, clips):
        self.clips = clips
        self.segs = lax.axis_size("seg")
        self.frames = lax.axis_size("frame")
        self.rings = lax.axis_size("clip")
        self.layout = (self.segs, self.frames, self.rings)
        self.devices = self.segs * self.frames * self.rings

    def chunk(self, rows):
        share = -(-rows // self.devices)
        return -(-share // 16) * 16

    def packet(self, rows, width):
        chunk = self.chunk(rows)
        shape = (self.frames, self.rings, chunk, width)
        return chunk * self.devices, [full(shape)] * 2, [shape_of(shape, bf16)] * 2


def swap(x, axis, k):
    count = lax.axis_size(axis)
    return lax.ppermute(x, axis, [(i, i ^ k) for i in range(count)])


def behind(x, *others):
    return lax.optimization_barrier((x, others))[0]


class Sum:
    def __init__(self, arrays, views=None):
        self.arrays = list(arrays)
        self.views = list(views or [()] * len(self.arrays))

    def part(self, view):
        return Sum(self.arrays, [v + (view,) for v in self.views])

    def plus(self, *arrays):
        return Sum(self.arrays + list(arrays), self.views + [()] * len(arrays))

    def value(self):
        terms = []
        for x, views in zip(self.arrays, self.views):
            for view in views:
                x = view(x)
            terms.append(x.astype(f32))
        return functools.reduce(jnp.add, terms).astype(bf16)


jax.tree_util.register_pytree_node(
    Sum, lambda s: (s.arrays, s.views), lambda views, arrays: Sum(arrays, views)
)


def at(k):
    return lambda x: x[k]


def total(one, two):
    return (one.astype(f32) + two.astype(f32)).astype(bf16)


def reduce_seg(keep, send):
    return Sum([keep, swap(send, "seg", 1)])


def frame_sends(terms):
    return [terms.part(at(b)).value() for b in range(1, lax.axis_size("frame"))]


def reduce_frame(terms, sends):
    return terms.part(at(0)).plus(*[swap(x, "frame", b + 1) for b, x in enumerate(sends)])


def clip_bits():
    count = lax.axis_size("clip")
    return [1 << j for j in range(count.bit_length() - 1)]


def swap_two(one, two, axis, k):
    width = one.shape[-1]
    rows = one.size // width
    got = swap(jnp.concatenate([one.reshape(-1, width), two.reshape(-1, width)]), axis, k)
    return got[:rows].reshape(one.shape), got[rows:].reshape(two.shape)


def exchange(part, rows, bit):
    got, got_rows = swap_two(part, rows, "clip", bit)
    return total(part, got), jnp.concatenate([rows, got_rows])


def gather_frame(held):
    return [held] + [swap(held, "frame", b) for b in range(1, lax.axis_size("frame"))]


def gather_seg(held):
    return held + [swap(h, "seg", 1) for h in held]


def place(layout, where_ref, piece, whole, chunk):
    segs, frames, clips = layout
    me_f, me_s = where_ref[0], where_ref[1]
    for a in range(segs):
        for b in range(frames):
            for d in range(clips):
                of = ((me_s ^ a) * frames + (me_f ^ b)) * clips + d
                whole[pl.ds(pl.multiple_of(of * chunk, 16), chunk), :] = piece(a, b, d)


def unpack_kernel(layout, where_ref, *refs):
    segs, frames, clips = layout
    main = refs[:segs]
    up_ref, down_ref, whole = refs[segs:]
    width, ff = up_ref.shape
    wide = whole.shape[1]
    place(layout, where_ref, lambda a, b, d: main[a][b * clips + d], whole, main[0].shape[1])
    blocks = ff // wide
    for c in range(blocks):
        span = slice(c * wide, (c + 1) * wide)
        up_ref[:, span] = whole[c * width : (c + 1) * width, :].astype(f32)
        other = whole[(blocks + c) * width : (blocks + c + 1) * width, :]
        down_ref[span, :] = other.astype(f32).T


def unpack(where, main, width, ff, plan):
    chunk, wide = main[0].shape[1:]
    return pl.pallas_call(
        functools.partial(unpack_kernel, plan.layout),
        grid=(1,),
        in_specs=[scalars()] + [full(x.shape) for x in main],
        out_specs=[full((width, ff)), full((ff, width))],
        out_shape=[shape_of((width, ff), f32), shape_of((ff, width), f32)],
        scratch_shapes=[pltpu.VMEM((plan.devices * chunk, wide), bf16)],
        compiler_params=params(40),
        cost_estimate=cost(2e9, 10e6),
        name="unpack",
    )(where, *main)


def unpack_side_kernel(layout, where_ref, *refs):
    segs = layout[0]
    side = refs[:segs]
    big_ref, out_ref, whole = refs[segs:]
    width = out_ref.shape[-1]
    place(layout, where_ref, lambda a, b, d: side[a][b, d], whole, side[0].shape[2])
    for j in range(3):
        big_ref[0, j] = whole[j * width : (j + 1) * width, :].astype(f32)
    out_ref[0] = whole[3 * width : 4 * width, :].astype(f32)


def unpack_side(where, side, plan):
    rows, width = side[0].shape[2:]
    return pl.pallas_call(
        functools.partial(unpack_side_kernel, plan.layout),
        grid=(1,),
        in_specs=[scalars()] + [full(x.shape) for x in side],
        out_specs=[
            pl.BlockSpec((1, 3, width, width), lambda i: (2, 0, 0, 0)),
            pl.BlockSpec((1, width, width), lambda i: (2, 0, 0)),
        ],
        out_shape=[shape_of((3, 3, width, width), f32), shape_of((3, width, width), f32)],
        scratch_shapes=[pltpu.VMEM((plan.devices * rows, width), bf16)],
        compiler_params=params(30),
        cost_estimate=cost(1e9, 4e6),
        name="unpack_side",
    )(where, *side)


def last_rows_kernel(gain_a, gain_b, gain_c, dmsg_ref, out_ref):
    slots, width = dmsg_ref.shape
    rows = [
        dmsg_ref[0 : slots - 6, :],
        jnp.zeros((2, width), f32),
        gain_a[0:1, :],
        gain_b[0:1, :],
        gain_b[1:2, :],
        gain_c[0:1, :],
    ]
    out_ref[...] = jnp.concatenate(rows, axis=0).astype(bf16)


def last_rows(gain_a, gain_b, gain_c, dmsg):
    return pl.pallas_call(
        last_rows_kernel,
        out_shape=shape_of(dmsg.shape, bf16),
        name="last_rows",
    )(gain_a, gain_b, gain_c, dmsg)


def local(
    video, captions, caption_lengths, message_weight, message_gain, qkv_weights, out_weights,
    mlp_up, mlp_down, gains, video_cot, caption_cot,
):
    micro, clips, per_frame, patch, width = video.shape
    count = micro * clips * per_frame
    ff = mlp_up.shape[1]
    plan = Plan(clips)
    tokens = patch + 1
    rows = -(-tokens // 16) * 16
    slots = -(-(count + 6) // 16) * 16
    where = jnp.stack(
        [lax.axis_index("frame"), lax.axis_index("seg"), lax.axis_index("clip")]
    ).astype(jnp.int32)
    frames = video.reshape(count, patch, width)
    cots = video_cot.reshape(count, patch, width)
    caps = captions.reshape(-1, width)
    cap_cots = caption_cot.reshape(-1, width)
    lengths = caption_lengths.reshape(micro, -1)
    gain = message_gain.reshape(1, width)

    classes = class_rows(video, slots)
    gathered = gather_frame(classes)
    normed, kv = norm_tokens(frames, gains, qkv_weights, rows)
    message, nmsg, kvmsg, visual, final = first_rows(
        gathered, message_weight, gain, qkv_weights, out_weights, mlp_up, mlp_down, gains,
        kv, tokens,
    )
    visuals = gather_frame(visual)
    results = captions_step(
        where, lengths, visuals, caps, cap_cots, qkv_weights, out_weights, gains, plan
    )
    caption_out, caption_grad, gain_c = results[:3]
    parts = list(results[3:-2])
    parts = [parts[0]] + [swap(parts[b], "frame", b) for b in range(1, plan.frames)]
    bits = clip_bits()
    rows_all = jnp.stack(gathered)[None]
    side = reduce_seg(*results[-2:])
    side = behind(side, results[3])
    sends = frame_sends(side)
    resid, ctx, lse = attend(
        normed, kv, frames, message, nmsg, kvmsg, qkv_weights, out_weights, tokens, sends
    )
    side = reduce_frame(side, sends)
    parts, resid, side = behind((parts, resid, side))
    side = side.value()
    side, resid = behind((side, resid))
    video_out, dresid, gain_b, keep, send = mlp_step(
        where, resid, cots, final, gains, mlp_up, mlp_down, parts, plan
    )
    for bit in bits[:-1]:
        side, rows_all = exchange(side, rows_all, bit)
    side, rows_all, video_out, dresid, keep, send = behind(
        (side, rows_all, video_out, dresid, keep, send)
    )
    main = reduce_seg(keep, send)
    turned = video_out.reshape(video.shape).transpose(1, 2, 3, 0, 4)
    main, dresid, turned = behind((main, dresid, turned))
    video_out = turned.transpose(3, 0, 1, 2, 4)
    sends = frame_sends(main)
    sends, dresid, side, rows_all = behind((sends, dresid, side, rows_all))
    batch = share_of(count, 2)
    steps = count // batch
    late_steps = 2
    back = functools.partial(
        attend_back, where, normed, kv, frames, message, nmsg, kvmsg, ctx, lse, dresid, gains,
        qkv_weights, out_weights, plan, batch,
    )
    carried = back(0, steps - late_steps)
    main = reduce_frame(main, sends)
    side, rows_all = exchange(side, rows_all, bits[-1])
    carried, main, side, rows_all = behind((carried, main, side, rows_all))
    main = main.value()
    main, carried, side = behind((main, carried, side))
    for bit in bits[:-1]:
        main = total(main, swap(main, "clip", bit))
    side = gather_frame(side)
    grad, dmsg, dcls, gain_a, keep, send = back(steps - late_steps, late_steps, carried)
    main, side, keep, send, gain_a, dmsg = behind((main, side, keep, send, gain_a, dmsg))

    main = total(main, swap(main, "clip", bits[-1]))
    late = reduce_seg(keep, send)
    rest = last_rows(gain_a, gain_b, gain_c, dmsg)
    side = jnp.stack(side)
    other, other_rows = swap_two(side, rows_all, "seg", 1)
    late, rest = behind((late, rest))
    late = reduce_frame(late, frame_sends(late))
    main, late, other, other_rows = behind((main, late, other, other_rows))

    held = gather_frame(main)
    late, rest = late.value(), rest[None]
    for bit in bits:
        late, rest = exchange(late, rest, bit)
    big, out = unpack_side(where, [side, other], plan)
    groups = Groups(plan.layout, slots)
    forward = message_forward(
        where, [rows_all, other_rows], message_weight, gain, qkv_weights, groups
    )
    held, late, rest, big, forward = behind((held, late, rest, big, forward))

    late = gather_frame(jnp.concatenate([late.reshape(-1, width), rest.reshape(-1, width)]))
    held = gather_seg([jnp.concatenate(held, axis=0)])
    up_grad, down_grad = unpack(where, held, width, ff, plan)
    late, up_grad = behind((late, up_grad))

    late = gather_seg(late)
    big, out, mw_grad, mg_grad, gains_grad, dclass = message_back(
        where, late, forward, message_weight, gain, qkv_weights, out_weights, big, out,
        plan.layout, groups,
    )
    fixed = (dclass + dcls)[:count].astype(bf16).reshape(micro, clips, per_frame, 1, width)
    grad = lax.dynamic_update_slice(grad.reshape(video.shape), fixed, (0, 0, 0, 0, 0))
    return (
        video_out.reshape(video.shape),
        caption_out.reshape(captions.shape),
        grad,
        caption_grad.reshape(captions.shape),
        mw_grad,
        mg_grad,
        big,
        out,
        up_grad,
        down_grad,
        gains_grad,
    )


def solution(mesh):
    rows = P(None, ("clip", "seg"), "frame", None, None)
    caps = P(None, ("clip", "seg"), "frame", None)
    return jax.shard_map(
        local,
        mesh=mesh,
        in_specs=(rows, caps, P(None, ("clip", "seg"), None)) + (P(),) * 7 + (rows, caps),
        out_specs=(rows, caps, rows, caps) + (P(),) * 7,
        check_vma=False,
    )
```

```python
import functools

import jax
import jax.numpy as jnp
from jax import lax
from jax.experimental import pallas as pl
from jax.experimental.pallas import tpu as pltpu
from jax.sharding import PartitionSpec as P

HEADS = 6
HEAD_DIM = 64
EPS = 1e-05
SCALE = 0.125
MASKED = -1e30

f32 = jnp.float32
bf16 = jnp.bfloat16


def nn(a, b):
    return lax.dot_general(a, b, (((1,), (0,)), ((), ())), preferred_element_type=f32)


def nt(a, b):
    return lax.dot_general(a, b, (((1,), (1,)), ((), ())), preferred_element_type=f32)


def tn(a, b):
    return lax.dot_general(a, b, (((0,), (0,)), ((), ())), preferred_element_type=f32)


def exact(a, b):
    return lax.dot_general(
        a, b, (((1,), (0,)), ((), ())), precision=lax.Precision.HIGHEST, preferred_element_type=f32
    )


def unit_norm(x):
    center = x - jnp.mean(x, axis=-1, keepdims=True)
    inv = lax.rsqrt(jnp.mean(center * center, axis=-1, keepdims=True) + EPS)
    return center * inv, inv


def norm_back(unit, inv, gain, dy):
    du = dy * gain
    mean_du = jnp.mean(du, axis=-1, keepdims=True)
    mean_dot = jnp.mean(du * unit, axis=-1, keepdims=True)
    return inv * (du - mean_du - unit * mean_dot)


def row_sum(x):
    return jnp.sum(x, axis=0, keepdims=True)


def sigmoid(x):
    return 0.5 + 0.5 * jnp.tanh(0.5 * x)


def head_mask(shape, lane_dim, head):
    lane = lax.broadcasted_iota(jnp.int32, shape, lane_dim)
    return (lane >= head * HEAD_DIM) & (lane < (head + 1) * HEAD_DIM)


def head_columns(width):
    lane = lax.broadcasted_iota(jnp.int32, (width, 128), 0)
    col = lax.broadcasted_iota(jnp.int32, (width, 128), 1)
    return ((lane >= col * HEAD_DIM) & (lane < (col + 1) * HEAD_DIM)).astype(f32)


def head_rows(width):
    col = lax.broadcasted_iota(jnp.int32, (128, width), 0)
    lane = lax.broadcasted_iota(jnp.int32, (128, width), 1)
    return ((lane >= col * HEAD_DIM) & (lane < (col + 1) * HEAD_DIM)).astype(f32)


def pad_rows(x, rows):
    if x.shape[0] == rows:
        return x
    return jnp.concatenate([x, jnp.zeros((rows - x.shape[0], x.shape[1]), x.dtype)], axis=0)


def put_row(block, at, row):
    top = at // 16 * 16
    tail = block[top : top + 16]
    index = lax.broadcasted_iota(jnp.int32, tail.shape, 0)
    tail = jnp.where(index == at - top, row, tail)
    pieces = [tail]
    if top:
        pieces.insert(0, block[:top])
    if top + 16 < block.shape[0]:
        pieces.append(block[top + 16 :])
    return jnp.concatenate(pieces, axis=0) if len(pieces) > 1 else tail


def full(shape):
    return pl.BlockSpec(shape, lambda *_: (0,) * len(shape))


def frame_block(shape):
    return pl.BlockSpec((1,) + shape, lambda i, *_: (i, 0, 0))


def frames_block(batch, shape):
    return pl.BlockSpec((batch,) + shape, lambda i, *_: (i, 0, 0))


def stagger(jobs, stages, gap):
    for at in range(len(jobs) + (len(stages) - 1) * gap):
        for k, stage in enumerate(stages):
            j = at - k * gap
            if 0 <= j < len(jobs):
                stage(jobs[j])


def share_of(count, most):
    return max(b for b in range(1, most + 1) if count % b == 0)


def square(width, *at):
    return pl.BlockSpec((None,) * len(at) + (width, width), lambda *_: at + (0, 0))


def scalars():
    return pl.BlockSpec(memory_space=pltpu.SMEM)


def shape_of(shape, dtype):
    return jax.ShapeDtypeStruct(shape, dtype)


def params(mib):
    return pltpu.CompilerParams(vmem_limit_bytes=mib * 1024 * 1024)


def cost(flops, nbytes):
    return pl.CostEstimate(flops=int(flops), bytes_accessed=int(nbytes), transcendentals=0)


def class_kernel(video_ref, out_ref):
    clips, _, micro, width = video_ref.shape
    rows = [video_ref[c, 0, m : m + 1, :].astype(f32) for m in range(micro) for c in range(clips)]
    out_ref[...] = pad_rows(jnp.concatenate(rows, axis=0), out_ref.shape[0]).astype(bf16)


def class_rows(video, slots):
    micro, clips, per_frame, patch, width = video.shape
    turned = video.transpose(1, 2, 3, 0, 4).reshape(clips * per_frame, patch, micro, width)
    return pl.pallas_call(
        class_kernel,
        grid=(1,),
        in_specs=[pl.BlockSpec((clips * per_frame, 1, micro, width), lambda i: (0, 0, 0, 0))],
        out_specs=full((slots, width)),
        out_shape=shape_of((slots, width), bf16),
        name="class_rows",
    )(turned)


def norm_kernel(video_ref, gains_ref, wk_ref, wv_ref, normed_ref, kv_ref, wkv):
    batch, rows, width = normed_ref.shape

    @pl.when(pl.program_id(0) == 0)
    def _():
        wkv[:, :width] = wk_ref[...]
        wkv[:, width:] = wv_ref[...]

    parts = []
    for i in range(batch):
        unit, _ = unit_norm(video_ref[i].astype(f32))
        parts.append(pad_rows(unit * gains_ref[0:1, :], rows).astype(bf16))
        normed_ref[i] = parts[i]
    normed = jnp.concatenate(parts, axis=0)
    kv_ref[...] = nn(normed, wkv[...]).astype(bf16).reshape(batch, rows, 2 * width)


def norm_tokens(video, gains, qkv, rows):
    count, patch, width = video.shape
    batch = share_of(count, 5)
    return pl.pallas_call(
        norm_kernel,
        grid=(count // batch,),
        in_specs=[
            frames_block(batch, (patch, width)),
            full(gains.shape),
            square(width, 1, 1),
            square(width, 1, 2),
        ],
        out_specs=[
            frames_block(batch, (rows, width)),
            frames_block(batch, (rows, 2 * width)),
        ],
        out_shape=[
            shape_of((count, rows, width), bf16),
            shape_of((count, rows, 2 * width), bf16),
        ],
        scratch_shapes=[pltpu.VMEM((width, 2 * width), bf16)],
        compiler_params=params(20),
        cost_estimate=cost(4 * count * rows * width * width, 8 * count * rows * width),
        name="norm_tokens",
    )(video, gains, qkv, qkv)


def message_scores(query, keys, columns):
    return [exact(query.astype(f32) * key.astype(f32), columns) * SCALE for key in keys]


def message_probs(scores):
    top = functools.reduce(jnp.maximum, scores)
    expo = [jnp.exp(score - top) for score in scores]
    total = functools.reduce(jnp.add, expo)
    return [e / total for e in expo]


def first_kernel(
    pieces, count, tokens, *refs
):
    gathered = refs[:pieces]
    (
        mw_ref, mg_ref, qkv_ref, outw_ref, up_ref, down_ref, gains_ref, kv_ref,
        message_ref, nmsg_ref, kvmsg_ref, visual_ref, final_ref, ctx,
    ) = refs[pieces:]
    width = mw_ref.shape[0]
    slots = gathered[0].shape[0]
    rows = kv_ref.shape[1]
    classes = jnp.concatenate([g[...] for g in gathered], axis=0)
    start = nn(classes, mw_ref[...]).astype(bf16)
    unit, _ = unit_norm(start.astype(f32))
    normed = (unit * mg_ref[...]).astype(bf16)
    keys = nn(normed, qkv_ref[0, 1]).astype(bf16)
    values = nn(normed, qkv_ref[0, 2]).astype(bf16)
    query = nn(normed[:slots], qkv_ref[0, 0]).astype(bf16)
    columns, spread = head_columns(width), head_rows(width).astype(bf16)
    cut = [slice(g * slots, (g + 1) * slots) for g in range(pieces)]
    probs = message_probs(message_scores(query, [keys[c] for c in cut], columns))
    context = functools.reduce(
        jnp.add,
        [nn(p.astype(bf16), spread) * values[c].astype(f32) for p, c in zip(probs, cut)],
    ).astype(bf16)
    message = start[:slots].astype(f32) + nn(context, outw_ref[0])
    message_ref[...] = message
    unit, _ = unit_norm(message)
    nmsg = (unit * gains_ref[0:1, :]).astype(bf16)
    nmsg_ref[...] = nmsg.astype(f32)
    kmsg = nn(nmsg, qkv_ref[1, 1]).astype(bf16).astype(f32)
    vmsg = nn(nmsg, qkv_ref[1, 2]).astype(bf16).astype(f32)

    own = gathered[0][...].astype(f32)
    unit, _ = unit_norm(own)
    qcls = nn((unit * gains_ref[0:1, :]).astype(bf16), qkv_ref[1, 0]).astype(bf16).astype(f32) * SCALE
    head = lax.broadcasted_iota(jnp.int32, (16, width), 0)
    lane = lax.broadcasted_iota(jnp.int32, (16, width), 1)
    mine = (lane >= head * HEAD_DIM) & (lane < (head + 1) * HEAD_DIM)
    token = lax.broadcasted_iota(jnp.int32, (16, rows), 1)
    ctx[...] = jnp.zeros(ctx.shape, f32)
    kvmsg_ref[:, :width] = kmsg
    kvmsg_ref[:, width:] = vmsg
    queries = [jnp.where(mine, qcls[i : i + 1], 0.0) for i in range(count)]
    scores = [nt(queries[i].astype(bf16), kv_ref[i, :, :width]) for i in range(count)]
    probs = []
    for i in range(count):
        last = jnp.sum(queries[i] * kmsg[i : i + 1], axis=1, keepdims=True)
        score = jnp.where(token == tokens - 1, last, scores[i])
        score = jnp.where(token < tokens, score, MASKED)
        expo = jnp.exp(score - jnp.max(score, axis=1, keepdims=True))
        probs.append((expo / jnp.sum(expo, axis=1, keepdims=True)).astype(bf16))
    outs = [nn(probs[i], kv_ref[i, :, width:]) for i in range(count)]
    for i in range(count):
        extra = jnp.sum(
            jnp.where(token == tokens - 1, probs[i].astype(f32), 0.0), axis=1, keepdims=True
        )
        out = outs[i] + extra * vmsg[i : i + 1]
        ctx[i : i + 1, :] = row_sum(jnp.where(mine, out, 0.0))
    resid = own + nn(ctx[...].astype(bf16), outw_ref[1])
    unit, _ = unit_norm(resid)
    hidden = nn((unit * gains_ref[1:2, :]).astype(bf16), up_ref[...])
    active = (hidden * sigmoid(1.702 * hidden)).astype(bf16)
    final = resid + nn(active, down_ref[...])
    final_ref[...] = final
    unit, _ = unit_norm(final)
    visual_ref[...] = (unit * gains_ref[2:3, :]).astype(bf16)


def first_rows(gathered, mw, mg, qkv, outw, up, down, gains, kv, tokens):
    count, width = kv.shape[0], mw.shape[0]
    slots = gathered[0].shape[0]
    operands = list(gathered) + [mw, mg, qkv, outw, up, down, gains, kv]
    return pl.pallas_call(
        functools.partial(first_kernel, len(gathered), count, tokens),
        grid=(1,),
        in_specs=[full(x.shape) for x in gathered]
        + [
            full(mw.shape),
            full(mg.shape),
            pl.BlockSpec((2, 3, width, width), lambda i: (0, 0, 0, 0)),
            pl.BlockSpec((2, width, width), lambda i: (0, 0, 0)),
            full(up.shape),
            full(down.shape),
            full(gains.shape),
            full(kv.shape),
        ],
        out_specs=[full((slots, width))] * 2 + [full((slots, 2 * width))] + [full((slots, width))] * 2,
        out_shape=[
            shape_of((slots, width), f32),
            shape_of((slots, width), f32),
            shape_of((slots, 2 * width), f32),
            shape_of((slots, width), bf16),
            shape_of((slots, width), f32),
        ],
        scratch_shapes=[pltpu.VMEM((slots, width), f32)],
        compiler_params=params(56),
        cost_estimate=cost(4e9, 12e6),
        name="first_rows",
    )(*operands)


def with_message(block, rows_ref, tokens, frame):
    top = (tokens - 1) // 16 * 16
    tail = block[top : top + 16].astype(f32)
    index = lax.broadcasted_iota(jnp.int32, tail.shape, 0)
    tail = jnp.where(index == tokens - 1 - top, rows_ref[pl.ds(frame, 1), :], tail).astype(bf16)
    pieces = [block[:top], tail]
    if top + 16 < block.shape[0]:
        pieces.append(block[top + 16 :])
    return jnp.concatenate(pieces, axis=0)


def masked_tail(scores, tokens):
    top = tokens // 16 * 16
    if top >= scores.shape[0]:
        return scores
    tail = scores[top:]
    index = lax.broadcasted_iota(jnp.int32, tail.shape, 0)
    return jnp.concatenate([scores[:top], jnp.where(index < tokens - top, tail, MASKED)], axis=0)


def half_pair(block_t, head):
    own = block_t[head * HEAD_DIM : (head + 1) * HEAD_DIM]
    none = jnp.zeros(own.shape, own.dtype)
    return jnp.concatenate([own, none] if head % 2 == 0 else [none, own], axis=0)


def pair_lanes(block, head):
    at = head // 2 * 2 * HEAD_DIM
    return block[:, at : at + 2 * HEAD_DIM]


def attend_kernel(
    tokens, normed_ref, kv_ref, video_ref, message_ref, nmsg_ref, kvmsg_ref, wq_ref, wv_ref, wo_ref,
    *refs,
):
    resid_ref, ctx_ref, lse_ref, wqt, wvt = refs[-5:]
    step = pl.program_id(0)

    @pl.when(step == 0)
    def _():
        wqt[...] = wq_ref[...].T
        wvt[...] = wv_ref[...].T

    batch, rows, width = normed_ref.shape
    normed, keys = [], []
    for i in range(batch):
        frame = step * batch + i
        normed.append(with_message(normed_ref[i], nmsg_ref, tokens, frame))
        keys.append(with_message(kv_ref[i], kvmsg_ref, tokens, frame))
    queries_t = [nt(wqt[...], n).astype(bf16) * jnp.bfloat16(SCALE) for n in normed]
    values_t = [nt(wvt[...], n).astype(bf16) for n in normed]
    jobs = [(i, h) for i in range(batch) for h in range(HEADS)]
    contexts, stats, scores, expos, totals = {}, {}, {}, {}, {}

    def score(job):
        i, head = job
        scores[job] = nn(pair_lanes(keys[i], head), half_pair(queries_t[i], head))

    def soften(job):
        one = masked_tail(scores.pop(job), tokens)
        top = jnp.max(one, axis=0, keepdims=True)
        expo = jnp.exp(one - top)
        totals[job] = row_sum(expo)
        expos[job] = expo.astype(bf16)
        stats[job] = top + jnp.log(totals[job])

    def mix(job):
        i, head = job
        own = values_t[i][head * HEAD_DIM : (head + 1) * HEAD_DIM]
        contexts[job] = nn(own, expos.pop(job)) * (1.0 / totals[job])

    stagger(jobs, [score, soften, mix], 3)
    for i in range(batch):
        context_t = jnp.concatenate([contexts[i, h] for h in range(HEADS)], axis=0).astype(bf16)
        ctx_ref[i] = context_t
        pad = [jnp.zeros((8 - HEADS, rows), f32)]
        lse_ref[i] = jnp.concatenate([stats[i, h] for h in range(HEADS)] + pad, axis=0)
        row = message_ref[pl.ds(step * batch + i, 1), :]
        base = put_row(pad_rows(video_ref[i].astype(f32), rows), tokens - 1, row)
        resid_ref[i] = base + tn(context_t, wo_ref[...])


def attend(normed, kv, video, message, nmsg, kvmsg, qkv, outw, tokens, after=()):
    count, rows, width = normed.shape
    slots = message.shape[0]
    batch = share_of(count, 2)
    return pl.pallas_call(
        functools.partial(attend_kernel, tokens),
        grid=(count // batch,),
        in_specs=[
            frames_block(batch, (rows, width)),
            frames_block(batch, (rows, 2 * width)),
            frames_block(batch, video.shape[1:]),
            full((slots, width)),
            full((slots, width)),
            full((slots, 2 * width)),
            square(width, 1, 0),
            square(width, 1, 2),
            square(width, 1),
        ]
        + [pl.BlockSpec(memory_space=pl.ANY)] * len(after),
        out_specs=[
            frames_block(batch, (rows, width)),
            frames_block(batch, (width, rows)),
            frames_block(batch, (8, rows)),
        ],
        out_shape=[
            shape_of((count, rows, width), f32),
            shape_of((count, width, rows), bf16),
            shape_of((count, 8, rows), f32),
        ],
        scratch_shapes=[pltpu.VMEM((width, width), bf16)] * 2,
        compiler_params=params(20),
        cost_estimate=cost(14e9, 10e6),
        name="attend",
    )(normed, kv, video, message, nmsg, kvmsg, qkv, qkv, outw, *after)


def caption_kernel(
    pieces, groups, clips, local, where_ref, lengths_ref, *refs
):
    gathered = refs[:pieces]
    caps_ref, cot_ref, qkv_ref, outw_ref, gains_ref = refs[pieces : pieces + 5]
    out_ref, grad_ref, gain_ref = refs[pieces + 5 : pieces + 8]
    part_refs = refs[pieces + 8 : pieces + 8 + pieces]
    keep_ref, send_ref, acc = refs[pieces + 8 + pieces :]
    width = caps_ref.shape[1]
    slots = gathered[0].shape[0]
    count = caps_ref.shape[0]
    keys_n = pieces * slots
    runs = lengths_ref.shape[1]

    token = lax.broadcasted_iota(jnp.int32, (count, keys_n), 0)
    key = lax.broadcasted_iota(jnp.int32, (count, keys_n), 1)
    slot = key % slots
    group = token // local
    position = token - group * local + where_ref[0] * local
    document = jnp.zeros((count, keys_n), jnp.int32)
    for m in range(groups):
        end = jnp.int32(0)
        for j in range(runs):
            end = end + lengths_ref[m, j]
            document = document + jnp.where((group == m) & (position >= end), 1, 0)
    allowed = slot == group * clips + document % clips
    valid = (document[:, 0:1] < runs - 1).astype(f32)

    pack = caps_ref[...].astype(f32)
    unit, inv = unit_norm(pack)
    gain = gains_ref[3:4, :]
    normed = (unit * gain).astype(bf16)
    visual = jnp.concatenate([g[...] for g in gathered], axis=0)
    queries = nn(normed, qkv_ref[0, 0]).astype(bf16)
    keys = nn(visual, qkv_ref[0, 1]).astype(bf16)
    values = nn(visual, qkv_ref[0, 2]).astype(bf16)

    masks = [head_mask((count, width), 1, h) for h in range(HEADS)]
    zero = jnp.zeros((count, width), bf16)

    def by_head(x):
        return jnp.concatenate([jnp.where(m, x, zero) for m in masks], axis=0)

    def merge(x):
        cut = [x[h * count : (h + 1) * count] for h in range(HEADS)]
        return functools.reduce(jnp.add, [jnp.where(m, c, 0.0) for m, c in zip(masks, cut)])

    allowed_all = jnp.concatenate([allowed.astype(jnp.int32)] * HEADS, axis=0) > 0
    split_q = by_head(queries)
    scores = jnp.where(allowed_all, nt(split_q, keys) * SCALE, MASKED)
    expo = jnp.exp(scores - jnp.max(scores, axis=1, keepdims=True))
    probs = expo / jnp.sum(expo, axis=1, keepdims=True)
    low = probs.astype(bf16)
    context = merge(nn(low, values)).astype(bf16)
    out_ref[...] = (pack + valid * nn(context, outw_ref[0])).astype(bf16)

    cot = cot_ref[...].astype(f32)
    branch = (cot * valid).astype(bf16)
    split_d = by_head(nt(branch, outw_ref[0]).astype(bf16))
    dvalues = tn(low, split_d)
    dprobs = nt(split_d, values)
    dscores = probs * (dprobs - jnp.sum(dprobs * probs, axis=1, keepdims=True))
    dscores = jnp.where(allowed_all, dscores, 0.0).astype(bf16)
    dqueries = (merge(nn(dscores, keys)) * SCALE).astype(bf16)
    dkeys = tn(dscores, split_q) * SCALE
    dnormed = nt(dqueries, qkv_ref[0, 0])
    grad_ref[...] = (cot + norm_back(unit, inv, gain, dnormed)).astype(bf16)
    gain_ref[...] = jnp.concatenate([row_sum(dnormed * unit), jnp.zeros((7, width), f32)], axis=0)
    low_k, low_v = dkeys.astype(bf16), dvalues.astype(bf16)
    part = nt(low_k, qkv_ref[0, 1]) + nt(low_v, qkv_ref[0, 2])
    for g in range(pieces):
        part_refs[g][...] = part[g * slots : (g + 1) * slots]
    if acc.shape[0] > 4 * width:
        acc[...] = jnp.zeros(acc.shape, f32)
    acc[0:width, :] = tn(normed, dqueries)
    acc[width : 2 * width, :] = tn(visual, low_k)
    acc[2 * width : 3 * width, :] = tn(visual, low_v)
    acc[3 * width : 4 * width, :] = tn(context, branch)
    emit(where_ref, acc, keep_ref, send_ref)


def captions_step(where, lengths, gathered, caps, cot, qkv, outw, gains, plan):
    count, width = caps.shape
    groups = lengths.shape[0]
    pieces = len(gathered)
    slots = gathered[0].shape[0]
    operands = list(gathered) + [caps, cot, qkv, outw, gains]
    acc_rows, packet_specs, packet_shapes = plan.packet(4 * width, width)
    return pl.pallas_call(
        functools.partial(caption_kernel, pieces, groups, plan.clips, count // groups),
        grid=(1,),
        in_specs=[scalars(), scalars()]
        + [full(x.shape) for x in operands[:-3]]
        + [
            pl.BlockSpec((1, 3, width, width), lambda i: (2, 0, 0, 0)),
            pl.BlockSpec((1, width, width), lambda i: (2, 0, 0)),
            full(gains.shape),
        ],
        out_specs=[full((count, width))] * 2
        + [full((8, width))]
        + [full((slots, width))] * pieces
        + packet_specs,
        out_shape=[shape_of((count, width), bf16)] * 2
        + [shape_of((8, width), f32)]
        + [shape_of((slots, width), f32)] * pieces
        + packet_shapes,
        scratch_shapes=[pltpu.VMEM((acc_rows, width), f32)],
        compiler_params=params(12),
        cost_estimate=cost(4e9, 8e6),
        name="captions_step",
    )(where, lengths, *operands)


def mlp_kernel(
    pieces, patch, ff, where_ref, resid_ref, cot_ref, final_ref, gains_ref, up_ref, down_ref, *refs
):
    parts = refs[:pieces]
    out_ref, dresid_ref, gain_ref, keep_ref, send_ref, acc, dcls = refs[-7:]
    step = pl.program_id(0)
    batch, rows, width = resid_ref.shape
    wide = acc.shape[1]
    blocks = ff // wide

    @pl.when(step == 0)
    def _():
        acc[...] = jnp.zeros(acc.shape, f32)
        dvisual = functools.reduce(jnp.add, [p[...] for p in parts])
        unit, inv = unit_norm(final_ref[...])
        dcls[...] = norm_back(unit, inv, gains_ref[2:3, :], dvisual)
        gain_ref[...] = jnp.concatenate(
            [jnp.zeros((1, width), f32), row_sum(dvisual * unit), jnp.zeros((6, width), f32)],
            axis=0,
        )

    resid = resid_ref[...].reshape(batch * rows, width)
    gain = gains_ref[1:2, :]
    unit, inv = unit_norm(resid)
    normed32 = unit * gain
    normed = normed32.astype(bf16)
    normed_t = normed32.T.astype(bf16)
    pieces_d = []
    for i in range(batch):
        one = pad_rows(cot_ref[i].astype(f32), rows)
        pieces_d.append(put_row(one, 0, one[0:1] + dcls[pl.ds(step * batch + i, 1), :]))
    dfinal = jnp.concatenate(pieces_d, axis=0)
    branch = dfinal.astype(bf16)
    branch_t = dfinal.T.astype(bf16)
    final = resid
    dnormed = jnp.zeros((batch * rows, width), f32)
    for c in range(blocks):
        span = slice(c * wide, (c + 1) * wide)
        hidden = nn(normed, up_ref[:, span])
        gate = sigmoid(1.702 * hidden)
        active = (hidden * gate).astype(bf16)
        final = final + nn(active, down_ref[span, :])
        dactive = nt(branch, down_ref[span, :])
        dhidden = (dactive * gate * (1.0 + 1.702 * hidden * (1.0 - gate))).astype(bf16)
        dnormed = dnormed + nt(dhidden, up_ref[:, span])
        acc[c * width : (c + 1) * width, :] += nn(normed_t, dhidden)
        acc[(blocks + c) * width : (blocks + c + 1) * width, :] += nn(branch_t, active)
    for i in range(batch):
        out_ref[i] = final[i * rows : i * rows + patch].astype(bf16)
    dresid = dfinal + norm_back(unit, inv, gain, dnormed)
    dresid_ref[...] = dresid.reshape(batch, rows, width)
    gain_ref[0:1, :] += row_sum(dnormed * unit)

    @pl.when(step == pl.num_programs(0) - 1)
    def _():
        emit(where_ref, acc, keep_ref, send_ref)


def mlp_step(where, resid, cot, final, gains, up, down, parts, plan, after=()):
    count, rows, width = resid.shape
    patch = cot.shape[1]
    ff = up.shape[1]
    slots = final.shape[0]
    batch = share_of(count, 2)
    wide = 2 * width
    acc_rows, packet_specs, packet_shapes = plan.packet(2 * ff * width // wide, wide)
    return pl.pallas_call(
        functools.partial(mlp_kernel, len(parts), patch, ff),
        grid=(count // batch,),
        in_specs=[
            scalars(),
            frames_block(batch, (rows, width)),
            frames_block(batch, (patch, width)),
            full((slots, width)),
            full(gains.shape),
            full(up.shape),
            full(down.shape),
        ]
        + [full((slots, width))] * len(parts)
        + [pl.BlockSpec(memory_space=pl.ANY)] * len(after),
        out_specs=[
            frames_block(batch, (patch, width)),
            frames_block(batch, (rows, width)),
            full((8, width)),
        ]
        + packet_specs,
        out_shape=[
            shape_of((count, patch, width), bf16),
            shape_of((count, rows, width), f32),
            shape_of((8, width), f32),
        ]
        + packet_shapes,
        scratch_shapes=[pltpu.VMEM((acc_rows, wide), f32), pltpu.VMEM((slots, width), f32)],
        compiler_params=params(36),
        cost_estimate=cost(20e9, 20e6),
        name="mlp_step",
    )(where, resid, cot, final, gains, up, down, *parts, *after)


def attend_back_kernel(tokens, first, last, waits, where_ref, normed_ref, kv_ref, *refs):
    (
        video_ref, message_ref, nmsg_ref, kvmsg_ref, ctx_ref, lse_ref, dresid_ref, gains_ref,
        wq_ref, wk_ref, wv_ref, wo_ref,
    ) = refs[:12]
    refs = refs[12:]
    if first:
        carried, refs = refs[1:5], refs[5:]
    refs = refs[waits:]
    outs = refs[: 6 if last else 5]
    grad_ref, dmsg_ref, dcls_ref, gain_ref = outs[:4]
    acc, wqt, wkt, wall = refs[len(outs) :]
    here = pl.program_id(0)
    step = here + first
    batch, rows, width = dresid_ref.shape
    patch = tokens - 1

    @pl.when(here == 0)
    def _():
        wqt[...] = wq_ref[...].T
        wkt[...] = wk_ref[...].T
        wall[:, 0:width] = wq_ref[...]
        wall[:, width : 2 * width] = wk_ref[...]
        wall[:, 2 * width : 3 * width] = wv_ref[...]
        for k, ref in enumerate((dmsg_ref, dcls_ref, gain_ref, acc)):
            ref[...] = carried[k][...] if first else jnp.zeros(ref.shape, f32)

    frames = range(batch)
    normed, kv = [], []
    for i in frames:
        normed.append(with_message(normed_ref[i], nmsg_ref, tokens, step * batch + i))
        kv.append(with_message(kv_ref[i], kvmsg_ref, tokens, step * batch + i))
    branch = [dresid_ref[i].astype(bf16) for i in frames]
    queries_t = [nt(wqt[...], n).astype(bf16) * jnp.bfloat16(SCALE) for n in normed]
    dcontext_t = [nt(wo_ref[...], b).astype(bf16) for b in branch]
    keys_t = [nt(wkt[...], n).astype(bf16) for n in normed]
    acc[3 * width : 4 * width, :] += functools.reduce(
        jnp.add, [nn(ctx_ref[i], branch[i]) for i in frames]
    )
    jobs = [(i, h) for i in frames for h in range(HEADS)]
    own = [slice(h * HEAD_DIM, (h + 1) * HEAD_DIM) for h in range(HEADS)]
    scores, dprobs, low, dscores, dq, dk, dv = {}, {}, {}, {}, {}, {}, {}

    def score(job):
        i, h = job
        scores[job] = nn(pair_lanes(kv[i], h), half_pair(queries_t[i], h))
        dprobs[job] = nn(pair_lanes(kv[i], HEADS + h), half_pair(dcontext_t[i], h))

    def soften(job):
        i, h = job
        probs = jnp.exp(masked_tail(scores.pop(job), tokens) - lse_ref[i, h : h + 1, :])
        low[job] = probs.astype(bf16)
        weighted = dprobs.pop(job) * probs
        dscores[job] = (weighted - probs * row_sum(weighted)).astype(bf16)

    def mix(job):
        i, h = job
        dq[job] = nn(keys_t[i][own[h]], dscores[job]) * SCALE
        dk[job] = nt(queries_t[i][own[h]], dscores.pop(job))
        dv[job] = nt(dcontext_t[i][own[h]], low.pop(job))

    stagger(jobs, [score, soften, mix], 2)
    dall = []
    for i in frames:
        parts = [d[i, h] for d in (dq, dk, dv) for h in range(HEADS)]
        dall.append(jnp.concatenate(parts, axis=0).astype(bf16))
    acc[0 : 3 * width, :] += functools.reduce(
        jnp.add, [nn(dall[i], normed[i]) for i in frames]
    )
    gain_sum = jnp.zeros((1, width), f32)
    for i in frames:
        dnormed = nn(wall[...], dall[i]).T
        at = pl.ds(step * batch + i, 1)
        base = put_row(pad_rows(video_ref[i].astype(f32), rows), tokens - 1, message_ref[at, :])
        unit, inv = unit_norm(base)
        dtokens = dresid_ref[i] + norm_back(unit, inv, gains_ref[0:1, :], dnormed)
        gain_sum = gain_sum + row_sum(dnormed * unit)
        grad_ref[i] = dtokens[:patch].astype(bf16)
        dcls_ref[at, :] = dtokens[0:1]
        dmsg_ref[at, :] = dtokens[patch : patch + 1]
    gain_ref[0:1, :] += gain_sum

    @pl.when(here == pl.num_programs(0) - 1)
    def _():
        if last:
            emit(where_ref, acc, *outs[4:])
        else:
            outs[4][...] = acc[...]


def attend_back(
    where, normed, kv, video, message, nmsg, kvmsg, ctx, lse, dresid, gains, qkv, outw, plan,
    batch, first, steps, carried=(), after=(),
):
    count, rows, width = normed.shape
    patch = video.shape[1]
    slots = message.shape[0]
    last = (first + steps) * batch == count
    acc_rows, packet_specs, packet_shapes = plan.packet(4 * width, width)
    if not last:
        packet_specs, packet_shapes = [full((acc_rows, width))], [shape_of((acc_rows, width), f32)]

    def block(shape):
        return pl.BlockSpec((batch,) + shape, lambda i, *_: (i + first, 0, 0))

    anywhere = pl.BlockSpec(memory_space=pl.ANY)
    carry_specs = [anywhere] + [full(x.shape) for x in carried[1:]] if carried else []
    return pl.pallas_call(
        functools.partial(attend_back_kernel, patch + 1, first, last, len(after)),
        grid=(steps,),
        in_specs=[
            scalars(),
            block((rows, width)),
            block((rows, 2 * width)),
            block((patch, width)),
            full((slots, width)),
            full((slots, width)),
            full((slots, 2 * width)),
            block((width, rows)),
            block((8, rows)),
            block((rows, width)),
            full(gains.shape),
            square(width, 1, 0),
            square(width, 1, 1),
            square(width, 1, 2),
            square(width, 1),
        ]
        + carry_specs
        + [anywhere] * len(after),
        out_specs=[block((patch, width))]
        + [full((slots, width))] * 2
        + [full((8, width))]
        + packet_specs,
        out_shape=[shape_of((count, patch, width), bf16)]
        + [shape_of((slots, width), f32)] * 2
        + [shape_of((8, width), f32)]
        + packet_shapes,
        input_output_aliases={15: 0} if carried else {},
        scratch_shapes=[
            pltpu.VMEM((acc_rows, width), f32),
            pltpu.VMEM((width, width), bf16),
            pltpu.VMEM((width, width), bf16),
            pltpu.VMEM((width, 3 * width), bf16),
        ],
        compiler_params=params(26),
        cost_estimate=cost(4.5e9 * steps, 4e6 * steps),
        name="attend_back",
    )(
        where, normed, kv, video, message, nmsg, kvmsg, ctx, lse, dresid, gains, qkv, qkv, qkv,
        outw, *carried, *after,
    )


class Groups:
    def __init__(self, layout, slots):
        self.segs, self.frames, self.clips = layout
        self.slots = slots
        self.groups = self.segs * self.clips
        self.together = max(1, min(self.groups, 512 // (self.frames * slots)))
        self.steps = self.groups // self.together
        self.rows = self.frames * self.together * slots
        per_group = self.frames * slots
        self.side = per_group * max(1, min(self.together, 128 // per_group))
        self.blocks = [slice(at, at + self.side) for at in range(0, self.rows, self.side)]
        self.jobs = [(i, h) for i in range(len(self.blocks)) for h in range(HEADS)]

    def row_of(self, s, f, c):
        group = s * self.clips + c
        step, inside = group // self.together, group % self.together
        return step, pl.multiple_of((inside * self.frames + f) * self.slots, 16)

    def every(self, where_ref):
        me_f, me_s, me_c = where_ref[0], where_ref[1], where_ref[2]
        for a in range(self.segs):
            for b in range(self.frames):
                for d in range(self.clips):
                    yield a, b, d, *self.row_of(me_s ^ a, me_f ^ b, me_c ^ d)

    def run(self, batch):
        def first(ref, at, value):
            ref[at] = value

        def again(ref, at, value):
            ref[at] += value

        batch(0, first)
        if self.steps > 1:
            pl.loop(1, self.steps)(lambda step: batch(step, again))


def join(groups, *parts):
    lanes = [
        jnp.concatenate([p[i, h] for p in parts for h in range(HEADS)], axis=0)
        for i in range(len(groups.blocks))
    ]
    return (jnp.concatenate(lanes, axis=1) if len(lanes) > 1 else lanes[0]).astype(bf16)


OWN = [slice(h * HEAD_DIM, (h + 1) * HEAD_DIM) for h in range(HEADS)]


def message_forward_kernel(groups, where_ref, *refs):
    side = refs[: groups.segs]
    (
        mw_ref, mg_ref, qkv_ref, classes_ref, start_ref, values_ref, qt_ref, kt_ref, probs_ref,
        ctx_ref, wqt, wkt, wvt,
    ) = refs[groups.segs :]
    for a, b, d, step, row in groups.every(where_ref):
        classes_ref[step, pl.ds(row, groups.slots), :] = side[a][d, b]
    wqt[...] = qkv_ref[0, 0].T
    wkt[...] = qkv_ref[0, 1].T
    wvt[...] = qkv_ref[0, 2].T
    edge = (groups.side, groups.side)
    key, query = lax.broadcasted_iota(jnp.int32, edge, 0), lax.broadcasted_iota(jnp.int32, edge, 1)
    per_group = groups.frames * groups.slots
    same = (key % groups.slots == query % groups.slots) & (key // per_group == query // per_group)

    def batch(step, put):
        del put
        start = nn(classes_ref[step], mw_ref[...]).astype(bf16)
        start_ref[step] = start
        unit, _ = unit_norm(start.astype(f32))
        normed = (unit * mg_ref[...]).astype(bf16)
        keys = nn(normed, qkv_ref[0, 1]).astype(bf16)
        values_ref[step] = nn(normed, qkv_ref[0, 2]).astype(bf16)
        queries_t = nt(wqt[...], normed).astype(bf16) * jnp.bfloat16(SCALE)
        values_t = nt(wvt[...], normed).astype(bf16)
        qt_ref[step] = queries_t
        kt_ref[step] = nt(wkt[...], normed).astype(bf16)
        scores, low, ctx = {}, {}, {}

        def score(job):
            i, h = job
            at = groups.blocks[i]
            scores[job] = nn(pair_lanes(keys[at], h), half_pair(queries_t[:, at], h))

        def soften(job):
            i, h = job
            one = jnp.where(same, scores.pop(job), MASKED)
            expo = jnp.exp(one - jnp.max(one, axis=0, keepdims=True))
            probs = expo * (1.0 / row_sum(expo))
            probs_ref[step, i * HEADS + h] = probs.astype(probs_ref.dtype)
            low[job] = probs.astype(bf16)

        def mix(job):
            i, h = job
            ctx[job] = nn(values_t[OWN[h], groups.blocks[i]], low.pop(job))

        stagger(groups.jobs, [score, soften, mix], 3)
        ctx_ref[step] = join(groups, ctx)

    groups.run(batch)


def message_forward(where, side, mw, mg, qkv, groups):
    width = mw.shape[0]
    rows, steps = groups.rows, groups.steps
    outs = [
        shape_of((steps, rows, width), bf16),
        shape_of((steps, rows, width), bf16),
        shape_of((steps, rows, width), bf16),
        shape_of((steps, width, rows), bf16),
        shape_of((steps, width, rows), bf16),
        shape_of((steps, len(groups.jobs), groups.side, groups.side), f32 if steps == 1 else bf16),
        shape_of((steps, width, rows), bf16),
    ]
    return pl.pallas_call(
        functools.partial(message_forward_kernel, groups),
        grid=(1,),
        in_specs=[scalars()]
        + [full(x.shape) for x in side]
        + [
            full(mw.shape),
            full(mg.shape),
            pl.BlockSpec((1, 3, width, width), lambda i: (0, 0, 0, 0)),
        ],
        out_specs=[full(x.shape) for x in outs],
        out_shape=outs,
        scratch_shapes=[pltpu.VMEM((width, width), bf16)] * 3,
        compiler_params=params(48 if steps == 1 else 56),
        cost_estimate=cost(3e9, 6e6),
        name="message_forward",
    )(where, *side, mw, mg, qkv)


def message_back_kernel(layout, groups, where_ref, *refs):
    frame_part(layout, where_ref, *refs)
    message_part(groups, where_ref, *refs)


def frame_part(layout, where_ref, *refs):
    segs, frames, clips = layout
    pieces, refs = refs[: segs * frames], refs[segs * frames + 7 :]
    big_ref, out_ref, whole = refs[6], refs[7], refs[12]
    width = out_ref.shape[-1]
    chunk = whole.shape[0] // (segs * frames * clips)
    place(
        layout,
        where_ref,
        lambda a, b, d: pieces[a * frames + b][d * chunk : (d + 1) * chunk, :],
        whole,
        chunk,
    )
    for j in range(3):
        big_ref[1, j] = whole[j * width : (j + 1) * width, :].astype(f32).T
    out_ref[1] = whole[3 * width : 4 * width, :].astype(f32)


def message_part(groups, where_ref, *refs):
    count = groups.segs * groups.frames
    pieces, refs = refs[:count], refs[count:]
    classes_ref, start_ref, values_ref, qt_ref, kt_ref, probs_ref, ctx_ref = refs[:7]
    mw_ref, mg_ref, qkv_ref, outw_ref = refs[7:11]
    big_ref, out_ref, mwg_ref, gain_ref, gains_ref, dclass_ref, _, dmsgs, dstart, wall = refs[13:]
    width, slots = mw_ref.shape[0], groups.slots
    for a, b, d, step, row in groups.every(where_ref):
        piece = pieces[a * groups.frames + b]
        at = piece.shape[0] - (groups.clips - d) * slots
        dmsgs[step, pl.ds(row, slots), :] = piece[at : at + slots, :]
    gain_total = jnp.zeros((slots, width), f32)
    for i in range(groups.frames * groups.together):
        for step in range(groups.steps):
            gain_total += dmsgs[step, i * slots : (i + 1) * slots, :].astype(f32)
    gains_ref[...] = gain_total[slots - 4 : slots]
    for j in range(3):
        wall[:, j * width : (j + 1) * width] = qkv_ref[0, j]
    index = lax.broadcasted_iota(jnp.int32, (groups.rows, 1), 0) % slots
    my_step, my_row = groups.row_of(where_ref[1], where_ref[0], where_ref[2])

    def batch(step, put):
        dm = jnp.where(index < slots - 6, dmsgs[step].astype(f32), 0.0).astype(bf16)
        unit, inv = unit_norm(start_ref[step].astype(f32))
        normed = (unit * mg_ref[...]).astype(bf16)
        dcontext_t = nt(outw_ref[0], dm).astype(bf16)
        values, queries_t, keys_t = values_ref[step], qt_ref[step], kt_ref[step]
        dprobs, low, dscores, dq, dk, dv = {}, {}, {}, {}, {}, {}

        def score(job):
            i, h = job
            at = groups.blocks[i]
            dprobs[job] = nn(pair_lanes(values[at], h), half_pair(dcontext_t[:, at], h))

        def soften(job):
            i, h = job
            probs = probs_ref[step, i * HEADS + h].astype(f32)
            low[job] = probs.astype(bf16)
            weighted = dprobs.pop(job) * probs
            dscores[job] = (weighted - probs * row_sum(weighted)).astype(bf16)

        def mix(job):
            i, h = job
            at = groups.blocks[i]
            dq[job] = nn(keys_t[OWN[h], at], dscores[job]) * SCALE
            dk[job] = nt(queries_t[OWN[h], at], dscores.pop(job))
            dv[job] = nt(dcontext_t[OWN[h], at], low.pop(job))

        stagger(groups.jobs, [score, soften, mix], 2)
        put(out_ref, 0, nn(ctx_ref[step], dm))
        dall = join(groups, dq, dk, dv)
        grads = nn(dall, normed)
        for j in range(3):
            put(big_ref, (0, j), grads[j * width : (j + 1) * width].T)
        dnormed = nn(wall[...], dall).T
        put(gain_ref, ..., jnp.sum(dnormed * unit, axis=0))
        ds = norm_back(unit, inv, mg_ref[...], dnormed) + dm.astype(f32)
        dstart[...] = ds
        put(mwg_ref, ..., tn(classes_ref[step], ds.astype(bf16)))

        @pl.when(my_step == step)
        def _():
            dclass_ref[...] = nt(dstart[pl.ds(my_row, slots), :].astype(bf16), mw_ref[...])

    groups.run(batch)


def message_back(where, pieces, forward, mw, mg, qkv, outw, big, out, layout, groups):
    width = mw.shape[0]
    operands = list(pieces) + list(forward) + [mw, mg]
    chunk = pieces[0].shape[0] // groups.clips - groups.slots
    return pl.pallas_call(
        functools.partial(message_back_kernel, layout, groups),
        grid=(1,),
        in_specs=[scalars()]
        + [full(x.shape) for x in operands]
        + [
            pl.BlockSpec((1, 3, width, width), lambda i: (0, 0, 0, 0)),
            pl.BlockSpec((1, width, width), lambda i: (0, 0, 0)),
            pl.BlockSpec(memory_space=pl.ANY),
            pl.BlockSpec(memory_space=pl.ANY),
        ],
        out_specs=[
            pl.BlockSpec((2, 3, width, width), lambda i: (0, 0, 0, 0)),
            pl.BlockSpec((2, width, width), lambda i: (0, 0, 0)),
            full((width, width)),
            full((width,)),
            full((4, width)),
            full((groups.slots, width)),
        ],
        out_shape=[
            shape_of((3, 3, width, width), f32),
            shape_of((3, width, width), f32),
            shape_of((width, width), f32),
            shape_of((width,), f32),
            shape_of((4, width), f32),
            shape_of((groups.slots, width), f32),
        ],
        input_output_aliases={len(operands) + 3: 0, len(operands) + 4: 1},
        scratch_shapes=[
            pltpu.VMEM((groups.groups * groups.frames * chunk, width), bf16),
            pltpu.VMEM((groups.steps, groups.rows, width), bf16),
            pltpu.VMEM((groups.rows, width), f32),
            pltpu.VMEM((width, 3 * width), bf16),
        ],
        compiler_params=params(30 if groups.steps == 1 else 60),
        cost_estimate=cost(4e9, 12e6),
        name="message_back",
    )(where, *operands, qkv, outw, big, out)


def emit(where_ref, acc, keep_ref, send_ref):
    frames, clips, chunk = keep_ref.shape[:3]
    me_f, me_s = where_ref[0], where_ref[1]
    for a, out in enumerate((keep_ref, send_ref)):
        for b in range(frames):
            for d in range(clips):
                to = ((me_s ^ a) * frames + (me_f ^ b)) * clips + d
                at = pl.multiple_of(to * chunk, 16)
                out[b, d] = acc[pl.ds(at, chunk), :].astype(bf16)


class Plan:
    def __init__(self, clips):
        self.clips = clips
        self.segs = lax.axis_size("seg")
        self.frames = lax.axis_size("frame")
        self.rings = lax.axis_size("clip")
        self.layout = (self.segs, self.frames, self.rings)
        self.devices = self.segs * self.frames * self.rings

    def chunk(self, rows):
        share = -(-rows // self.devices)
        return -(-share // 16) * 16

    def packet(self, rows, width):
        chunk = self.chunk(rows)
        shape = (self.frames, self.rings, chunk, width)
        return chunk * self.devices, [full(shape)] * 2, [shape_of(shape, bf16)] * 2


def swap(x, axis, k):
    count = lax.axis_size(axis)
    return lax.ppermute(x, axis, [(i, i ^ k) for i in range(count)])


def behind(x, *others):
    return lax.optimization_barrier((x, others))[0]


class Sum:
    def __init__(self, arrays, views=None):
        self.arrays = list(arrays)
        self.views = list(views or [()] * len(self.arrays))

    def part(self, view):
        return Sum(self.arrays, [v + (view,) for v in self.views])

    def plus(self, *arrays):
        return Sum(self.arrays + list(arrays), self.views + [()] * len(arrays))

    def value(self):
        terms = []
        for x, views in zip(self.arrays, self.views):
            for view in views:
                x = view(x)
            terms.append(x.astype(f32))
        return functools.reduce(jnp.add, terms).astype(bf16)


jax.tree_util.register_pytree_node(
    Sum, lambda s: (s.arrays, s.views), lambda views, arrays: Sum(arrays, views)
)


def at(k):
    return lambda x: x[k]


def total(one, two):
    return (one.astype(f32) + two.astype(f32)).astype(bf16)


def reduce_seg(keep, send):
    return Sum([keep, swap(send, "seg", 1)])


def frame_sends(terms):
    return [terms.part(at(b)).value() for b in range(1, lax.axis_size("frame"))]


def reduce_frame(terms, sends):
    return terms.part(at(0)).plus(*[swap(x, "frame", b + 1) for b, x in enumerate(sends)])


def clip_bits():
    count = lax.axis_size("clip")
    return [1 << j for j in range(count.bit_length() - 1)]


def swap_two(one, two, axis, k):
    width = one.shape[-1]
    rows = one.size // width
    got = swap(jnp.concatenate([one.reshape(-1, width), two.reshape(-1, width)]), axis, k)
    return got[:rows].reshape(one.shape), got[rows:].reshape(two.shape)


def exchange(part, rows, bit):
    got, got_rows = swap_two(part, rows, "clip", bit)
    return total(part, got), jnp.concatenate([rows, got_rows])


def gather_frame(held):
    return [held] + [swap(held, "frame", b) for b in range(1, lax.axis_size("frame"))]


def gather_seg(held):
    return held + [swap(h, "seg", 1) for h in held]


def place(layout, where_ref, piece, whole, chunk):
    segs, frames, clips = layout
    me_f, me_s = where_ref[0], where_ref[1]
    for a in range(segs):
        for b in range(frames):
            for d in range(clips):
                of = ((me_s ^ a) * frames + (me_f ^ b)) * clips + d
                whole[pl.ds(pl.multiple_of(of * chunk, 16), chunk), :] = piece(a, b, d)


def unpack_kernel(layout, where_ref, *refs):
    segs, frames, clips = layout
    main = refs[:segs]
    up_ref, down_ref, whole = refs[segs:]
    width, ff = up_ref.shape
    wide = whole.shape[1]
    place(layout, where_ref, lambda a, b, d: main[a][b * clips + d], whole, main[0].shape[1])
    blocks = ff // wide
    for c in range(blocks):
        span = slice(c * wide, (c + 1) * wide)
        up_ref[:, span] = whole[c * width : (c + 1) * width, :].astype(f32)
        other = whole[(blocks + c) * width : (blocks + c + 1) * width, :]
        down_ref[span, :] = other.astype(f32).T


def unpack(where, main, width, ff, plan):
    chunk, wide = main[0].shape[1:]
    return pl.pallas_call(
        functools.partial(unpack_kernel, plan.layout),
        grid=(1,),
        in_specs=[scalars()] + [full(x.shape) for x in main],
        out_specs=[full((width, ff)), full((ff, width))],
        out_shape=[shape_of((width, ff), f32), shape_of((ff, width), f32)],
        scratch_shapes=[pltpu.VMEM((plan.devices * chunk, wide), bf16)],
        compiler_params=params(40),
        cost_estimate=cost(2e9, 10e6),
        name="unpack",
    )(where, *main)


def unpack_side_kernel(layout, where_ref, *refs):
    segs = layout[0]
    side = refs[:segs]
    big_ref, out_ref, whole = refs[segs:]
    width = out_ref.shape[-1]
    place(layout, where_ref, lambda a, b, d: side[a][b, d], whole, side[0].shape[2])
    for j in range(3):
        big_ref[0, j] = whole[j * width : (j + 1) * width, :].astype(f32)
    out_ref[0] = whole[3 * width : 4 * width, :].astype(f32)


def unpack_side(where, side, plan):
    rows, width = side[0].shape[2:]
    return pl.pallas_call(
        functools.partial(unpack_side_kernel, plan.layout),
        grid=(1,),
        in_specs=[scalars()] + [full(x.shape) for x in side],
        out_specs=[
            pl.BlockSpec((1, 3, width, width), lambda i: (2, 0, 0, 0)),
            pl.BlockSpec((1, width, width), lambda i: (2, 0, 0)),
        ],
        out_shape=[shape_of((3, 3, width, width), f32), shape_of((3, width, width), f32)],
        scratch_shapes=[pltpu.VMEM((plan.devices * rows, width), bf16)],
        compiler_params=params(30),
        cost_estimate=cost(1e9, 4e6),
        name="unpack_side",
    )(where, *side)


def last_rows_kernel(gain_a, gain_b, gain_c, dmsg_ref, out_ref):
    slots, width = dmsg_ref.shape
    rows = [
        dmsg_ref[0 : slots - 6, :],
        jnp.zeros((2, width), f32),
        gain_a[0:1, :],
        gain_b[0:1, :],
        gain_b[1:2, :],
        gain_c[0:1, :],
    ]
    out_ref[...] = jnp.concatenate(rows, axis=0).astype(bf16)


def last_rows(gain_a, gain_b, gain_c, dmsg):
    return pl.pallas_call(
        last_rows_kernel,
        out_shape=shape_of(dmsg.shape, bf16),
        name="last_rows",
    )(gain_a, gain_b, gain_c, dmsg)


def local(
    video, captions, caption_lengths, message_weight, message_gain, qkv_weights, out_weights,
    mlp_up, mlp_down, gains, video_cot, caption_cot,
):
    micro, clips, per_frame, patch, width = video.shape
    count = micro * clips * per_frame
    ff = mlp_up.shape[1]
    plan = Plan(clips)
    tokens = patch + 1
    rows = -(-tokens // 16) * 16
    slots = -(-(count + 6) // 16) * 16
    where = jnp.stack(
        [lax.axis_index("frame"), lax.axis_index("seg"), lax.axis_index("clip")]
    ).astype(jnp.int32)
    frames = video.reshape(count, patch, width)
    cots = video_cot.reshape(count, patch, width)
    caps = captions.reshape(-1, width)
    cap_cots = caption_cot.reshape(-1, width)
    lengths = caption_lengths.reshape(micro, -1)
    gain = message_gain.reshape(1, width)

    classes = class_rows(video, slots)
    gathered = gather_frame(classes)
    normed, kv = norm_tokens(frames, gains, qkv_weights, rows)
    message, nmsg, kvmsg, visual, final = first_rows(
        gathered, message_weight, gain, qkv_weights, out_weights, mlp_up, mlp_down, gains,
        kv, tokens,
    )
    visuals = gather_frame(visual)
    results = captions_step(
        where, lengths, visuals, caps, cap_cots, qkv_weights, out_weights, gains, plan
    )
    caption_out, caption_grad, gain_c = results[:3]
    parts = list(results[3:-2])
    parts = [parts[0]] + [swap(parts[b], "frame", b) for b in range(1, plan.frames)]
    bits = clip_bits()
    rows_all = jnp.stack(gathered)[None]
    side = reduce_seg(*results[-2:])
    side = behind(side, results[3])
    sends = frame_sends(side)
    resid, ctx, lse = attend(
        normed, kv, frames, message, nmsg, kvmsg, qkv_weights, out_weights, tokens, sends
    )
    side = reduce_frame(side, sends)
    parts, resid, side = behind((parts, resid, side))
    side = side.value()
    side, resid = behind((side, resid))
    video_out, dresid, gain_b, keep, send = mlp_step(
        where, resid, cots, final, gains, mlp_up, mlp_down, parts, plan
    )
    for bit in bits[:-1]:
        side, rows_all = exchange(side, rows_all, bit)
    side, rows_all, video_out, dresid, keep, send = behind(
        (side, rows_all, video_out, dresid, keep, send)
    )
    main = reduce_seg(keep, send)
    turned = video_out.reshape(video.shape).transpose(1, 2, 3, 0, 4)
    main, dresid, turned = behind((main, dresid, turned))
    video_out = turned.transpose(3, 0, 1, 2, 4)
    sends = frame_sends(main)
    sends, dresid, side, rows_all = behind((sends, dresid, side, rows_all))
    batch = share_of(count, 2)
    steps = count // batch
    late_steps = 2
    back = functools.partial(
        attend_back, where, normed, kv, frames, message, nmsg, kvmsg, ctx, lse, dresid, gains,
        qkv_weights, out_weights, plan, batch,
    )
    carried = back(0, steps - late_steps)
    main = reduce_frame(main, sends)
    side, rows_all = exchange(side, rows_all, bits[-1])
    carried, main, side, rows_all = behind((carried, main, side, rows_all))
    main = main.value()
    main, carried, side = behind((main, carried, side))
    for bit in bits[:-1]:
        main = total(main, swap(main, "clip", bit))
    side = gather_frame(side)
    grad, dmsg, dcls, gain_a, keep, send = back(steps - late_steps, late_steps, carried)
    main, side, keep, send, gain_a, dmsg = behind((main, side, keep, send, gain_a, dmsg))

    main = total(main, swap(main, "clip", bits[-1]))
    late = reduce_seg(keep, send)
    rest = last_rows(gain_a, gain_b, gain_c, dmsg)
    side = jnp.stack(side)
    other, other_rows = swap_two(side, rows_all, "seg", 1)
    late, rest = behind((late, rest))
    late = reduce_frame(late, frame_sends(late))
    main, late, other, other_rows = behind((main, late, other, other_rows))

    held = gather_frame(main)
    late, rest = late.value(), rest[None]
    for bit in bits:
        late, rest = exchange(late, rest, bit)
    big, out = unpack_side(where, [side, other], plan)
    groups = Groups(plan.layout, slots)
    forward = message_forward(
        where, [rows_all, other_rows], message_weight, gain, qkv_weights, groups
    )
    held, late, rest, big, forward = behind((held, late, rest, big, forward))

    late = gather_frame(jnp.concatenate([late.reshape(-1, width), rest.reshape(-1, width)]))
    held = gather_seg([jnp.concatenate(held, axis=0)])
    up_grad, down_grad = unpack(where, held, width, ff, plan)
    late, up_grad = behind((late, up_grad))

    late = gather_seg(late)
    big, out, mw_grad, mg_grad, gains_grad, dclass = message_back(
        where, late, forward, message_weight, gain, qkv_weights, out_weights, big, out,
        plan.layout, groups,
    )
    fixed = (dclass + dcls)[:count].astype(bf16).reshape(micro, clips, per_frame, 1, width)
    grad = lax.dynamic_update_slice(grad.reshape(video.shape), fixed, (0, 0, 0, 0, 0))
    return (
        video_out.reshape(video.shape),
        caption_out.reshape(captions.shape),
        grad,
        caption_grad.reshape(captions.shape),
        mw_grad,
        mg_grad,
        big,
        out,
        up_grad,
        down_grad,
        gains_grad,
    )


def solution(mesh):
    rows = P(None, ("clip", "seg"), "frame", None, None)
    caps = P(None, ("clip", "seg"), "frame", None)
    return jax.shard_map(
        local,
        mesh=mesh,
        in_specs=(rows, caps, P(None, ("clip", "seg"), None)) + (P(),) * 7 + (rows, caps),
        out_specs=(rows, caps, rows, caps) + (P(),) * 7,
        check_vma=False,
    )
```
